32 devices in a mesh: dp: 4 (over y, x), fsdp: 8 (over z, core).
Axes of the slice: x: 2, y: 2, z: 4, core: 2. Of those that a mesh axis runs over, the one named last changes fastest.
Arguments:
- tokens: bfloat16 [256, 104, 768], P(('dp', 'fsdp')), may hold values from -6 to 6
- captions: int32 [256], P(('dp', 'fsdp')), may hold values from 5 to 60, as said below
- cotangent: bfloat16 [256, 104, 768], P(('dp', 'fsdp')), may hold values from -6 to 6
- project_weight: bfloat16 [768, 2304], P('fsdp'), may hold values from -0.21875 to 0.21875
- project_bias: bfloat16 [1536], P('fsdp'), may hold values from -3 to 3
- output_weight: bfloat16 [768, 768], P('fsdp'), may hold values from -1.75 to 1.75
- output_bias: bfloat16 [768], P('fsdp'), may hold values from -3 to 3
- first_gain: bfloat16 [768], P('fsdp'), may hold values from 0.25 to 1.75
- first_shift: bfloat16 [768], P('fsdp'), may hold values from -2 to 2
- expand_weight: bfloat16 [768, 3072], P('fsdp'), may hold values from -0.21875 to 0.21875
- expand_bias: bfloat16 [3072], P('fsdp'), may hold values from -3 to 3
- shrink_weight: bfloat16 [3072, 768], P('fsdp'), may hold values from -0.15625 to 0.15625
- shrink_bias: bfloat16 [768], P('fsdp'), may hold values from -3 to 3
- second_gain: bfloat16 [768], P('fsdp'), may hold values from 0.25 to 1.75
- second_shift: bfloat16 [768], P('fsdp'), may hold values from -2 to 2
Outputs:
- layer_out: bfloat16 [256, 104, 768], P(('dp', 'fsdp'))
- token_grad: float32 [256, 104, 768], P(('dp', 'fsdp'))
- grad_project_weight: float32 [768, 2304], P('fsdp')
- grad_project_bias: float32 [1536], P('fsdp')
- grad_output_weight: float32 [768, 768], P('fsdp')
- grad_output_bias: float32 [768], P('fsdp')
- grad_first_gain: float32 [768], P('fsdp')
- grad_first_shift: float32 [768], P('fsdp')
- grad_expand_weight: float32 [768, 3072], P('fsdp')
- grad_expand_bias: float32 [3072], P('fsdp')
- grad_shrink_weight: float32 [3072, 768], P('fsdp')
- grad_shrink_bias: float32 [768], P('fsdp')
- grad_second_gain: float32 [768], P('fsdp')
- grad_second_shift: float32 [768], P('fsdp')
The draws below stay inside these ranges and needn't reach their ends.
Inputs may be any that keep to these rules, and one draw needn't show every extreme that they name: In every draw some pair's caption has exactly 5 words and some pair's exactly 60; most captions are short (lengths are heavy-tailed toward 5).
All inputs are finite; a program needn't handle non-finite values.
Results may differ from the reference program's by a relative error of at most 0.017.
Values may be sent and summed in bfloat16 or wider, within the bound.
No kernel may reach another device: no remote copies, remote signals or barrier semaphores. Data moves between devices by JAX's collectives and lax.ppermute only.
A program may use at most 128 MiB of HBM per device.

```python
import jax
import jax.numpy as jnp
from jax import lax

D = 768
FF = 3072
HEADS = 12
HEAD_DIM = 64
PAIRS_DEV = 8
SEQ = 104
REGIONS = 36
CAPTION_MIN = 5
CAPTION_MAX = 60
PAIRS = 256
N_DP = 4
N_FSDP = 8


def draw_captions(key, part):
    key = jax.random.fold_in(key, 11)
    subkeys = jax.random.split(key, 5)
    span = CAPTION_MAX - CAPTION_MIN + 1
    first_draw = jax.random.randint(subkeys[0], (PAIRS,), 0, span)
    second_draw = jax.random.randint(subkeys[1], (PAIRS,), 0, span)
    third_draw = jax.random.randint(subkeys[2], (PAIRS,), 0, span)
    lengths = CAPTION_MIN + jnp.minimum(jnp.minimum(first_draw, second_draw), third_draw)
    longest = jax.random.randint(subkeys[3], (), 0, PAIRS)
    shortest = (longest + 1 + jax.random.randint(subkeys[4], (), 0, PAIRS - 1)) % PAIRS
    position = jnp.arange(PAIRS)
    lengths = jnp.where(position == longest, CAPTION_MAX, lengths)
    lengths = jnp.where(position == shortest, CAPTION_MIN, lengths)
    return lengths.astype(jnp.int32)


def shard_levels(stream_key, dims, cuts, least, top_value):
    level, own = 1.0, jax.random.fold_in(stream_key, 6)
    for axis_at, blocks in cuts:
        steps = jnp.exp(jax.random.uniform(jax.random.fold_in(own, axis_at), (blocks,), jnp.float32, least / len(cuts), top_value / len(cuts)))
        level = level * jnp.repeat(steps, dims[axis_at] // blocks).reshape([-1 if axis == axis_at else 1 for axis in range(len(dims))])
    return level


def noise(stream_key, shape, deviation, limit, shards=(), kind=jnp.bfloat16):
    gain = shard_levels(stream_key, shape, shards, -0.22, 0.18) if shards else 1.0
    values = jax.random.normal(stream_key, shape, jnp.float32) * deviation * gain
    return jnp.minimum(jnp.maximum(values, -limit), limit).astype(kind)


def setup_inputs(seed: int = 0) -> dict:
    keys = jax.random.split(jax.random.key(seed), 16)
    return {
        "tokens": noise(keys[0], (PAIRS, SEQ, D), 1.0, 6.0, ((0, 32),)),
        "captions": draw_captions(jax.random.fold_in(keys[15], 71), 0),
        "cotangent": noise(keys[2], (PAIRS, SEQ, D), 1.0, 6.0, ((0, 32),)),
        "project_weight": noise(keys[3], (D, 3 * D), D ** -0.5, 0.21875, ((0, 8),)),
        "project_bias": noise(keys[4], (2 * D,), 0.5, 3.0, ((0, 8),)),
        "output_weight": noise(keys[5], (D, D), (D // 64) ** -0.5, 1.75, ((0, 8),)),
        "output_bias": noise(keys[6], (D,), 0.5, 3.0, ((0, 8),)),
        "first_gain": jnp.clip(1.0 + 0.15 * jax.random.normal(keys[7], (D,), jnp.float32), 0.25, 1.75).astype(jnp.bfloat16),
        "first_shift": noise(keys[8], (D,), 0.3, 2.0, ((0, 8),)),
        "expand_weight": noise(keys[9], (D, FF), D ** -0.5, 0.21875, ((0, 8),)),
        "expand_bias": noise(keys[10], (FF,), 0.5, 3.0, ((0, 8),)),
        "shrink_weight": noise(keys[11], (FF, D), (FF // 2) ** -0.5, 0.15625, ((0, 8),)),
        "shrink_bias": noise(keys[12], (D,), 0.5, 3.0, ((0, 8),)),
        "second_gain": jnp.clip(1.0 + 0.15 * jax.random.normal(keys[13], (D,), jnp.float32), 0.25, 1.75).astype(jnp.bfloat16),
        "second_shift": noise(keys[14], (D,), 0.3, 2.0, ((0, 8),)),
    }


HIGHEST = lax.Precision.HIGHEST

@jax.custom_vjp
def low(v):
    return lax.optimization_barrier(v.astype(jnp.bfloat16)).astype(jnp.float32)

@jax.custom_vjp
def low_back(v):
    return v

def low_keep(v):
    return (low(v), None)

def low_pass(kept, grad):
    return (grad,)

def back_keep(v):
    return (v, None)

def back_low(kept, grad):
    return (low(grad),)
low.defvjp(low_keep, low_pass)
low_back.defvjp(back_keep, back_low)

def layer_norm(inputs, scale_row, shift_row):
    row_mean = lax.optimization_barrier(jnp.mean(inputs, axis=-1, keepdims=True))
    centred = inputs - row_mean
    spread = lax.optimization_barrier(jnp.mean(centred * centred, axis=-1, keepdims=True))
    return centred * lax.rsqrt(spread + 1e-05) * scale_row + shift_row

def gelu_exact(inputs):
    return 0.5 * inputs * (1.0 + jax.scipy.special.erf(inputs * 0.7071067811865476))

def layer_forward(tokens, key_valid, params):
    project_weight, project_bias, output_weight, output_bias, first_gain, first_shift, expand_weight, expand_bias, shrink_weight, shrink_bias, second_gain, second_shift = params
    pair_count, seq_len, model_width = tokens.shape
    token_rows = low(tokens.reshape(pair_count * seq_len, model_width))
    raw_joined = jnp.dot(token_rows, project_weight, precision=HIGHEST)
    bias_full = jnp.concatenate([project_bias[:model_width], jnp.zeros((model_width,), project_bias.dtype), project_bias[model_width:]])
    joined = low(low_back(raw_joined) + bias_full)
    shaped = joined.reshape(pair_count, seq_len, 3, HEADS, HEAD_DIM)
    query_heads = shaped[:, :, 0]
    key_heads = shaped[:, :, 1]
    value_heads = shaped[:, :, 2]
    raw_scores = jnp.einsum('pqhd,pkhd->phqk', query_heads, key_heads, precision=HIGHEST)
    mask_bias = jnp.where(key_valid, 0.0, -1000000000.0).astype(raw_scores.dtype)
    scores = low_back(raw_scores) * HEAD_DIM ** (-0.5) + mask_bias[:, None, None, :]
    prob_low = low(jax.nn.softmax(scores, axis=-1))
    context = jnp.einsum('phqk,pkhd->pqhd', prob_low, value_heads, precision=HIGHEST)
    context_low = low(low_back(context.reshape(pair_count * seq_len, model_width)))
    branch = low_back(jnp.dot(context_low, output_weight, precision=HIGHEST)) + output_bias
    normed = layer_norm(token_rows + branch, first_gain, first_shift)
    expand = low_back(jnp.dot(low(normed), expand_weight, precision=HIGHEST)) + expand_bias
    active_low = low(gelu_exact(expand))
    shrink = low_back(jnp.dot(active_low, shrink_weight, precision=HIGHEST)) + shrink_bias
    result = layer_norm(normed + shrink, second_gain, second_shift)
    return result.reshape(pair_count, seq_len, model_width)

def reference(tokens, captions, cotangent, project_weight, project_bias, output_weight, output_bias, first_gain, first_shift, expand_weight, expand_bias, shrink_weight, shrink_bias, second_gain, second_shift):
    params = (project_weight.astype(jnp.float32), project_bias.astype(jnp.float32), output_weight.astype(jnp.float32), output_bias.astype(jnp.float32), first_gain.astype(jnp.float32), first_shift.astype(jnp.float32), expand_weight.astype(jnp.float32), expand_bias.astype(jnp.float32), shrink_weight.astype(jnp.float32), shrink_bias.astype(jnp.float32), second_gain.astype(jnp.float32), second_shift.astype(jnp.float32))
    group_count = N_FSDP
    group_size = PAIRS_DEV * N_DP
    seq_len = tokens.shape[1]
    model_width = tokens.shape[2]
    token_groups = tokens.astype(jnp.float32).reshape(group_count, group_size, seq_len, model_width)
    cot_groups = cotangent.astype(jnp.float32).reshape(group_count, group_size, seq_len, model_width)
    caption_groups = captions.reshape(group_count, group_size)
    positions = jnp.arange(seq_len, dtype=jnp.int32)

    def group_step(running, group_items):
        token_group, cot_group, caption_group = group_items
        key_valid = positions[None, :] < caption_group[:, None] + 2 + REGIONS
        group_out, pullback = jax.vjp(lambda inputs, weights: layer_forward(inputs, key_valid, weights), token_group, params)
        cot_masked = cot_group * key_valid[:, :, None].astype(cot_group.dtype)
        token_part, param_part = pullback(cot_masked)
        running = jax.tree.map(lambda left, right: left + right, running, param_part)
        return (running, (group_out.astype(jnp.bfloat16), token_part))
    zeros_start = tuple((jnp.zeros_like(array) for array in params))
    totals, (outputs, token_parts) = lax.scan(group_step, zeros_start, (token_groups, cot_groups, caption_groups))
    layer_out = outputs.reshape(tokens.shape)
    token_grad = token_parts.reshape(tokens.shape)
    return (layer_out, token_grad, totals[0], totals[1], totals[2], totals[3], totals[4], totals[5], totals[6], totals[7], totals[8], totals[9], totals[10], totals[11])
```

```python
import functools

import jax
import jax.numpy as jnp
from jax import lax
from jax.experimental import pallas as pl
from jax.experimental.pallas import tpu as pltpu
from jax.sharding import PartitionSpec as P

HEADS = 12
HEAD_DIM = 64
REGIONS = 36
BF16 = jnp.bfloat16
F32 = jnp.float32
VMEM_LIMIT = 56 * 1024 * 1024

NN = (((1,), (0,)), ((), ()))
NT = (((1,), (1,)), ((), ()))
TN = (((0,), (0,)), ((), ()))


def dot(left, right, dims=NN):
    return lax.dot_general(left, right, dims, preferred_element_type=F32)


def params():
    return pltpu.CompilerParams(vmem_limit_bytes=VMEM_LIMIT)


def cost(flops, moved):
    return pl.CostEstimate(flops=flops, bytes_accessed=moved, transcendentals=0)


def whole(shape):
    return pl.BlockSpec(shape, lambda *at: (0,) * len(shape))


def tile_of(size, most):
    return max(t for t in range(128, most + 1, 128) if size % t == 0)


def rows_of(count, most):
    fits = [t for t in range(16, most + 1, 16) if count % t == 0]
    return max(fits) if fits else count


def join_kernel(tokens, weight, bias, out):
    out[...] = (dot(tokens[...], weight[...]) + bias[...]).astype(BF16)


def join(token_rows, weight, bias):
    rows, width = token_rows.shape
    columns = weight.shape[1]
    tile = tile_of(columns, 768)
    return pl.pallas_call(
        join_kernel,
        grid=(columns // tile,),
        in_specs=[
            whole((rows, width)),
            pl.BlockSpec((width, tile), lambda i: (0, i)),
            pl.BlockSpec((1, tile), lambda i: (0, i)),
        ],
        out_specs=pl.BlockSpec((rows, tile), lambda i: (0, i)),
        out_shape=jax.ShapeDtypeStruct((rows, columns), BF16),
        compiler_params=params(),
        cost_estimate=cost(2 * rows * width * columns, 2 * (width * columns + rows * columns)),
        name="join",
    )(token_rows, weight, bias)


def head_stack(block, low_half, padded):
    rows = block.shape[0]
    filler = jnp.zeros((padded - rows, block.shape[1]), F32)
    first = jnp.where(low_half, block, 0.0)
    second = jnp.where(low_half, 0.0, block)
    return jnp.concatenate([first, filler, second, filler], axis=0).astype(BF16)


def attend_kernel(captions, joined, context, probs):
    seq = joined.shape[1]
    width = context.shape[2]
    padded = probs.shape[3] // 2
    valid = captions[pl.program_id(0)] + 2 + REGIONS
    keep = lax.broadcasted_iota(jnp.int32, (seq, 2 * padded), 0) < valid
    low_half = lax.broadcasted_iota(jnp.int32, (1, 2 * HEAD_DIM), 1) < HEAD_DIM
    for pair in range(HEADS // 2):
        at = pair * 2 * HEAD_DIM
        query = joined[0, :, at : at + 2 * HEAD_DIM].astype(F32)
        keys = joined[0, :, width + at : width + at + 2 * HEAD_DIM]
        values = joined[0, :, 2 * width + at : 2 * width + at + 2 * HEAD_DIM]
        stacked = head_stack(query, low_half, padded)
        scores = dot(keys, stacked, NT) * HEAD_DIM ** (-0.5)
        scores = jnp.where(keep, scores, -1000000000.0)
        top = jnp.max(scores, axis=0, keepdims=True)
        grown = jnp.exp(scores - top)
        total = jnp.sum(grown, axis=0, keepdims=True)
        prob = (grown * (1.0 / total)).astype(BF16)
        probs[0, pair] = prob
        mixed = dot(prob, values, TN)
        context[0, :, at : at + 2 * HEAD_DIM] = jnp.where(
            low_half, mixed[:seq], mixed[padded : padded + seq]
        ).astype(BF16)


def attend(joined, captions):
    pairs, seq, columns = joined.shape
    width = columns // 3
    padded = (seq + 127) // 128 * 128
    return pl.pallas_call(
        attend_kernel,
        grid_spec=pltpu.PrefetchScalarGridSpec(
            num_scalar_prefetch=1,
            grid=(pairs,),
            in_specs=[pl.BlockSpec((1, seq, columns), lambda i, c: (i, 0, 0))],
            out_specs=[
                pl.BlockSpec((1, seq, width), lambda i, c: (i, 0, 0)),
                pl.BlockSpec((1, HEADS // 2, seq, 2 * padded), lambda i, c: (i, 0, 0, 0)),
            ],
        ),
        out_shape=[
            jax.ShapeDtypeStruct((pairs, seq, width), BF16),
            jax.ShapeDtypeStruct((pairs, HEADS // 2, seq, 2 * padded), BF16),
        ],
        compiler_params=params(),
        cost_estimate=cost(8 * pairs * seq * padded * width, 2 * joined.size),
        name="attend",
    )(captions, joined)


def attend_back_kernel(joined, probs, grads, out, sums):
    seq = joined.shape[1]
    width = grads.shape[2]
    padded = probs.shape[3] // 2
    low_half = lax.broadcasted_iota(jnp.int32, (1, 2 * HEAD_DIM), 1) < HEAD_DIM

    @pl.when(pl.program_id(0) == 0)
    def _():
        sums[...] = jnp.zeros_like(sums)

    for pair in range(HEADS // 2):
        at = pair * 2 * HEAD_DIM
        query = joined[0, :, at : at + 2 * HEAD_DIM].astype(F32)
        keys = joined[0, :, width + at : width + at + 2 * HEAD_DIM]
        values = joined[0, :, 2 * width + at : 2 * width + at + 2 * HEAD_DIM]
        grad = grads[0, :, at : at + 2 * HEAD_DIM].astype(F32)
        query_stack = head_stack(query, low_half, padded)
        grad_stack = head_stack(grad, low_half, padded)
        prob = probs[0, pair]
        prob_full = prob.astype(F32)
        prob_grad = dot(values, grad_stack, NT)
        row_dot = jnp.sum(prob_full * prob_grad, axis=0, keepdims=True)
        score_grad = (prob_full * (prob_grad - row_dot) * HEAD_DIM ** (-0.5)).astype(BF16)
        values_grad = dot(prob, grad_stack)
        keys_grad = dot(score_grad, query_stack)
        mixed = dot(score_grad, keys, TN)
        query_grad = jnp.where(low_half, mixed[:seq], mixed[padded : padded + seq])
        out[0, :, at : at + 2 * HEAD_DIM] = query_grad.astype(BF16)
        out[0, :, width + at : width + at + 2 * HEAD_DIM] = keys_grad.astype(BF16)
        out[0, :, 2 * width + at : 2 * width + at + 2 * HEAD_DIM] = values_grad.astype(BF16)
        sums[:, at : at + 2 * HEAD_DIM] += jnp.sum(query_grad, axis=0, keepdims=True)
        sums[:, width + at : width + at + 2 * HEAD_DIM] += jnp.sum(values_grad, axis=0, keepdims=True)


def attend_back(joined, probs, grads):
    pairs, seq, columns = joined.shape
    width = columns // 3
    padded = probs.shape[3] // 2
    return pl.pallas_call(
        attend_back_kernel,
        grid=(pairs,),
        in_specs=[
            pl.BlockSpec((1, seq, columns), lambda i: (i, 0, 0)),
            pl.BlockSpec((1, HEADS // 2, seq, 2 * padded), lambda i: (i, 0, 0, 0)),
            pl.BlockSpec((1, seq, width), lambda i: (i, 0, 0)),
        ],
        out_specs=[
            pl.BlockSpec((1, seq, columns), lambda i: (i, 0, 0)),
            pl.BlockSpec((1, 2 * width), lambda i: (0, 0)),
        ],
        out_shape=[
            jax.ShapeDtypeStruct((pairs, seq, columns), BF16),
            jax.ShapeDtypeStruct((1, 2 * width), F32),
        ],
        compiler_params=params(),
        cost_estimate=cost(20 * pairs * seq * padded * width, 5 * joined.size),
        name="attend_back",
    )(joined, probs, grads)


def norm_parts(values):
    centred = values - jnp.mean(values, axis=-1, keepdims=True)
    spread = jnp.mean(centred * centred, axis=-1, keepdims=True)
    scale = lax.rsqrt(spread + 1e-05)
    return centred * scale, scale


def norm_back(upstream, unit, scale, gain):
    scaled = upstream * gain
    return scale * (
        scaled
        - jnp.mean(scaled, axis=-1, keepdims=True)
        - unit * jnp.mean(scaled * unit, axis=-1, keepdims=True)
    )


def add_sums(sums, rows):
    @pl.when(pl.program_id(0) == 0)
    def _():
        sums[...] = jnp.zeros_like(sums)

    for at, values in enumerate(rows):
        sums[at : at + 1, :] += jnp.sum(values, axis=0, keepdims=True)


def first_kernel(context, weight, bias, tokens, gain, shift, unit, scale, normed_low):
    total = tokens[...].astype(F32) + (dot(context[...], weight[...]) + bias[...])
    unit_rows, scale_rows = norm_parts(total)
    unit[...] = unit_rows
    scale[...] = scale_rows
    normed_low[...] = (unit_rows * gain[...] + shift[...]).astype(BF16)


def first_norm(context, weight, bias, token_rows, gain, shift):
    rows, width = token_rows.shape
    tile = rows_of(rows, 416)
    block = pl.BlockSpec((tile, width), lambda i: (i, 0))
    return pl.pallas_call(
        first_kernel,
        grid=(rows // tile,),
        in_specs=[block, whole((width, width)), whole((1, width)), block, whole((1, width)), whole((1, width))],
        out_specs=[block, pl.BlockSpec((tile, 1), lambda i: (i, 0)), block],
        out_shape=[
            jax.ShapeDtypeStruct((rows, width), F32),
            jax.ShapeDtypeStruct((rows, 1), F32),
            jax.ShapeDtypeStruct((rows, width), BF16),
        ],
        compiler_params=params(),
        cost_estimate=cost(2 * rows * width * width, 10 * rows * width + 2 * width * width),
        name="first_norm",
    )(context, weight, bias, token_rows, gain, shift)


def expand_kernel(normed_low, weight, bias, active, slope):
    expand = dot(normed_low[...], weight[...]) + bias[...]
    half = 0.5 * (1.0 + lax.erf(expand * 0.7071067811865476))
    active[...] = (expand * half).astype(BF16)
    slope[...] = (half + expand * jnp.exp(-0.5 * expand * expand) * 0.3989422804014327).astype(BF16)


def expand_act(normed_low, weight, bias):
    rows, width = normed_low.shape
    columns = weight.shape[1]
    tile = tile_of(columns, 768)
    out = jax.ShapeDtypeStruct((rows, columns), BF16)
    block = pl.BlockSpec((rows, tile), lambda i: (0, i))
    return pl.pallas_call(
        expand_kernel,
        grid=(columns // tile,),
        in_specs=[
            whole((rows, width)),
            pl.BlockSpec((width, tile), lambda i: (0, i)),
            pl.BlockSpec((1, tile), lambda i: (0, i)),
        ],
        out_specs=[block, block],
        out_shape=[out, out],
        compiler_params=params(),
        cost_estimate=cost(2 * rows * width * columns, 2 * width * columns + 4 * rows * columns),
        name="expand_act",
    )(normed_low, weight, bias)


def second_kernel(captions, active, weight, bias, unit, gain, shift, gain2, shift2, cotangent, out, low, grad, sums, *, seq):
    normed = unit[...] * gain[...] + shift[...]
    total = normed + (dot(active[...], weight[...]) + bias[...])
    unit2, scale2 = norm_parts(total)
    out[...] = (unit2 * gain2[...] + shift2[...]).astype(BF16)
    tile = unit.shape[0]
    at = lax.broadcasted_iota(jnp.int32, (tile, 1), 0)
    live = jnp.zeros((tile, 1), jnp.bool_)
    for pair in range(tile // seq):
        count = captions[pl.program_id(0) * (tile // seq) + pair] + 2 + REGIONS
        live = live | ((at >= pair * seq) & (at < pair * seq + count))
    upstream = jnp.where(live, cotangent[...].astype(F32), 0.0)
    second = norm_back(upstream, unit2, scale2, gain2[...])
    grad[...] = second
    low[...] = second.astype(BF16)
    add_sums(sums, (upstream * unit2, upstream, second))


def second_norm(captions, active, weight, bias, unit, gain, shift, gain2, shift2, cotangent, seq):
    rows, width = unit.shape
    hidden = active.shape[1]
    tile = rows_of(rows, 416)
    block = pl.BlockSpec((tile, width), lambda i, c: (i, 0))
    row = whole((1, width))
    return pl.pallas_call(
        functools.partial(second_kernel, seq=seq),
        grid_spec=pltpu.PrefetchScalarGridSpec(
            num_scalar_prefetch=1,
            grid=(rows // tile,),
            in_specs=[
                pl.BlockSpec((tile, hidden), lambda i, c: (i, 0)),
                whole((hidden, width)),
                row, block, row, row, row, row, block,
            ],
            out_specs=[block, block, block, whole((8, width))],
        ),
        out_shape=[
            jax.ShapeDtypeStruct((rows, width), BF16),
            jax.ShapeDtypeStruct((rows, width), BF16),
            jax.ShapeDtypeStruct((rows, width), F32),
            jax.ShapeDtypeStruct((8, width), F32),
        ],
        compiler_params=params(),
        cost_estimate=cost(2 * rows * width * hidden, 2 * hidden * width + 2 * rows * hidden + 14 * rows * width),
        name="second_norm",
    )(captions, active, weight, bias, unit, gain, shift, gain2, shift2, cotangent)


def hidden_back_kernel(low, weight, slope, out, sums):
    grad = dot(low[...], weight[...], NT) * slope[...].astype(F32)
    out[...] = grad.astype(BF16)
    sums[...] = jnp.sum(grad, axis=0, keepdims=True)


def hidden_back(low, weight, slope):
    rows, width = low.shape
    hidden = weight.shape[0]
    tile = tile_of(hidden, 768)
    return pl.pallas_call(
        hidden_back_kernel,
        grid=(hidden // tile,),
        in_specs=[
            whole((rows, width)),
            pl.BlockSpec((tile, width), lambda i: (i, 0)),
            pl.BlockSpec((rows, tile), lambda i: (0, i)),
        ],
        out_specs=[
            pl.BlockSpec((rows, tile), lambda i: (0, i)),
            pl.BlockSpec((1, tile), lambda i: (0, i)),
        ],
        out_shape=[
            jax.ShapeDtypeStruct((rows, hidden), BF16),
            jax.ShapeDtypeStruct((1, hidden), F32),
        ],
        compiler_params=params(),
        cost_estimate=cost(2 * rows * width * hidden, 2 * hidden * width + 4 * rows * hidden),
        name="hidden_back",
    )(low, weight, slope)


def first_back_kernel(hidden, weight, second, unit, scale, gain, out_weight, grad, low, context_grad, sums):
    normed_grad = dot(hidden[...], weight[...], NT) + second[...]
    first = norm_back(normed_grad, unit[...], scale[...], gain[...])
    grad[...] = first
    first_low = first.astype(BF16)
    low[...] = first_low
    context_grad[...] = dot(first_low, out_weight[...], NT).astype(BF16)
    add_sums(sums, (normed_grad * unit[...], normed_grad, first))


def first_back(hidden, weight, second, unit, scale, gain, out_weight):
    rows, width = second.shape
    columns = hidden.shape[1]
    tile = rows_of(rows, 416)
    block = pl.BlockSpec((tile, width), lambda i: (i, 0))
    return pl.pallas_call(
        first_back_kernel,
        grid=(rows // tile,),
        in_specs=[
            pl.BlockSpec((tile, columns), lambda i: (i, 0)),
            whole((width, columns)),
            block, block,
            pl.BlockSpec((tile, 1), lambda i: (i, 0)),
            whole((1, width)),
            whole((width, width)),
        ],
        out_specs=[block, block, block, whole((8, width))],
        out_shape=[
            jax.ShapeDtypeStruct((rows, width), F32),
            jax.ShapeDtypeStruct((rows, width), BF16),
            jax.ShapeDtypeStruct((rows, width), BF16),
            jax.ShapeDtypeStruct((8, width), F32),
        ],
        compiler_params=params(),
        cost_estimate=cost(2 * rows * width * (columns + width), 2 * columns * width + 2 * rows * columns + 16 * rows * width),
        name="first_back",
    )(hidden, weight, second, unit, scale, gain, out_weight)


def token_back_kernel(grads, weight, first, out):
    out[...] = dot(grads[...], weight[...], NT) + first[...]


def token_back(grads, weight, first):
    rows, width = first.shape
    columns = grads.shape[1]
    tile = rows_of(rows, 416)
    block = pl.BlockSpec((tile, width), lambda i: (i, 0))
    return pl.pallas_call(
        token_back_kernel,
        grid=(rows // tile,),
        in_specs=[pl.BlockSpec((tile, columns), lambda i: (i, 0)), whole((width, columns)), block],
        out_specs=block,
        out_shape=jax.ShapeDtypeStruct((rows, width), F32),
        compiler_params=params(),
        cost_estimate=cost(2 * rows * width * columns, 2 * columns * (width + rows) + 8 * rows * width),
        name="token_back",
    )(grads, weight, first)


def weight_grad_kernel(left, right, out):
    out[...] = dot(left[...], right[...], TN).astype(BF16)


def weight_grad(left, right):
    rows, height = left.shape
    columns = right.shape[1]
    tile = tile_of(columns, 768)
    high = tile_of(height, 768)
    return pl.pallas_call(
        weight_grad_kernel,
        grid=(height // high, columns // tile),
        in_specs=[
            pl.BlockSpec((rows, high), lambda i, j: (0, i)),
            pl.BlockSpec((rows, tile), lambda i, j: (0, j)),
        ],
        out_specs=pl.BlockSpec((high, tile), lambda i, j: (i, j)),
        out_shape=jax.ShapeDtypeStruct((height, columns), BF16),
        compiler_params=params(),
        cost_estimate=cost(2 * rows * height * columns, 2 * (rows * height + rows * columns + height * columns)),
        name="weight_grad",
    )(left, right)


def gather(values):
    return lax.all_gather(values, "fsdp", axis=0, tiled=True)


def local(
    tokens,
    captions,
    cotangent,
    project_weight,
    project_bias,
    output_weight,
    output_bias,
    first_gain,
    first_shift,
    expand_weight,
    expand_bias,
    shrink_weight,
    shrink_bias,
    second_gain,
    second_shift,
):
    pairs, seq, width = tokens.shape
    rows = pairs * seq
    parts = lax.axis_size("fsdp")
    token_rows = tokens.reshape(rows, width)
    cot_rows = cotangent.reshape(rows, width)

    vectors = (project_bias, output_bias, first_gain, first_shift, expand_bias, shrink_bias, second_gain, second_shift)
    packed = gather(jnp.concatenate(vectors)[None, :])
    full, at = [], 0
    for vector in vectors:
        size = vector.shape[0]
        full.append(packed[:, at : at + size].reshape(1, parts * size).astype(F32))
        at += size
    bias_row, out_bias, gain1, shift1, hidden_bias, down_bias, gain2, shift2 = full
    bias_full = jnp.concatenate([bias_row[:, :width], jnp.zeros((1, width), F32), bias_row[:, width:]], axis=1)
    project = gather(project_weight)
    output = gather(output_weight)
    expand = gather(expand_weight)
    shrink = gather(shrink_weight)

    joined = join(token_rows, project, bias_full)
    joined3 = joined.reshape(pairs, seq, 3 * width)
    context, probs = attend(joined3, captions)
    context_rows = context.reshape(rows, width)
    unit1, scale1, normed_low = first_norm(context_rows, output, out_bias, token_rows, gain1, shift1)
    active, slope = expand_act(normed_low, expand, hidden_bias)
    out_rows, shrink_low, second_grad, sums2 = second_norm(
        captions, active, shrink, down_bias, unit1, gain1, shift1, gain2, shift2, cot_rows, seq
    )
    grad_shrink = weight_grad(active, shrink_low)
    expand_low, sums_hidden = hidden_back(shrink_low, shrink, slope)
    grad_expand = weight_grad(normed_low, expand_low)
    first_grad, branch_low, context_grad, sums1 = first_back(
        expand_low, expand, second_grad, unit1, scale1, gain1, output
    )
    grad_output = weight_grad(context_rows, branch_low)
    joined_grad, sums_joined = attend_back(joined3, probs, context_grad.reshape(pairs, seq, width))
    joined_grad_rows = joined_grad.reshape(rows, 3 * width)
    grad_project = weight_grad(token_rows, joined_grad_rows)
    token_grad = token_back(joined_grad_rows, project, first_grad)

    def owned(grad):
        part = lax.psum_scatter(grad, "fsdp", scatter_dimension=0, tiled=True)
        return lax.psum(part, "dp").astype(F32)

    small = (sums_joined[0], sums1[2], sums1[0], sums1[1], sums_hidden[0], sums2[2], sums2[0], sums2[1])
    packed_grad = jnp.concatenate([v.reshape(parts, -1) for v in small], axis=1).reshape(-1)
    shard = lax.psum(lax.psum_scatter(packed_grad, "fsdp", scatter_dimension=0, tiled=True), "dp")
    smalls, at = [], 0
    for vector in vectors:
        smalls.append(shard[at : at + vector.shape[0]])
        at += vector.shape[0]
    return (
        out_rows.reshape(pairs, seq, width),
        token_grad.reshape(pairs, seq, width),
        owned(grad_project),
        smalls[0],
        owned(grad_output),
        smalls[1],
        smalls[2],
        smalls[3],
        owned(grad_expand),
        smalls[4],
        owned(grad_shrink),
        smalls[5],
        smalls[6],
        smalls[7],
    )


def solution(mesh):
    rows3 = P(("dp", "fsdp"), None, None)
    matrix, vector = P("fsdp", None), P("fsdp")
    return jax.shard_map(
        local,
        mesh=mesh,
        in_specs=(
            rows3, P(("dp", "fsdp")), rows3,
            matrix, vector, matrix, vector, vector, vector,
            matrix, vector, matrix, vector, vector, vector,
        ),
        out_specs=(
            rows3, rows3,
            matrix, vector, matrix, vector, vector, vector,
            matrix, vector, matrix, vector, vector, vector,
        ),
        check_vma=False,
    )
```

```python
import functools

import jax
import jax.numpy as jnp
from jax import lax
from jax.experimental import pallas as pl
from jax.experimental.pallas import tpu as pltpu
from jax.sharding import PartitionSpec as P

HEADS = 12
HEAD_DIM = 64
REGIONS = 36
BF16 = jnp.bfloat16
F32 = jnp.float32

COVER = 100 * 10**9

NN = (((1,), (0,)), ((), ()))
NT = (((1,), (1,)), ((), ()))
TN = (((0,), (0,)), ((), ()))


def dot(left, right, dims=NN):
    return lax.dot_general(left, right, dims, preferred_element_type=F32)


def params(mebibytes):
    return pltpu.CompilerParams(vmem_limit_bytes=mebibytes * 1024 * 1024)


def cost(flops=0):
    return pl.CostEstimate(flops=flops, bytes_accessed=0, transcendentals=0)


def whole(shape, buffers=None):
    mode = None if buffers is None else pl.Buffered(buffers)
    return pl.BlockSpec(shape, lambda *at: (0,) * len(shape), pipeline_mode=mode)


HELD = pl.BlockSpec(memory_space=pltpu.VMEM)


def inside(shape, dtype=BF16):
    return pltpu.VMEM(shape, dtype)


def outside(shape, dtype=BF16):
    return pltpu.HBM(shape, dtype)


def in_vmem(values):
    return pltpu.with_memory_space_constraint(values, pltpu.VMEM)


def in_hbm(values):
    return pltpu.with_memory_space_constraint(values, pltpu.HBM)


def tile_of(size, most):
    return max(t for t in range(128, most + 1, 128) if size % t == 0)


def rows_of(count, most):
    fits = [t for t in range(16, most + 1, 16) if count % t == 0]
    return max(fits) if fits else count


def chip_of(pos, flip):
    return pos[0] ^ flip


def halves_copies(refs, into, pos, high, wide):
    half = wide // 2
    rows = high // 2
    for side in range(2):
        core = pos[1] if side == 0 else 1 - pos[1]
        shard = pos[0] * 2 + core
        yield refs[side], into.at[pl.ds(pl.multiple_of(shard * high, 16), high), :]
        for flip in range(4):
            buffer, at = refs[2 + side * 2 + (flip > 0)], max(flip - 1, 0) * 3 * rows
            up = pos[2] ^ (flip // 2)
            along = pos[3] ^ (flip % 2)
            for back in range(1, 4):
                shard = chip_of(pos, back) * 2 + core
                to_row = pl.multiple_of(shard * high + up * rows, 16)
                to_column = pl.multiple_of(along * half, 128)
                yield (
                    buffer.at[pl.ds(at + (back - 1) * rows, rows), :],
                    into.at[pl.ds(to_row, rows), pl.ds(to_column, half)],
                )


def stacked_copies(refs, into, pos, high, wide):
    rows = high // 8
    for side in range(2):
        core = pos[1] if side == 0 else 1 - pos[1]
        shard = pos[0] * 2 + core
        yield refs[side], into.at[pl.ds(pl.multiple_of(shard * high, 16), high), :]
        for flip in range(4):
            buffer, at = refs[2 + side * 2 + (flip > 0)], max(flip - 1, 0) * 3 * rows
            quarter = (pos[2] * 2 + pos[3]) ^ flip
            for back in range(1, 4):
                shard = chip_of(pos, back) * 2 + core
                for part in range(2):
                    to_row = pl.multiple_of(shard * high + (quarter * 2 + part) * rows, 16)
                    yield (
                        buffer.at[pl.ds(at + (back - 1) * rows, rows), pl.ds(part * wide, wide)],
                        into.at[pl.ds(to_row, rows), :],
                    )


MOST_PIECES = 64


def assemble(copies, refs, into, pos, sems):
    started = [
        pltpu.make_async_copy(source, target, sems.at[at])
        for at, (source, target) in enumerate(copies(refs, into, pos))
    ]
    for copy in started:
        copy.start()
    for copy in started:
        copy.wait()


ANYWHERE = pl.BlockSpec(memory_space=pl.ANY)


def natural_copies(refs, into, pos):
    yield refs[0], into


class Weight:
    def __init__(self, shape, arrays, copies=natural_copies):
        self.shape, self.copies = shape, copies
        self.arrays = [in_hbm(array) for array in arrays]

    def specs(self):
        return [ANYWHERE] * len(self.arrays)

    def out(self):
        return inside(self.shape)

    def scratch(self):
        return [pltpu.SemaphoreType.DMA((MOST_PIECES,))]

    def split(self, refs):
        return refs[: len(self.arrays)], refs[len(self.arrays) : -2], refs[-2], refs[-1]

    def arrive(self, refs, full, pos, sems):
        @pl.when(pl.program_id(0) == 0)
        def _():
            assemble(self.copies, refs, full, pos, sems)


def spread_kernel(pos, own, other, bias, hidden, rows, held):
    part = held.shape[2] * 3 // 4
    for back in range(4):
        held[chip_of(pos, back) * 2 + pos[1]] = own[back * 16 : back * 16 + 16].astype(F32)
        held[chip_of(pos, back) * 2 + 1 - pos[1]] = other[back * 16 : back * 16 + 16].astype(F32)
    bias[...] = jnp.zeros_like(bias)
    width = rows.shape[1]
    for shard in range(8):
        for at in range(2):
            to = (shard * 2 + at) * part
            to += width if to >= width else 0
            bias[0:1, to : to + part] = held[shard, at : at + 1, :part]
        for at in range(4):
            to = (shard * 4 + at) * part
            hidden[0:1, to : to + part] = held[shard, 5 + at : 6 + at, :part]
        to = shard * part
        rows[0:3, to : to + part] = held[shard, 2:5, :part]
        rows[3:6, to : to + part] = held[shard, 9:12, :part]


def spread(pos, shards, width, hidden_width):
    shapes = [(1, 3 * width), (1, hidden_width), (8, width)]
    return pl.pallas_call(
        spread_kernel,
        grid_spec=pltpu.PrefetchScalarGridSpec(
            num_scalar_prefetch=1,
            grid=(1,),
            in_specs=[whole((64, 128))] * 2,
            out_specs=[whole(shape) for shape in shapes],
            scratch_shapes=[pltpu.VMEM((8, 16, 128), F32)],
        ),
        out_shape=[jax.ShapeDtypeStruct(shape, F32) for shape in shapes],
        compiler_params=params(4),
        cost_estimate=cost(COVER),
        name="spread",
    )(pos, *shards)


def bundle_kernel(joined, first, second, hidden, out):
    part = out.shape[2] * 3 // 4
    out[...] = jnp.zeros_like(out)
    for shard in range(8):
        for at in range(2):
            of = (shard * 2 + at) * part
            out[shard, at : at + 1, :part] = joined[0:1, of : of + part]
        for at in range(4):
            of = (shard * 4 + at) * part
            out[shard, 5 + at : 6 + at, :part] = hidden[0:1, of : of + part]
        of = shard * part
        out[shard, 2:5, :part] = first[0:3, of : of + part]
        out[shard, 9:12, :part] = second[0:3, of : of + part]


def bundle(joined, first, second, hidden):
    return pl.pallas_call(
        bundle_kernel,
        out_shape=jax.ShapeDtypeStruct((8, 16, 128), F32),
        compiler_params=params(4),
        cost_estimate=cost(),
        name="bundle",
    )(joined, first, second, hidden)


def step_of(size):
    return pl.ds(pl.multiple_of(pl.program_id(0) * size, 16), size)


def columns_of(size):
    return pl.ds(pl.multiple_of(pl.program_id(0) * size, 128), size)


def join_kernel(pos, tokens, bias, *rest, weight, tile):
    pieces, (out,), full, sems = weight.split(rest)
    weight.arrive(pieces, full, pos, sems)
    out[...] = (dot(tokens[...], full[:, columns_of(tile)]) + bias[...]).astype(BF16)


def join(pos, token_rows, weight, bias):
    rows, width = token_rows.shape
    columns = weight.shape[1]
    tile = tile_of(columns, 768)
    return pl.pallas_call(
        functools.partial(join_kernel, weight=weight, tile=tile),
        grid_spec=pltpu.PrefetchScalarGridSpec(
            num_scalar_prefetch=1,
            grid=(columns // tile,),
            in_specs=[whole((rows, width), 1), pl.BlockSpec((1, tile), lambda i, p: (0, i))] + weight.specs(),
            out_specs=[pl.BlockSpec((rows, tile), lambda i, p: (0, i)), HELD],
            scratch_shapes=weight.scratch(),
        ),
        out_shape=[outside((rows, columns)), weight.out()],
        compiler_params=params(14),
        cost_estimate=cost(),
        name="join",
    )(pos, token_rows, bias, *weight.arrays)


def head_stack(block, low_half, padded):
    rows = block.shape[0]
    filler = jnp.zeros((padded - rows, block.shape[1]), F32)
    first = jnp.where(low_half, block, 0.0)
    second = jnp.where(low_half, 0.0, block)
    return jnp.concatenate([first, filler, second, filler], axis=0).astype(BF16)


def attend_kernel(captions, joined, context, probs):
    seq = joined.shape[1]
    width = context.shape[2]
    padded = probs.shape[3] // 2
    valid = captions[pl.program_id(0)] + 2 + REGIONS
    keep = lax.broadcasted_iota(jnp.int32, (seq, 2 * padded), 0) < valid
    low_half = lax.broadcasted_iota(jnp.int32, (1, 2 * HEAD_DIM), 1) < HEAD_DIM
    for pair in range(HEADS // 2):
        at = pair * 2 * HEAD_DIM
        query = joined[0, :, at : at + 2 * HEAD_DIM].astype(F32)
        keys = joined[0, :, width + at : width + at + 2 * HEAD_DIM]
        values = joined[0, :, 2 * width + at : 2 * width + at + 2 * HEAD_DIM]
        stacked = head_stack(query, low_half, padded)
        scores = dot(keys, stacked, NT) * HEAD_DIM ** (-0.5)
        scores = jnp.where(keep, scores, -1000000000.0)
        top = jnp.max(scores, axis=0, keepdims=True)
        grown = jnp.exp(scores - top)
        total = jnp.sum(grown, axis=0, keepdims=True)
        prob = (grown * (1.0 / total)).astype(BF16)
        probs[0, pair] = prob
        mixed = dot(prob, values, TN)
        context[0, :, at : at + 2 * HEAD_DIM] = jnp.where(
            low_half, mixed[:seq], mixed[padded : padded + seq]
        ).astype(BF16)


def attend(joined, captions):
    pairs, seq, columns = joined.shape
    width = columns // 3
    padded = (seq + 127) // 128 * 128
    return pl.pallas_call(
        attend_kernel,
        grid_spec=pltpu.PrefetchScalarGridSpec(
            num_scalar_prefetch=1,
            grid=(pairs,),
            in_specs=[pl.BlockSpec((1, seq, columns), lambda i, c: (i, 0, 0))],
            out_specs=[
                pl.BlockSpec((1, seq, width), lambda i, c: (i, 0, 0)),
                pl.BlockSpec((1, HEADS // 2, seq, 2 * padded), lambda i, c: (i, 0, 0, 0)),
            ],
        ),
        out_shape=[
            inside((pairs, seq, width)),
            outside((pairs, HEADS // 2, seq, 2 * padded)),
        ],
        compiler_params=params(8),
        cost_estimate=cost(),
        name="attend",
    )(captions, in_hbm(joined))


def attend_back_kernel(joined, probs, grads, out, sums):
    seq = joined.shape[1]
    width = grads.shape[2]
    padded = probs.shape[3] // 2
    low_half = lax.broadcasted_iota(jnp.int32, (1, 2 * HEAD_DIM), 1) < HEAD_DIM

    @pl.when(pl.program_id(0) == 0)
    def _():
        sums[...] = jnp.zeros_like(sums)

    for pair in range(HEADS // 2):
        at = pair * 2 * HEAD_DIM
        query = joined[0, :, at : at + 2 * HEAD_DIM].astype(F32)
        keys = joined[0, :, width + at : width + at + 2 * HEAD_DIM]
        values = joined[0, :, 2 * width + at : 2 * width + at + 2 * HEAD_DIM]
        grad = grads[0, :, at : at + 2 * HEAD_DIM].astype(F32)
        query_stack = head_stack(query, low_half, padded)
        grad_stack = head_stack(grad, low_half, padded)
        prob = probs[0, pair]
        prob_full = prob.astype(F32)
        prob_grad = dot(values, grad_stack, NT)
        row_dot = jnp.sum(prob_full * prob_grad, axis=0, keepdims=True)
        score_grad = (prob_full * (prob_grad - row_dot) * HEAD_DIM ** (-0.5)).astype(BF16)
        values_grad = dot(prob, grad_stack)
        keys_grad = dot(score_grad, query_stack)
        mixed = dot(score_grad, keys, TN)
        query_grad = jnp.where(low_half, mixed[:seq], mixed[padded : padded + seq])
        out[0, :, at : at + 2 * HEAD_DIM] = query_grad.astype(BF16)
        out[0, :, width + at : width + at + 2 * HEAD_DIM] = keys_grad.astype(BF16)
        out[0, :, 2 * width + at : 2 * width + at + 2 * HEAD_DIM] = values_grad.astype(BF16)
        sums[:, at : at + 2 * HEAD_DIM] += jnp.sum(query_grad, axis=0, keepdims=True)
        sums[:, width + at : width + at + 2 * HEAD_DIM] += jnp.sum(values_grad, axis=0, keepdims=True)


def attend_back(joined, probs, grads):
    pairs, seq, columns = joined.shape
    width = columns // 3
    padded = probs.shape[3] // 2
    return pl.pallas_call(
        attend_back_kernel,
        grid=(pairs,),
        in_specs=[
            pl.BlockSpec((1, seq, columns), lambda i: (i, 0, 0)),
            pl.BlockSpec((1, HEADS // 2, seq, 2 * padded), lambda i: (i, 0, 0, 0)),
            pl.BlockSpec((1, seq, width), lambda i: (i, 0, 0)),
        ],
        out_specs=[
            pl.BlockSpec((1, seq, columns), lambda i: (i, 0, 0)),
            pl.BlockSpec((1, 2 * width), lambda i: (0, 0)),
        ],
        out_shape=[
            inside((pairs, seq, columns)),
            jax.ShapeDtypeStruct((1, 2 * width), F32),
        ],
        compiler_params=params(10),
        cost_estimate=cost(),
        name="attend_back",
    )(in_hbm(joined), in_hbm(probs), in_vmem(grads))


def norm_parts(values):
    centred = values - jnp.mean(values, axis=-1, keepdims=True)
    spread = jnp.mean(centred * centred, axis=-1, keepdims=True)
    scale = lax.rsqrt(spread + 1e-05)
    return centred * scale, scale


def norm_back(upstream, unit, scale, gain):
    scaled = upstream * gain
    return scale * (
        scaled
        - jnp.mean(scaled, axis=-1, keepdims=True)
        - unit * jnp.mean(scaled * unit, axis=-1, keepdims=True)
    )


def add_sums(sums, rows):
    @pl.when(pl.program_id(0) == 0)
    def _():
        sums[...] = jnp.zeros_like(sums)

    for at, values in enumerate(rows):
        sums[at : at + 1, :] += jnp.sum(values, axis=0, keepdims=True)


def first_kernel(pos, context, bias, tokens, gain, shift, *rest, weight):
    pieces, (unit, scale, normed_low), full, sems = weight.split(rest)
    weight.arrive(pieces, full, pos, sems)
    at = step_of(tokens.shape[0])
    total = tokens[...].astype(F32) + (dot(context[at, :], full[...]) + bias[...])
    unit_rows, scale_rows = norm_parts(total)
    unit[at, :] = unit_rows
    scale[at, :] = scale_rows
    normed_low[at, :] = (unit_rows * gain[...] + shift[...]).astype(BF16)


def first_norm(pos, context, weight, bias, token_rows, gain, shift):
    rows, width = token_rows.shape
    tile = rows_of(rows, 416)
    row = whole((1, width))
    return pl.pallas_call(
        functools.partial(first_kernel, weight=weight),
        grid_spec=pltpu.PrefetchScalarGridSpec(
            num_scalar_prefetch=1,
            grid=(rows // tile,),
            in_specs=[HELD, row, pl.BlockSpec((tile, width), lambda i, p: (i, 0)), row, row] + weight.specs(),
            out_specs=[HELD] * 4,
            scratch_shapes=weight.scratch(),
        ),
        out_shape=[inside((rows, width), F32), inside((rows, 1), F32), inside((rows, width)), weight.out()],
        compiler_params=params(14),
        cost_estimate=cost(),
        name="first_norm",
    )(pos, in_vmem(context), bias, token_rows, gain, shift, *weight.arrays)


def expand_kernel(pos, normed_low, bias, *rest, weight, tile):
    pieces, (active, slope), full, sems = weight.split(rest)
    weight.arrive(pieces, full, pos, sems)
    at = columns_of(tile)
    expand = dot(normed_low[...], full[:, at]) + bias[...]
    half = 0.5 * (1.0 + lax.erf(expand * 0.7071067811865476))
    active[:, at] = (expand * half).astype(BF16)
    slope[:, at] = (half + expand * jnp.exp(-0.5 * expand * expand) * 0.3989422804014327).astype(BF16)


def expand_act(pos, normed_low, weight, bias):
    rows, width = normed_low.shape
    columns = weight.shape[1]
    tile = tile_of(columns, 768)
    return pl.pallas_call(
        functools.partial(expand_kernel, weight=weight, tile=tile),
        grid_spec=pltpu.PrefetchScalarGridSpec(
            num_scalar_prefetch=1,
            grid=(columns // tile,),
            in_specs=[HELD, pl.BlockSpec((1, tile), lambda i, p: (0, i))] + weight.specs(),
            out_specs=[HELD] * 3,
            scratch_shapes=weight.scratch(),
        ),
        out_shape=[inside((rows, columns))] * 2 + [weight.out()],
        compiler_params=params(16),
        cost_estimate=cost(),
        name="expand_act",
    )(pos, in_vmem(normed_low), bias, *weight.arrays)


def second_kernel(pos, captions, active, bias, unit, gain, shift, gain2, shift2, cotangent, *rest, weight, seq):
    pieces, (out, low, grad, sums), full, sems = weight.split(rest)
    weight.arrive(pieces, full, pos, sems)
    tile = out.shape[0]
    at = step_of(tile)
    normed = unit[at, :] * gain[...] + shift[...]
    total = normed + (dot(active[at, :], full[...]) + bias[...])
    unit2, scale2 = norm_parts(total)
    out[...] = (unit2 * gain2[...] + shift2[...]).astype(BF16)
    row = lax.broadcasted_iota(jnp.int32, (tile, 1), 0)
    live = jnp.zeros((tile, 1), jnp.bool_)
    for pair in range(tile // seq):
        count = captions[pl.program_id(0) * (tile // seq) + pair] + 2 + REGIONS
        live = live | ((row >= pair * seq) & (row < pair * seq + count))
    upstream = jnp.where(live, cotangent[...].astype(F32), 0.0)
    second = norm_back(upstream, unit2, scale2, gain2[...])
    grad[at, :] = second
    low[at, :] = second.astype(BF16)
    add_sums(sums, (second, upstream * unit2, upstream))


def second_norm(pos, captions, active, weight, bias, unit, gain, shift, gain2, shift2, cotangent, seq):
    rows, width = unit.shape
    hidden = active.shape[1]
    tile = rows_of(rows, 416)
    block = pl.BlockSpec((tile, width), lambda i, p, c: (i, 0))
    row = whole((1, width))
    return pl.pallas_call(
        functools.partial(second_kernel, weight=weight, seq=seq),
        grid_spec=pltpu.PrefetchScalarGridSpec(
            num_scalar_prefetch=2,
            grid=(rows // tile,),
            in_specs=[HELD, row, HELD, row, row, row, row, block] + weight.specs(),
            out_specs=[block, HELD, HELD, whole((8, width)), HELD],
            scratch_shapes=weight.scratch(),
        ),
        out_shape=[
            outside((rows, width)),
            inside((rows, width)),
            inside((rows, width), F32),
            jax.ShapeDtypeStruct((8, width), F32),
            weight.out(),
        ],
        compiler_params=params(18),
        cost_estimate=cost(),
        name="second_norm",
    )(pos, captions, in_vmem(active), bias, in_vmem(unit), gain, shift, gain2, shift2, cotangent, *weight.arrays)


def hidden_back_kernel(low, weight, slope, out, sums):
    at = columns_of(sums.shape[1])
    grad = dot(low[...], weight[at, :], NT) * slope[:, at].astype(F32)
    out[:, at] = grad.astype(BF16)
    sums[...] = jnp.sum(grad, axis=0, keepdims=True)


def hidden_back(low, weight, slope):
    rows, width = low.shape
    hidden = weight.shape[0]
    tile = tile_of(hidden, 768)
    return pl.pallas_call(
        hidden_back_kernel,
        grid=(hidden // tile,),
        in_specs=[HELD] * 3,
        out_specs=[HELD, pl.BlockSpec((1, tile), lambda i: (0, i))],
        out_shape=[inside((rows, hidden)), jax.ShapeDtypeStruct((1, hidden), F32)],
        compiler_params=params(14),
        cost_estimate=cost(),
        name="hidden_back",
    )(in_vmem(low), in_vmem(weight), in_vmem(slope))


def first_back_kernel(hidden, weight, second, unit, scale, gain, out_weight, grad, low, context_grad, sums):
    at = step_of(grad.shape[0])
    unit_rows = unit[at, :]
    normed_grad = dot(hidden[at, :], weight[...], NT) + second[at, :]
    first = norm_back(normed_grad, unit_rows, scale[at, :], gain[...])
    grad[...] = first
    first_low = first.astype(BF16)
    low[at, :] = first_low
    context_grad[at, :] = dot(first_low, out_weight[...], NT).astype(BF16)
    add_sums(sums, (first, normed_grad * unit_rows, normed_grad))


def first_back(hidden, weight, second, unit, scale, gain, out_weight):
    rows, width = second.shape
    columns = hidden.shape[1]
    tile = rows_of(rows, 416)
    return pl.pallas_call(
        first_back_kernel,
        grid=(rows // tile,),
        in_specs=[HELD] * 5 + [whole((1, width)), HELD],
        out_specs=[pl.BlockSpec((tile, width), lambda i: (i, 0)), HELD, HELD, whole((8, width))],
        out_shape=[
            outside((rows, width), F32),
            inside((rows, width)),
            inside((rows, width)),
            jax.ShapeDtypeStruct((8, width), F32),
        ],
        compiler_params=params(18),
        cost_estimate=cost(),
        name="first_back",
    )(in_vmem(hidden), in_vmem(weight), in_vmem(second), in_vmem(unit), in_vmem(scale), gain, in_vmem(out_weight))


def token_back_kernel(grads, weight, first, out):
    out[...] = dot(grads[step_of(out.shape[0]), :], weight[...], NT) + first[...]


def token_back(grads, weight, first):
    rows, width = first.shape
    columns = grads.shape[1]
    tile = rows_of(rows, 416)
    block = pl.BlockSpec((tile, width), lambda i: (i, 0))
    return pl.pallas_call(
        token_back_kernel,
        grid=(rows // tile,),
        in_specs=[HELD, HELD, block],
        out_specs=block,
        out_shape=outside((rows, width), F32),
        compiler_params=params(14),
        cost_estimate=cost(COVER),
        name="token_back",
    )(in_vmem(grads), in_vmem(weight), in_hbm(first))


def weight_grad_kernel(left, right, out):
    out[...] = dot(left[...], right[...], TN).astype(BF16)


def weight_grad(left, right):
    rows, height = left.shape
    columns = right.shape[1]
    tile = tile_of(columns, 768)
    high = tile_of(height, 768)
    return pl.pallas_call(
        weight_grad_kernel,
        grid=(height // high, columns // tile),
        in_specs=[
            pl.BlockSpec((rows, high), lambda i, j: (0, i)),
            pl.BlockSpec((rows, tile), lambda i, j: (0, j)),
        ],
        out_specs=pl.BlockSpec((high, tile), lambda i, j: (i, j)),
        out_shape=outside((height, columns)),
        compiler_params=params(24),
        cost_estimate=cost(),
        name="weight_grad",
    )(left, right)


def store_halves(out, core, grads, pos, rows, extra):
    for chip in range(4):
        ahead = chip ^ pos[0]
        for up in range(2):
            at = ((chip * 2 + core) * 2 + up) * rows
            across = up ^ pos[2]
            block = grads[at : at + rows].astype(BF16)
            out[ahead, across, 0, :, : block.shape[1]] = block
            if extra is not None:
                out[ahead, across, 0, :, block.shape[1] :] = jnp.zeros((rows, 128), BF16)
                out[ahead, across, 0, 0:16, block.shape[1] :] = extra[chip * 2 + core].astype(BF16)


def halves_grad_kernel(pos, left, right, *rest, tile):
    extra, (mine, theirs) = (rest[0] if len(rest) == 3 else None), rest[-2:]
    step = pl.program_id(0) * pl.num_programs(1) + pl.program_id(1)
    grads = dot(left[...], right[:, pl.ds(pl.multiple_of(step * tile, 128), tile)], TN)
    rows = mine.shape[3]

    @pl.when(pos[1] == 0)
    def _():
        store_halves(mine, 0, grads, pos, rows, extra)
        store_halves(theirs, 1, grads, pos, rows, extra)

    @pl.when(pos[1] == 1)
    def _():
        store_halves(mine, 1, grads, pos, rows, extra)
        store_halves(theirs, 0, grads, pos, rows, extra)


def halves_grad(pos, left, right, extra=None, held=True, flops=0):
    rows, height = left.shape
    half = right.shape[1] // 2
    tile = half if extra is not None else tile_of(half, 768)
    steps = half // tile
    room = 0 if extra is None else 128
    out = outside((4, 2, 2, height // 16, half + room))
    block = pl.BlockSpec((4, 2, 1, height // 16, tile + room), lambda i, j, p: (0, 0, i ^ p[3], 0, j))
    return pl.pallas_call(
        functools.partial(halves_grad_kernel, tile=tile),
        grid_spec=pltpu.PrefetchScalarGridSpec(
            num_scalar_prefetch=1,
            grid=(2, steps),
            in_specs=[HELD if held else whole((rows, height), 1), HELD]
            + ([] if extra is None else [whole(extra.shape)]),
            out_specs=[block, block],
        ),
        out_shape=[out, out],
        compiler_params=params(14),
        cost_estimate=cost(flops),
        name="halves_grad",
    )(pos, in_vmem(left) if held else left, in_vmem(right), *(() if extra is None else (extra,)))


def store_stacked(out, core, grads, pos, rows):
    wide = grads.shape[1]
    for quarter in range(4):
        for part in range(2):
            at = ((core * 4 + quarter) * 2 + part) * rows
            block = grads[at : at + rows].astype(BF16)
            out[0, (quarter // 2) ^ pos[2], (quarter % 2) ^ pos[3], :, part * wide : (part + 1) * wide] = block


def stacked_grad_kernel(pos, left, right, mine, theirs):
    wide = left.shape[1] // 4
    grads = dot(left[:, columns_of(wide)], right[...], TN)
    rows = mine.shape[3]

    @pl.when(pos[1] == 0)
    def _():
        store_stacked(mine, 0, grads, pos, rows)
        store_stacked(theirs, 1, grads, pos, rows)

    @pl.when(pos[1] == 1)
    def _():
        store_stacked(mine, 1, grads, pos, rows)
        store_stacked(theirs, 0, grads, pos, rows)


def stacked_grad(pos, left, right):
    rows, height = left.shape
    wide = right.shape[1]
    out = outside((4, 2, 2, height // 64, 2 * wide))
    block = pl.BlockSpec((1, 2, 2, height // 64, 2 * wide), lambda i, p: (i ^ p[0], 0, 0, 0, 0))
    return pl.pallas_call(
        stacked_grad_kernel,
        grid_spec=pltpu.PrefetchScalarGridSpec(
            num_scalar_prefetch=1,
            grid=(4,),
            in_specs=[HELD, HELD],
            out_specs=[block, block],
        ),
        out_shape=[out, out],
        compiler_params=params(14),
        cost_estimate=cost(),
        name="stacked_grad",
    )(pos, in_vmem(left), in_vmem(right))


def core_sum_kernel(*refs, count):
    outs = refs[2 * count :]
    for flip in range(4):
        at = 0
        for mine, theirs in zip(refs[:count], refs[count : 2 * count]):
            wide = mine.shape[4]
            pick = (0, flip // 2, flip % 2)
            outs[flip][0, :, at : at + wide] = (mine[pick].astype(F32) + theirs[pick].astype(F32)).astype(BF16)
            at += wide


def core_sum(mine, theirs):
    rows = mine[0].shape[3]
    wide = sum(m.shape[4] for m in mine)
    return pl.pallas_call(
        functools.partial(core_sum_kernel, count=len(mine)),
        grid=(4,),
        in_specs=[pl.BlockSpec((1,) + m.shape[1:], lambda i: (i, 0, 0, 0, 0)) for m in (*mine, *theirs)],
        out_specs=[pl.BlockSpec((1, rows, wide), lambda i: (i, 0, 0))] * 4,
        out_shape=[inside((4, rows, wide))] * 4,
        compiler_params=params(10),
        cost_estimate=cost(),
        name="core_sum",
    )(*map(in_hbm, (*mine, *theirs)))


def plane_sum_kernel(own, one, two, three, *outs):
    for flip in range(4):
        total = own[flip].astype(F32) + one[flip].astype(F32)
        total += two[flip].astype(F32) + three[flip].astype(F32)
        if len(outs) == 4:
            outs[flip][...] = total.astype(BF16)
        else:
            outs[flip // 2][flip % 2] = total.astype(BF16)


def plane_sum(parts, apart):
    _, rows, wide = parts[0].shape
    outs = [inside((rows, wide))] * 4 if apart else [inside((2, rows, wide))] * 2
    return pl.pallas_call(
        plane_sum_kernel,
        in_specs=[HELD] * 4,
        out_specs=[HELD] * len(outs),
        out_shape=outs,
        compiler_params=params(4),
        cost_estimate=cost(),
        name="plane_sum",
    )(*map(in_vmem, parts))


def pair_sum_kernel(near, received, one, two):
    one[...] = (near[0].astype(F32) + received[0].astype(F32)).astype(BF16)
    two[...] = (near[1].astype(F32) + received[1].astype(F32)).astype(BF16)


def pair_sum(near, received):
    _, rows, wide = near.shape
    return pl.pallas_call(
        pair_sum_kernel,
        in_specs=[HELD] * 2,
        out_specs=[HELD] * 2,
        out_shape=[inside((rows, wide))] * 2,
        compiler_params=params(4),
        cost_estimate=cost(),
        name="pair_sum",
    )(in_vmem(near), in_vmem(received))


def chip_sum_kernel(*refs, count):
    out, at = refs[-1], 0
    for group in range(count):
        terms = refs[group:-1:count]
        wide = terms[0].shape[1]
        total = terms[0][...].astype(F32)
        for term in terms[1:]:
            total += term[...].astype(F32)
        out[:, at : at + wide] = total.astype(BF16)
        at += wide


def chip_sum(*lists, flops=0):
    parts = [part for parts in lists for part in parts]
    rows = parts[0].shape[0]
    wide = sum(part.shape[1] for part in lists[0])
    return pl.pallas_call(
        functools.partial(chip_sum_kernel, count=len(lists[0])),
        in_specs=[HELD] * len(parts),
        out_specs=HELD,
        out_shape=inside((rows, wide)),
        compiler_params=params(4),
        cost_estimate=cost(flops),
        name="chip_sum",
    )(*map(in_vmem, parts))


def place_kernel(pos, *refs, layout):
    parts, outs = refs[:4], refs[4:]
    rows = parts[0].shape[0]
    for flip, part in enumerate(parts):
        up, along = pos[2] ^ (flip // 2), pos[3] ^ (flip % 2)
        at = 0
        for (kind, wide), out in zip(layout, outs):
            if kind == "halves":
                to_row = pl.multiple_of(up * rows, 16)
                to_column = pl.multiple_of(along * wide, 128)
                out[pl.ds(to_row, rows), pl.ds(to_column, wide)] = part[:, at : at + wide].astype(F32)
            elif kind == "stacked":
                for side in range(2):
                    to_row = pl.multiple_of(((up * 2 + along) * 2 + side) * rows, 16)
                    from_column = at + side * (wide // 2)
                    out[pl.ds(to_row, rows), :] = part[:, from_column : from_column + wide // 2].astype(F32)
            else:

                @pl.when((up == 0) & (along == 0))
                def _(out=out, part=part, at=at, wide=wide):
                    out[...] = part[0:16, at : at + wide].astype(F32)

            at += wide


def place(pos, parts, layout):
    rows = parts[0].shape[0]
    shapes = {
        "halves": lambda wide: (2 * rows, 2 * wide),
        "stacked": lambda wide: (8 * rows, wide // 2),
        "small": lambda wide: (16, wide),
    }
    outs = [jax.ShapeDtypeStruct(shapes[kind](wide), F32) for kind, wide in layout]
    return pl.pallas_call(
        functools.partial(place_kernel, layout=layout),
        grid_spec=pltpu.PrefetchScalarGridSpec(
            num_scalar_prefetch=1,
            grid=(1,),
            in_specs=[HELD] * 4,
            out_specs=[whole(out.shape, 1) for out in outs],
        ),
        out_shape=outs,
        compiler_params=params(10),
        cost_estimate=cost(),
        name="place",
    )(pos, *map(in_vmem, parts))


def from_core(values):
    return lax.ppermute(values, "fsdp", [(i, i ^ 1) for i in range(8)])


def from_plane(values):
    parts = values if isinstance(values, (list, tuple)) else [values] * 3
    return [
        lax.ppermute(part, "dp", [(i, i ^ flip) for i in range(4)]) for flip, part in zip((1, 2, 3), parts)
    ]


def from_chips(values):
    parts = values if isinstance(values, (list, tuple)) else [values] * 3
    return [from_chip(part, flip) for flip, part in zip((1, 2, 3), parts)]


def from_chip(values, flip):
    return lax.ppermute(values, "fsdp", [(i, i ^ (2 * flip)) for i in range(8)])


def below_kernel(*refs):
    at = 0
    for ref in refs[:-1]:
        rows, wide = ref.shape[0], refs[-1].shape[1]
        refs[-1][at : at + rows] = ref[:, :wide]
        at += rows


def below(*parts, wide=None):
    rows = sum(part.shape[0] for part in parts)
    return pl.pallas_call(
        below_kernel,
        in_specs=[HELD] * len(parts),
        out_specs=HELD,
        out_shape=inside((rows, wide or parts[0].shape[1])),
        compiler_params=params(4),
        cost_estimate=cost(),
        name="below",
    )(*map(in_vmem, parts))


def after(values, *others):
    return lax.optimization_barrier((values, others))[0]


def half_of(pos, shard):
    rows, wide = shard.shape[0] // 2, shard.shape[1] // 2
    return lax.dynamic_slice(shard, (pos[2] * rows, pos[3] * wide), (rows, wide))


def both_cores(pieces):
    return [*pieces, *(from_core(piece) for piece in pieces)]


def gather(values):
    return lax.all_gather(values, "fsdp", axis=0, tiled=True)


def local(
    pieces,
    tokens,
    captions,
    cotangent,
    project_weight,
    project_bias,
    output_weight,
    output_bias,
    first_gain,
    first_shift,
    expand_weight,
    expand_bias,
    shrink_weight,
    shrink_bias,
    second_gain,
    second_shift,
):
    pairs, seq, width = tokens.shape
    rows = pairs * seq
    parts = lax.axis_size("fsdp")
    token_rows = tokens.reshape(rows, width)
    cot_rows = cotangent.reshape(rows, width)

    vectors = (project_bias, output_bias, first_gain, first_shift, expand_bias, shrink_bias, second_gain, second_shift)
    widths = [vector.shape[0] for vector in vectors]
    replica, part = lax.axis_index("dp"), lax.axis_index("fsdp")
    pos = jnp.stack([part // 2, part % 2, replica // 2, replica % 2]).astype(jnp.int32)
    shapes = [(parts * shard.shape[0], shard.shape[1]) for shard in (project_weight, output_weight, expand_weight, shrink_weight)]
    if pieces:
        held = jnp.concatenate([vector.reshape(-1, 96) for vector in vectors], axis=0)
        held = jnp.pad(held, ((0, 4), (0, 32)))
        quarter_p, wide_p = half_of(pos, project_weight), project_weight.shape[1] // 2
        chips_p = from_chips(jnp.concatenate([quarter_p, jnp.pad(held, ((0, 32), (0, 0)))], axis=1))
        sibling_p = from_core(project_weight)
        chips_p = after(chips_p, sibling_p)
        mine_p = below(*chips_p, wide=wide_p)
        held = jnp.concatenate([held, *(chip[:16, wide_p:] for chip in chips_p)], axis=0)
        quarter_e = after(half_of(pos, expand_weight), *chips_p)
        one_e = from_chip(quarter_e, 1)
        plane_p = from_plane(mine_p)
        far_e = from_chip(below(quarter_e, one_e), 2)
        plane_p = below(*after(plane_p, one_e))
        other_p = [from_core(mine_p), from_core(plane_p)]
        project = Weight(
            shapes[0],
            [project_weight, sibling_p, mine_p, plane_p, *other_p],
            functools.partial(halves_copies, high=project_weight.shape[0], wide=project_weight.shape[1]),
        )
        rows_s = shrink_weight.shape[0] // 8
        quarter_s = lax.dynamic_slice(
            shrink_weight, ((pos[2] * 2 + pos[3]) * 2 * rows_s, 0), (2 * rows_s, shrink_weight.shape[1])
        )
        quarter_s = jnp.concatenate([quarter_s[:rows_s], quarter_s[rows_s:]], axis=1)
        one_s = from_chip(after(quarter_s, plane_p), 1)
        mine_e = below(one_e, far_e)
        plane_e = from_plane(mine_e)
        held = after(held, mine_e)
        bias_full, hidden_bias, rows6 = spread(pos, [held, from_core(held)], width, expand_weight.shape[1])
        out_bias, gain1, shift1, down_bias, gain2, shift2 = (rows6[at : at + 1] for at in range(6))
    else:
        project, output, expand, shrink = (
            Weight(shape, [gather(shard)])
            for shape, shard in zip(shapes, (project_weight, output_weight, expand_weight, shrink_weight))
        )
        packed = gather(jnp.concatenate(vectors)[None, :])
        full, at = [], 0
        for size in widths:
            full.append(packed[:, at : at + size].reshape(1, parts * size).astype(F32))
            at += size
        bias_row, out_bias, gain1, shift1, hidden_bias, down_bias, gain2, shift2 = full
        bias_full = jnp.concatenate([bias_row[:, :width], jnp.zeros((1, width), F32), bias_row[:, width:]], axis=1)

    joined, project = join(pos, token_rows, project, bias_full)
    joined3 = joined.reshape(pairs, seq, 3 * width)
    if pieces:
        output = Weight(shapes[1], [gather(after(output_weight, far_e))])
        far_s = below(quarter_s, after(one_s, joined))
        joined3 = after(joined3, far_s)
        far_s = from_chip(far_s, 2)
    context, probs = attend(joined3, captions)
    context_rows = context.reshape(rows, width)
    if pieces:
        far_s = after(far_s, context)
        plane_e = below(*after(plane_e, far_s))
        other_e = [from_core(mine_e), from_core(plane_e)]
        sibling_e = from_core(after(expand_weight, context))
        expand = Weight(
            shapes[2],
            [expand_weight, sibling_e, mine_e, plane_e, *other_e],
            functools.partial(halves_copies, high=expand_weight.shape[0], wide=expand_weight.shape[1]),
        )
        mine_s = below(one_s, after(far_s, plane_e))
        plane_s = from_plane(mine_s)
        context_rows = after(context_rows, mine_s)
    unit1, scale1, normed_low, output = first_norm(pos, context_rows, output, out_bias, token_rows, gain1, shift1)
    active, slope, expand = expand_act(pos, normed_low, expand, hidden_bias)
    if pieces:
        plane_s = below(*after(plane_s, active))
        other_s = [from_core(mine_s), from_core(plane_s)]
        sibling_s = from_core(after(shrink_weight, active))
        shrink = Weight(
            shapes[3],
            [shrink_weight, sibling_s, mine_s, plane_s, *other_s],
            functools.partial(stacked_copies, high=shrink_weight.shape[0], wide=shrink_weight.shape[1]),
        )
    out_rows, shrink_low, second_grad, sums2, shrink = second_norm(
        pos, captions, active, shrink, down_bias, unit1, gain1, shift1, gain2, shift2, cot_rows, seq
    )
    if pieces:
        mine_s, theirs_s = stacked_grad(pos, active, shrink_low)
        theirs_s = from_core(theirs_s)
        shrink_low = after(shrink_low, mine_s)
    else:
        grad_shrink = weight_grad(active, shrink_low)
    expand_low, sums_hidden = hidden_back(shrink_low, shrink, slope)
    if pieces:
        own_s, *out_s = core_sum([mine_s], [after(theirs_s, expand_low)])
        plane_s = from_plane(out_s)
        expand_low = after(expand_low, own_s)
        mine_e, theirs_e = halves_grad(pos, normed_low, expand_low)
        theirs_e = from_core(theirs_e)
        expand_low = after(expand_low, mine_e)
    first_grad, branch_low, context_grad, sums1 = first_back(
        expand_low, expand, second_grad, unit1, scale1, gain1, output
    )
    if pieces:
        near_s, far_s = plane_sum([own_s, *after(plane_s, branch_low)], False)
        far_s = from_chip(far_s, 2)
        mine_o, theirs_o = halves_grad(pos, context_rows, after(branch_low, near_s), flops=COVER)
        theirs_o = from_core(theirs_o)
        own_eo, *out_eo = core_sum([mine_e, mine_o], after([theirs_e, theirs_o], mine_o))
        plane_eo = from_plane(out_eo)
        context_grad = after(context_grad, own_eo)
    else:
        grad_expand = weight_grad(normed_low, expand_low)
        grad_output = weight_grad(context_rows, branch_low)
    joined_grad, sums_joined = attend_back(joined3, probs, context_grad.reshape(pairs, seq, width))
    joined_grad_rows = joined_grad.reshape(rows, 3 * width)
    if pieces:
        near_s, last_s = pair_sum(near_s, after(far_s, joined_grad))
        last_s = from_chip(last_s, 1)
        extra = after(bundle(sums_joined, sums1, sums2, sums_hidden), near_s)
        mine_p, theirs_p = halves_grad(pos, token_rows, joined_grad_rows, extra, held=False)
        theirs_p = from_core(theirs_p)
        near_eo, far_eo = plane_sum([own_eo, *after(plane_eo, mine_p)], False)
        far_eo = from_chip(far_eo, 2)
        joined_grad_rows = after(joined_grad_rows, near_eo)
    else:
        grad_project = weight_grad(token_rows, joined_grad_rows)

        def owned(grad):
            part = lax.psum_scatter(grad, "fsdp", scatter_dimension=0, tiled=True)
            return lax.psum(part, "dp").astype(F32)

        own_project, own_output, own_expand, own_shrink = (
            owned(grad) for grad in (grad_project, grad_output, grad_expand, grad_shrink)
        )
        small = (sums_joined[0], sums1[0], sums1[1], sums1[2], sums_hidden[0], sums2[0], sums2[1], sums2[2])
        packed_grad = jnp.concatenate([v.reshape(parts, -1) for v in small], axis=1)
        shard = lax.psum(lax.psum_scatter(packed_grad.reshape(-1), "fsdp", scatter_dimension=0, tiled=True), "dp")
    token_grad = token_back(joined_grad_rows, project, first_grad)
    if pieces:
        half_p, half_e, half_o = project_weight.shape[1] // 2, expand_weight.shape[1] // 2, width // 2
        own_p, *out_p = core_sum([mine_p], [after(theirs_p, token_grad)])
        plane_p = from_plane(out_p)
        near_eo, last_eo = pair_sum(near_eo, after(far_eo, own_p))
        last_eo = from_chip(last_eo, 1)
        ahead_p = plane_sum([own_p, *after(plane_p, near_eo)], True)
        chips_p = from_chips(ahead_p[1:])
        total_seo = chip_sum([near_s, near_eo], after([last_s, last_eo], ahead_p[0]))
        quarters_seo = from_plane(total_seo)
        total_p = chip_sum([ahead_p[0]], *([chip] for chip in after(chips_p, total_seo)), flops=COVER)
        quarters_p = from_plane(after(total_p, *quarters_seo))
        own_shrink, own_expand, own_output = place(
            pos, [total_seo, *after(quarters_seo, total_p)], (("stacked", 2 * width), ("halves", half_e), ("halves", half_o))
        )
        own_project, shard = place(
            pos, [total_p, *after(quarters_p, own_expand)], (("halves", half_p), ("small", 128))
        )
        shard = shard[:12, :96].reshape(-1)

    smalls, at = [], 0
    for size in widths:
        smalls.append(shard[at : at + size])
        at += size
    return (
        out_rows.reshape(pairs, seq, width),
        token_grad.reshape(pairs, seq, width),
        own_project,
        smalls[0],
        own_output,
        smalls[1],
        smalls[2],
        smalls[3],
        own_expand,
        smalls[4],
        own_shrink,
        smalls[5],
        smalls[6],
        smalls[7],
    )


def solution(mesh):
    rows3 = P(("dp", "fsdp"), None, None)
    matrix, vector = P("fsdp", None), P("fsdp")
    pieces = mesh.shape["dp"] == 4 and mesh.shape["fsdp"] == 8
    return jax.shard_map(
        functools.partial(local, pieces),
        mesh=mesh,
        in_specs=(
            rows3, P(("dp", "fsdp")), rows3,
            matrix, vector, matrix, vector, vector, vector,
            matrix, vector, matrix, vector, vector, vector,
        ),
        out_specs=(
            rows3, rows3,
            matrix, vector, matrix, vector, vector, vector,
            matrix, vector, matrix, vector, vector, vector,
        ),
        check_vma=False,
    )
```

```python
import functools

import jax
import jax.numpy as jnp
from jax import lax
from jax.experimental import pallas as pl
from jax.experimental.pallas import tpu as pltpu
from jax.sharding import PartitionSpec as P

HEADS = 12
HEAD_DIM = 64
REGIONS = 36
BF16 = jnp.bfloat16
F32 = jnp.float32

COVER = 100 * 10**9

NN = (((1,), (0,)), ((), ()))
NT = (((1,), (1,)), ((), ()))
TN = (((0,), (0,)), ((), ()))


def dot(left, right, dims=NN):
    return lax.dot_general(left, right, dims, preferred_element_type=F32)


def params(mebibytes):
    return pltpu.CompilerParams(vmem_limit_bytes=mebibytes * 1024 * 1024)


def cost(flops=0):
    return pl.CostEstimate(flops=flops, bytes_accessed=0, transcendentals=0)


def whole(shape, buffers=None):
    mode = None if buffers is None else pl.Buffered(buffers)
    return pl.BlockSpec(shape, lambda *at: (0,) * len(shape), pipeline_mode=mode)


HELD = pl.BlockSpec(memory_space=pltpu.VMEM)


def inside(shape, dtype=BF16):
    return pltpu.VMEM(shape, dtype)


def outside(shape, dtype=BF16):
    return pltpu.HBM(shape, dtype)


def in_vmem(values):
    return pltpu.with_memory_space_constraint(values, pltpu.VMEM)


def in_hbm(values):
    return pltpu.with_memory_space_constraint(values, pltpu.HBM)


def tile_of(size, most):
    return max(t for t in range(128, most + 1, 128) if size % t == 0)


def rows_of(count, most):
    fits = [t for t in range(16, most + 1, 16) if count % t == 0]
    return max(fits) if fits else count


CHIPS = (1, 3, 2)


def halves_copies(refs, into, pos, at, high, wide):
    half = wide // 2
    rows = high // 2
    for side in range(2):
        core = pos[1] if side == 0 else 1 - pos[1]
        shard = pos[0] * 2 + core
        yield refs[side], into.at[pl.ds(pl.multiple_of(shard * high, 16), high), :]
        for flip in range(4):
            buffer, first = refs[2 + side * 2 + (flip > 0)], max(flip - 1, 0) * 3 * rows
            up = pos[2] ^ (flip // 2)
            along = pos[3] ^ (flip % 2)
            for place, chip in enumerate(CHIPS):
                shard = (pos[0] ^ chip) * 2 + core
                to_row = pl.multiple_of(shard * high + up * rows, 16)
                to_column = pl.multiple_of(along * half, 128)
                yield (
                    buffer.at[pl.ds(first + place * rows, rows), pl.ds(at, half)],
                    into.at[pl.ds(to_row, rows), pl.ds(to_column, half)],
                )


def stacked_copies(refs, into, pos, high, wide):
    rows = high // 8
    for side in range(2):
        core = pos[1] if side == 0 else 1 - pos[1]
        shard = pos[0] * 2 + core
        yield refs[side], into.at[pl.ds(pl.multiple_of(shard * high, 16), high), :]
        for flip in range(4):
            buffer, first = refs[2 + side * 2 + (flip > 0)], max(flip - 1, 0) * 3 * rows
            quarter = (pos[2] * 2 + pos[3]) ^ flip
            for place, chip in enumerate(CHIPS):
                shard = (pos[0] ^ chip) * 2 + core
                for part in range(2):
                    to_row = pl.multiple_of(shard * high + (quarter * 2 + part) * rows, 16)
                    yield (
                        buffer.at[pl.ds(first + place * rows, rows), pl.ds(part * wide, wide)],
                        into.at[pl.ds(to_row, rows), :],
                    )


MOST_PIECES = 64


def assemble(copies, refs, into, pos, sems):
    started = [
        pltpu.make_async_copy(source, target, sems.at[at])
        for at, (source, target) in enumerate(copies(refs, into, pos))
    ]
    for copy in started:
        copy.start()
    for copy in started:
        copy.wait()


ANYWHERE = pl.BlockSpec(memory_space=pl.ANY)


def natural_copies(refs, into, pos):
    yield refs[0], into


class Weight:
    def __init__(self, shape, arrays, copies=natural_copies):
        self.shape, self.copies = shape, copies
        self.arrays = [in_hbm(array) for array in arrays]

    def specs(self):
        return [ANYWHERE] * len(self.arrays)

    def out(self):
        return inside(self.shape)

    def scratch(self):
        return [pltpu.SemaphoreType.DMA((MOST_PIECES,))]

    def split(self, refs):
        return refs[: len(self.arrays)], refs[len(self.arrays) : -2], refs[-2], refs[-1]

    def arrive(self, refs, full, pos, sems):
        @pl.when(pl.program_id(0) == 0)
        def _():
            assemble(self.copies, refs, full, pos, sems)


def spread_kernel(pos, own, other, bias, hidden, rows, held):
    part = held.shape[2] * 3 // 4
    for at, chip in enumerate((0, *CHIPS)):
        held[(pos[0] ^ chip) * 2 + pos[1]] = own[at * 16 : at * 16 + 16].astype(F32)
        held[(pos[0] ^ chip) * 2 + 1 - pos[1]] = other[at * 16 : at * 16 + 16].astype(F32)
    bias[...] = jnp.zeros_like(bias)
    width = rows.shape[1]
    for shard in range(8):
        for at in range(2):
            to = (shard * 2 + at) * part
            to += width if to >= width else 0
            bias[0:1, to : to + part] = held[shard, at : at + 1, :part]
        for at in range(4):
            to = (shard * 4 + at) * part
            hidden[0:1, to : to + part] = held[shard, 5 + at : 6 + at, :part]
        to = shard * part
        rows[0:3, to : to + part] = held[shard, 2:5, :part]
        rows[3:6, to : to + part] = held[shard, 9:12, :part]


def spread(pos, shards, width, hidden_width):
    shapes = [(1, 3 * width), (1, hidden_width), (8, width)]
    return pl.pallas_call(
        spread_kernel,
        grid_spec=pltpu.PrefetchScalarGridSpec(
            num_scalar_prefetch=1,
            grid=(1,),
            in_specs=[whole((64, 128))] * 2,
            out_specs=[whole(shape) for shape in shapes],
            scratch_shapes=[pltpu.VMEM((8, 16, 128), F32)],
        ),
        out_shape=[jax.ShapeDtypeStruct(shape, F32) for shape in shapes],
        compiler_params=params(4),
        cost_estimate=cost(COVER),
        name="spread",
    )(pos, *shards)


def bundle_kernel(joined, first, second, hidden, out):
    part = out.shape[2] * 3 // 4
    out[...] = jnp.zeros_like(out)
    for shard in range(8):
        for at in range(2):
            of = (shard * 2 + at) * part
            out[shard, at : at + 1, :part] = joined[0:1, of : of + part]
        for at in range(4):
            of = (shard * 4 + at) * part
            out[shard, 5 + at : 6 + at, :part] = hidden[0:1, of : of + part]
        of = shard * part
        out[shard, 2:5, :part] = first[0:3, of : of + part]
        out[shard, 9:12, :part] = second[0:3, of : of + part]


def bundle(joined, first, second, hidden):
    return pl.pallas_call(
        bundle_kernel,
        out_shape=jax.ShapeDtypeStruct((8, 16, 128), F32),
        compiler_params=params(4),
        cost_estimate=cost(),
        name="bundle",
    )(joined, first, second, hidden)


def step_of(size):
    return pl.ds(pl.multiple_of(pl.program_id(0) * size, 16), size)


def columns_of(size):
    return pl.ds(pl.multiple_of(pl.program_id(0) * size, 128), size)


def join_kernel(pos, tokens, bias, *rest, weight, tile):
    pieces, (out,), full, sems = weight.split(rest)
    weight.arrive(pieces, full, pos, sems)
    out[...] = (dot(tokens[...], full[:, columns_of(tile)]) + bias[...]).astype(BF16)


def join(pos, token_rows, weight, bias):
    rows, width = token_rows.shape
    columns = weight.shape[1]
    tile = tile_of(columns, 768)
    return pl.pallas_call(
        functools.partial(join_kernel, weight=weight, tile=tile),
        grid_spec=pltpu.PrefetchScalarGridSpec(
            num_scalar_prefetch=1,
            grid=(columns // tile,),
            in_specs=[whole((rows, width), 1), pl.BlockSpec((1, tile), lambda i, p: (0, i))] + weight.specs(),
            out_specs=[pl.BlockSpec((rows, tile), lambda i, p: (0, i)), HELD],
            scratch_shapes=weight.scratch(),
        ),
        out_shape=[outside((rows, columns)), weight.out()],
        compiler_params=params(14),
        cost_estimate=cost(),
        name="join",
    )(pos, token_rows, bias, *weight.arrays)


def head_stack(block, low_half, padded):
    rows = block.shape[0]
    filler = jnp.zeros((padded - rows, block.shape[1]), F32)
    first = jnp.where(low_half, block, 0.0)
    second = jnp.where(low_half, 0.0, block)
    return jnp.concatenate([first, filler, second, filler], axis=0).astype(BF16)


def attend_kernel(captions, joined, context, probs):
    seq = joined.shape[1]
    width = context.shape[2]
    padded = probs.shape[3] // 2
    valid = captions[pl.program_id(0)] + 2 + REGIONS
    keep = lax.broadcasted_iota(jnp.int32, (seq, 2 * padded), 0) < valid
    low_half = lax.broadcasted_iota(jnp.int32, (1, 2 * HEAD_DIM), 1) < HEAD_DIM
    for pair in range(HEADS // 2):
        at = pair * 2 * HEAD_DIM
        query = joined[0, :, at : at + 2 * HEAD_DIM].astype(F32)
        keys = joined[0, :, width + at : width + at + 2 * HEAD_DIM]
        values = joined[0, :, 2 * width + at : 2 * width + at + 2 * HEAD_DIM]
        stacked = head_stack(query, low_half, padded)
        scores = dot(keys, stacked, NT) * HEAD_DIM ** (-0.5)
        scores = jnp.where(keep, scores, -1000000000.0)
        top = jnp.max(scores, axis=0, keepdims=True)
        grown = jnp.exp(scores - top)
        total = jnp.sum(grown, axis=0, keepdims=True)
        prob = (grown * (1.0 / total)).astype(BF16)
        probs[0, pair] = prob
        mixed = dot(prob, values, TN)
        context[0, :, at : at + 2 * HEAD_DIM] = jnp.where(
            low_half, mixed[:seq], mixed[padded : padded + seq]
        ).astype(BF16)


def attend(joined, captions):
    pairs, seq, columns = joined.shape
    width = columns // 3
    padded = (seq + 127) // 128 * 128
    return pl.pallas_call(
        attend_kernel,
        grid_spec=pltpu.PrefetchScalarGridSpec(
            num_scalar_prefetch=1,
            grid=(pairs,),
            in_specs=[pl.BlockSpec((1, seq, columns), lambda i, c: (i, 0, 0))],
            out_specs=[
                pl.BlockSpec((1, seq, width), lambda i, c: (i, 0, 0)),
                pl.BlockSpec((1, HEADS // 2, seq, 2 * padded), lambda i, c: (i, 0, 0, 0)),
            ],
        ),
        out_shape=[
            inside((pairs, seq, width)),
            outside((pairs, HEADS // 2, seq, 2 * padded)),
        ],
        compiler_params=params(8),
        cost_estimate=cost(),
        name="attend",
    )(captions, in_hbm(joined))


def attend_back_kernel(joined, probs, grads, out, sums):
    seq = joined.shape[1]
    width = grads.shape[2]
    padded = probs.shape[3] // 2
    low_half = lax.broadcasted_iota(jnp.int32, (1, 2 * HEAD_DIM), 1) < HEAD_DIM

    @pl.when(pl.program_id(0) == 0)
    def _():
        sums[...] = jnp.zeros_like(sums)

    for pair in range(HEADS // 2):
        at = pair * 2 * HEAD_DIM
        query = joined[0, :, at : at + 2 * HEAD_DIM].astype(F32)
        keys = joined[0, :, width + at : width + at + 2 * HEAD_DIM]
        values = joined[0, :, 2 * width + at : 2 * width + at + 2 * HEAD_DIM]
        grad = grads[0, :, at : at + 2 * HEAD_DIM].astype(F32)
        query_stack = head_stack(query, low_half, padded)
        grad_stack = head_stack(grad, low_half, padded)
        prob = probs[0, pair]
        prob_full = prob.astype(F32)
        prob_grad = dot(values, grad_stack, NT)
        row_dot = jnp.sum(prob_full * prob_grad, axis=0, keepdims=True)
        score_grad = (prob_full * (prob_grad - row_dot) * HEAD_DIM ** (-0.5)).astype(BF16)
        values_grad = dot(prob, grad_stack)
        keys_grad = dot(score_grad, query_stack)
        mixed = dot(score_grad, keys, TN)
        query_grad = jnp.where(low_half, mixed[:seq], mixed[padded : padded + seq])
        out[0, :, at : at + 2 * HEAD_DIM] = query_grad.astype(BF16)
        out[0, :, width + at : width + at + 2 * HEAD_DIM] = keys_grad.astype(BF16)
        out[0, :, 2 * width + at : 2 * width + at + 2 * HEAD_DIM] = values_grad.astype(BF16)
        sums[:, at : at + 2 * HEAD_DIM] += jnp.sum(query_grad, axis=0, keepdims=True)
        sums[:, width + at : width + at + 2 * HEAD_DIM] += jnp.sum(values_grad, axis=0, keepdims=True)


def attend_back(joined, probs, grads):
    pairs, seq, columns = joined.shape
    width = columns // 3
    padded = probs.shape[3] // 2
    return pl.pallas_call(
        attend_back_kernel,
        grid=(pairs,),
        in_specs=[
            pl.BlockSpec((1, seq, columns), lambda i: (i, 0, 0)),
            pl.BlockSpec((1, HEADS // 2, seq, 2 * padded), lambda i: (i, 0, 0, 0)),
            pl.BlockSpec((1, seq, width), lambda i: (i, 0, 0)),
        ],
        out_specs=[
            pl.BlockSpec((1, seq, columns), lambda i: (i, 0, 0)),
            pl.BlockSpec((1, 2 * width), lambda i: (0, 0)),
        ],
        out_shape=[
            inside((pairs, seq, columns)),
            jax.ShapeDtypeStruct((1, 2 * width), F32),
        ],
        compiler_params=params(10),
        cost_estimate=cost(),
        name="attend_back",
    )(in_hbm(joined), in_hbm(probs), in_vmem(grads))


def norm_parts(values):
    centred = values - jnp.mean(values, axis=-1, keepdims=True)
    spread = jnp.mean(centred * centred, axis=-1, keepdims=True)
    scale = lax.rsqrt(spread + 1e-05)
    return centred * scale, scale


def norm_back(upstream, unit, scale, gain):
    scaled = upstream * gain
    return scale * (
        scaled
        - jnp.mean(scaled, axis=-1, keepdims=True)
        - unit * jnp.mean(scaled * unit, axis=-1, keepdims=True)
    )


def add_sums(sums, rows):
    @pl.when(pl.program_id(0) == 0)
    def _():
        sums[...] = jnp.zeros_like(sums)

    for at, values in enumerate(rows):
        sums[at : at + 1, :] += jnp.sum(values, axis=0, keepdims=True)


def first_kernel(pos, context, bias, tokens, gain, shift, *rest, weight):
    pieces, (unit, scale, normed_low), full, sems = weight.split(rest)
    weight.arrive(pieces, full, pos, sems)
    at = step_of(tokens.shape[0])
    total = tokens[...].astype(F32) + (dot(context[at, :], full[...]) + bias[...])
    unit_rows, scale_rows = norm_parts(total)
    unit[at, :] = unit_rows
    scale[at, :] = scale_rows
    normed_low[at, :] = (unit_rows * gain[...] + shift[...]).astype(BF16)


def first_norm(pos, context, weight, bias, token_rows, gain, shift):
    rows, width = token_rows.shape
    tile = rows_of(rows, 416)
    row = whole((1, width))
    return pl.pallas_call(
        functools.partial(first_kernel, weight=weight),
        grid_spec=pltpu.PrefetchScalarGridSpec(
            num_scalar_prefetch=1,
            grid=(rows // tile,),
            in_specs=[HELD, row, pl.BlockSpec((tile, width), lambda i, p: (i, 0)), row, row] + weight.specs(),
            out_specs=[HELD] * 4,
            scratch_shapes=weight.scratch(),
        ),
        out_shape=[inside((rows, width), F32), inside((rows, 1), F32), inside((rows, width)), weight.out()],
        compiler_params=params(14),
        cost_estimate=cost(),
        name="first_norm",
    )(pos, in_vmem(context), bias, token_rows, gain, shift, *weight.arrays)


def expand_kernel(pos, normed_low, bias, *rest, weight, tile):
    pieces, (active, slope), full, sems = weight.split(rest)
    weight.arrive(pieces, full, pos, sems)
    at = columns_of(tile)
    expand = dot(normed_low[...], full[:, at]) + bias[...]
    half = 0.5 * (1.0 + lax.erf(expand * 0.7071067811865476))
    active[:, at] = (expand * half).astype(BF16)
    slope[:, at] = (half + expand * jnp.exp(-0.5 * expand * expand) * 0.3989422804014327).astype(BF16)


def expand_act(pos, normed_low, weight, bias):
    rows, width = normed_low.shape
    columns = weight.shape[1]
    tile = tile_of(columns, 768)
    return pl.pallas_call(
        functools.partial(expand_kernel, weight=weight, tile=tile),
        grid_spec=pltpu.PrefetchScalarGridSpec(
            num_scalar_prefetch=1,
            grid=(columns // tile,),
            in_specs=[HELD, pl.BlockSpec((1, tile), lambda i, p: (0, i))] + weight.specs(),
            out_specs=[HELD] * 3,
            scratch_shapes=weight.scratch(),
        ),
        out_shape=[inside((rows, columns))] * 2 + [weight.out()],
        compiler_params=params(16),
        cost_estimate=cost(),
        name="expand_act",
    )(pos, in_vmem(normed_low), bias, *weight.arrays)


def second_kernel(pos, captions, active, bias, unit, gain, shift, gain2, shift2, cotangent, *rest, weight, seq):
    pieces, (out, low, grad, sums), full, sems = weight.split(rest)
    weight.arrive(pieces, full, pos, sems)
    tile = out.shape[0]
    at = step_of(tile)
    normed = unit[at, :] * gain[...] + shift[...]
    total = normed + (dot(active[at, :], full[...]) + bias[...])
    unit2, scale2 = norm_parts(total)
    out[...] = (unit2 * gain2[...] + shift2[...]).astype(BF16)
    row = lax.broadcasted_iota(jnp.int32, (tile, 1), 0)
    live = jnp.zeros((tile, 1), jnp.bool_)
    for pair in range(tile // seq):
        count = captions[pl.program_id(0) * (tile // seq) + pair] + 2 + REGIONS
        live = live | ((row >= pair * seq) & (row < pair * seq + count))
    upstream = jnp.where(live, cotangent[...].astype(F32), 0.0)
    second = norm_back(upstream, unit2, scale2, gain2[...])
    grad[at, :] = second
    low[at, :] = second.astype(BF16)
    add_sums(sums, (second, upstream * unit2, upstream))


def second_norm(pos, captions, active, weight, bias, unit, gain, shift, gain2, shift2, cotangent, seq):
    rows, width = unit.shape
    hidden = active.shape[1]
    tile = rows_of(rows, 416)
    block = pl.BlockSpec((tile, width), lambda i, p, c: (i, 0))
    row = whole((1, width))
    return pl.pallas_call(
        functools.partial(second_kernel, weight=weight, seq=seq),
        grid_spec=pltpu.PrefetchScalarGridSpec(
            num_scalar_prefetch=2,
            grid=(rows // tile,),
            in_specs=[HELD, row, HELD, row, row, row, row, block] + weight.specs(),
            out_specs=[block, HELD, HELD, whole((8, width)), HELD],
            scratch_shapes=weight.scratch(),
        ),
        out_shape=[
            outside((rows, width)),
            inside((rows, width)),
            inside((rows, width), F32),
            jax.ShapeDtypeStruct((8, width), F32),
            weight.out(),
        ],
        compiler_params=params(18),
        cost_estimate=cost(),
        name="second_norm",
    )(pos, captions, in_vmem(active), bias, in_vmem(unit), gain, shift, gain2, shift2, cotangent, *weight.arrays)


def hidden_back_kernel(low, weight, slope, out, sums):
    at = columns_of(sums.shape[1])
    grad = dot(low[...], weight[at, :], NT) * slope[:, at].astype(F32)
    out[:, at] = grad.astype(BF16)
    sums[...] = jnp.sum(grad, axis=0, keepdims=True)


def hidden_back(low, weight, slope):
    rows, width = low.shape
    hidden = weight.shape[0]
    tile = tile_of(hidden, 768)
    return pl.pallas_call(
        hidden_back_kernel,
        grid=(hidden // tile,),
        in_specs=[HELD] * 3,
        out_specs=[HELD, pl.BlockSpec((1, tile), lambda i: (0, i))],
        out_shape=[inside((rows, hidden)), jax.ShapeDtypeStruct((1, hidden), F32)],
        compiler_params=params(14),
        cost_estimate=cost(),
        name="hidden_back",
    )(in_vmem(low), in_vmem(weight), in_vmem(slope))


def first_back_kernel(hidden, weight, second, unit, scale, gain, out_weight, grad, low, context_grad, sums):
    at = step_of(grad.shape[0])
    unit_rows = unit[at, :]
    normed_grad = dot(hidden[at, :], weight[...], NT) + second[at, :]
    first = norm_back(normed_grad, unit_rows, scale[at, :], gain[...])
    grad[...] = first
    first_low = first.astype(BF16)
    low[at, :] = first_low
    context_grad[at, :] = dot(first_low, out_weight[...], NT).astype(BF16)
    add_sums(sums, (first, normed_grad * unit_rows, normed_grad))


def first_back(hidden, weight, second, unit, scale, gain, out_weight):
    rows, width = second.shape
    columns = hidden.shape[1]
    tile = rows_of(rows, 416)
    return pl.pallas_call(
        first_back_kernel,
        grid=(rows // tile,),
        in_specs=[HELD] * 5 + [whole((1, width)), HELD],
        out_specs=[pl.BlockSpec((tile, width), lambda i: (i, 0)), HELD, HELD, whole((8, width))],
        out_shape=[
            outside((rows, width), F32),
            inside((rows, width)),
            inside((rows, width)),
            jax.ShapeDtypeStruct((8, width), F32),
        ],
        compiler_params=params(18),
        cost_estimate=cost(COVER),
        name="first_back",
    )(in_vmem(hidden), in_vmem(weight), in_vmem(second), in_vmem(unit), in_vmem(scale), gain, in_vmem(out_weight))


def token_back_kernel(grads, weight, first, out):
    out[...] = dot(grads[step_of(out.shape[0]), :], weight[...], NT) + first[...]


def token_back(grads, weight, first):
    rows, width = first.shape
    columns = grads.shape[1]
    tile = rows_of(rows, 416)
    block = pl.BlockSpec((tile, width), lambda i: (i, 0))
    return pl.pallas_call(
        token_back_kernel,
        grid=(rows // tile,),
        in_specs=[HELD, HELD, block],
        out_specs=block,
        out_shape=outside((rows, width), F32),
        compiler_params=params(14),
        cost_estimate=cost(),
        name="token_back",
    )(in_vmem(grads), in_vmem(weight), in_hbm(first))


def weight_grad_kernel(left, right, out):
    out[...] = dot(left[...], right[...], TN).astype(BF16)


def weight_grad(left, right):
    rows, height = left.shape
    columns = right.shape[1]
    tile = tile_of(columns, 768)
    high = tile_of(height, 768)
    return pl.pallas_call(
        weight_grad_kernel,
        grid=(height // high, columns // tile),
        in_specs=[
            pl.BlockSpec((rows, high), lambda i, j: (0, i)),
            pl.BlockSpec((rows, tile), lambda i, j: (0, j)),
        ],
        out_specs=pl.BlockSpec((high, tile), lambda i, j: (i, j)),
        out_shape=outside((height, columns)),
        compiler_params=params(24),
        cost_estimate=cost(),
        name="weight_grad",
    )(left, right)


def store_halves(out, core, grads, pos, rows, extra):
    for chip in range(4):
        ahead = chip ^ pos[0]
        for up in range(2):
            at = ((chip * 2 + core) * 2 + up) * rows
            across = up ^ pos[2]
            block = grads[at : at + rows].astype(BF16)
            out[ahead, across, 0, :, : block.shape[1]] = block
            if extra is not None:
                out[ahead, across, 0, :, block.shape[1] :] = jnp.zeros((rows, 128), BF16)
                out[ahead, across, 0, 0:16, block.shape[1] :] = extra[chip * 2 + core].astype(BF16)


def halves_grad_kernel(pos, left, right, *rest, tile):
    extra, (mine, theirs) = (rest[0] if len(rest) == 3 else None), rest[-2:]
    step = pl.program_id(0) * pl.num_programs(1) + pl.program_id(1)
    grads = dot(left[...], right[:, pl.ds(pl.multiple_of(step * tile, 128), tile)], TN)
    rows = mine.shape[3]

    @pl.when(pos[1] == 0)
    def _():
        store_halves(mine, 0, grads, pos, rows, extra)
        store_halves(theirs, 1, grads, pos, rows, extra)

    @pl.when(pos[1] == 1)
    def _():
        store_halves(mine, 1, grads, pos, rows, extra)
        store_halves(theirs, 0, grads, pos, rows, extra)


def halves_grad(pos, left, right, extra=None, held=True):
    rows, height = left.shape
    half = right.shape[1] // 2
    tile = half if extra is not None else tile_of(half, 768)
    steps = half // tile
    room = 0 if extra is None else 128
    out = inside((4, 2, 2, height // 16, half + room))
    block = pl.BlockSpec((4, 2, 1, height // 16, tile + room), lambda i, j, p: (0, 0, i ^ p[3], 0, j))
    return pl.pallas_call(
        functools.partial(halves_grad_kernel, tile=tile),
        grid_spec=pltpu.PrefetchScalarGridSpec(
            num_scalar_prefetch=1,
            grid=(2, steps),
            in_specs=[HELD if held else whole((rows, height), 1), HELD]
            + ([] if extra is None else [whole(extra.shape)]),
            out_specs=[block, block],
        ),
        out_shape=[out, out],
        compiler_params=params(14),
        cost_estimate=cost(),
        name="halves_grad",
    )(pos, in_vmem(left) if held else left, in_vmem(right), *(() if extra is None else (extra,)))


def store_stacked(out, core, grads, pos, rows):
    wide = grads.shape[1]
    for quarter in range(4):
        for part in range(2):
            at = ((core * 4 + quarter) * 2 + part) * rows
            block = grads[at : at + rows].astype(BF16)
            out[0, (quarter // 2) ^ pos[2], (quarter % 2) ^ pos[3], :, part * wide : (part + 1) * wide] = block


def stacked_grad_kernel(pos, left, right, mine, theirs):
    wide = left.shape[1] // 4
    grads = dot(left[:, columns_of(wide)], right[...], TN)
    rows = mine.shape[3]

    @pl.when(pos[1] == 0)
    def _():
        store_stacked(mine, 0, grads, pos, rows)
        store_stacked(theirs, 1, grads, pos, rows)

    @pl.when(pos[1] == 1)
    def _():
        store_stacked(mine, 1, grads, pos, rows)
        store_stacked(theirs, 0, grads, pos, rows)


def stacked_grad(pos, left, right):
    rows, height = left.shape
    wide = right.shape[1]
    out = inside((4, 2, 2, height // 64, 2 * wide))
    block = pl.BlockSpec((1, 2, 2, height // 64, 2 * wide), lambda i, p: (i ^ p[0], 0, 0, 0, 0))
    return pl.pallas_call(
        stacked_grad_kernel,
        grid_spec=pltpu.PrefetchScalarGridSpec(
            num_scalar_prefetch=1,
            grid=(4,),
            in_specs=[HELD, HELD],
            out_specs=[block, block],
        ),
        out_shape=[out, out],
        compiler_params=params(14),
        cost_estimate=cost(),
        name="stacked_grad",
    )(pos, in_vmem(left), in_vmem(right))


def held_call(kernel, name, outs, values, flops=0):
    return pl.pallas_call(
        kernel,
        in_specs=[HELD] * len(values),
        out_specs=[HELD] * len(outs),
        out_shape=[inside(out) for out in outs],
        compiler_params=params(4),
        cost_estimate=cost(flops),
        name=name,
    )(*map(in_vmem, values))


def add(*terms):
    total = terms[0].astype(F32)
    for term in terms[1:]:
        total += term.astype(F32)
    return total


def core_sum_kernel(*refs, count):
    outs = refs[-4:]
    for flip in range(4):
        at = 0
        for mine, theirs in zip(refs[:count], refs[count : 2 * count]):
            wide = mine.shape[4]
            for chip in range(4):
                pick = (chip, flip // 2, flip % 2)
                outs[flip][chip, :, at : at + wide] = add(mine[pick], theirs[pick]).astype(BF16)
            at += wide
        if len(refs) > 2 * count + 4:
            near, far = refs[2 * count : 2 * count + 2]
            total = add(near[flip], far[flip]).astype(BF16)
            wide = total.shape[1] // 4
            for part in range(4):
                outs[flip][part, :, at:] = total[:, part * wide : (part + 1) * wide]


def core_sum(mine, theirs, more=()):
    rows = mine[0].shape[3]
    wide = sum(m.shape[4] for m in mine) + sum(m.shape[2] // 8 for m in more)
    kernel = functools.partial(core_sum_kernel, count=len(mine))
    return held_call(kernel, "core_sum", [(4, rows, wide)] * 4, [*mine, *theirs, *more])


def near_sum_kernel(mine, theirs, keep, near):
    for chip in range(4):
        for flip in range(4):
            pick = (chip, flip // 2, flip % 2)
            (keep, near)[chip % 2][chip // 2, flip] = add(mine[pick], theirs[pick]).astype(BF16)


def near_sum(mine, theirs):
    shape = (2, 4) + mine.shape[3:]
    return held_call(near_sum_kernel, "near_sum", [shape] * 2, [mine, theirs])


def plane_sum_kernel(own, one, two, three, keep, near, *more):
    wide = keep.shape[2]
    for chip in range(4):
        total = add(own[chip], one[chip], two[chip], three[chip]).astype(BF16)
        (keep, near)[chip % 2][chip // 2] = total[:, :wide]
        if more:
            part = total.shape[1] - wide
            more[0][:, chip * part : (chip + 1) * part] = total[:, wide:]


def plane_sum(parts, more=0, flops=0):
    _, rows, wide = parts[0].shape
    shape = (2, rows, wide - more)
    outs = [shape] * 2 + ([(rows, 4 * more)] if more else [])
    return held_call(plane_sum_kernel, "plane_sum", outs, parts, flops)


def pair_sum_kernel(keep, received, one, two):
    one[...] = add(keep[0], received[0]).astype(BF16)
    two[...] = add(keep[1], received[1]).astype(BF16)


def pair_sum(keep, received, flops=0):
    return held_call(pair_sum_kernel, "pair_sum", [keep.shape[1:]] * 2, [keep, received], flops)


def last_sum_kernel(*refs):
    out, at = refs[-1], refs[-1].shape[1] - refs[-2].shape[1]
    if at:
        out[:, :at] = refs[0][...]
    out[:, at:] = add(refs[-3][...], refs[-2][...]).astype(BF16)


def last_sum(one, two, beside=None):
    values = [one, two] if beside is None else [beside, one, two]
    rows, wide = one.shape[0], one.shape[1] + (0 if beside is None else beside.shape[1])
    return held_call(last_sum_kernel, "last_sum", [(rows, wide)], values)[0]


def place_kernel(pos, *refs, layout):
    parts, outs = refs[:4], refs[4:]
    rows = parts[0].shape[0]
    for flip, part in enumerate(parts):
        up, along = pos[2] ^ (flip // 2), pos[3] ^ (flip % 2)
        at = 0
        for (kind, wide), out in zip(layout, outs):
            if kind == "halves":
                to_row = pl.multiple_of(up * rows, 16)
                to_column = pl.multiple_of(along * wide, 128)
                out[pl.ds(to_row, rows), pl.ds(to_column, wide)] = part[:, at : at + wide].astype(F32)
            elif kind == "stacked":
                for side in range(2):
                    to_row = pl.multiple_of(((up * 2 + along) * 2 + side) * rows, 16)
                    from_column = at + side * (wide // 2)
                    out[pl.ds(to_row, rows), :] = part[:, from_column : from_column + wide // 2].astype(F32)
            else:

                @pl.when((up == 0) & (along == 0))
                def _(out=out, part=part, at=at, wide=wide):
                    out[...] = part[0:16, at : at + wide].astype(F32)

            at += wide


def place(pos, parts, layout):
    rows = parts[0].shape[0]
    shapes = {
        "halves": lambda wide: (2 * rows, 2 * wide),
        "stacked": lambda wide: (8 * rows, wide // 2),
        "small": lambda wide: (16, wide),
    }
    outs = [jax.ShapeDtypeStruct(shapes[kind](wide), F32) for kind, wide in layout]
    return pl.pallas_call(
        functools.partial(place_kernel, layout=layout),
        grid_spec=pltpu.PrefetchScalarGridSpec(
            num_scalar_prefetch=1,
            grid=(1,),
            in_specs=[HELD] * 4,
            out_specs=[whole(out.shape, 1) for out in outs],
        ),
        out_shape=outs,
        compiler_params=params(10),
        cost_estimate=cost(),
        name="place",
    )(pos, *map(in_vmem, parts))


def from_core(values):
    return lax.ppermute(values, "fsdp", [(i, i ^ 1) for i in range(8)])


def from_plane(values):
    parts = values if isinstance(values, (list, tuple)) else [values] * 3
    return [
        lax.ppermute(part, "dp", [(i, i ^ flip) for i in range(4)]) for flip, part in zip((1, 2, 3), parts)
    ]


def from_chips(values):
    return [from_chip(values, flip) for flip in CHIPS]


def from_chip(values, flip):
    return lax.ppermute(values, "fsdp", [(i, i ^ (2 * flip)) for i in range(8)])


def below_kernel(*refs):
    at = 0
    for ref in refs[:-1]:
        rows, wide = ref.shape[0], refs[-1].shape[1]
        refs[-1][at : at + rows] = ref[:, :wide]
        at += rows


def below(*parts, wide=None):
    rows = sum(part.shape[0] for part in parts)
    return pl.pallas_call(
        below_kernel,
        in_specs=[HELD] * len(parts),
        out_specs=HELD,
        out_shape=inside((rows, wide or parts[0].shape[1])),
        compiler_params=params(4),
        cost_estimate=cost(),
        name="below",
    )(*map(in_vmem, parts))


def after(values, *others):
    return lax.optimization_barrier((values, others))[0]


def half_of(pos, shard):
    rows, wide = shard.shape[0] // 2, shard.shape[1] // 2
    return lax.dynamic_slice(shard, (pos[2] * rows, pos[3] * wide), (rows, wide))


def both_cores(pieces):
    return [*pieces, *(from_core(piece) for piece in pieces)]


def gather(values):
    return lax.all_gather(values, "fsdp", axis=0, tiled=True)


def local(
    pieces,
    tokens,
    captions,
    cotangent,
    project_weight,
    project_bias,
    output_weight,
    output_bias,
    first_gain,
    first_shift,
    expand_weight,
    expand_bias,
    shrink_weight,
    shrink_bias,
    second_gain,
    second_shift,
):
    pairs, seq, width = tokens.shape
    rows = pairs * seq
    parts = lax.axis_size("fsdp")
    token_rows = tokens.reshape(rows, width)
    cot_rows = cotangent.reshape(rows, width)

    vectors = (project_bias, output_bias, first_gain, first_shift, expand_bias, shrink_bias, second_gain, second_shift)
    widths = [vector.shape[0] for vector in vectors]
    replica, part = lax.axis_index("dp"), lax.axis_index("fsdp")
    pos = jnp.stack([part // 2, part % 2, replica // 2, replica % 2]).astype(jnp.int32)
    shapes = [(parts * shard.shape[0], shard.shape[1]) for shard in (project_weight, output_weight, expand_weight, shrink_weight)]
    if pieces:
        chips_p = from_chips(half_of(pos, project_weight))
        sibling_p = from_core(project_weight)
        held = jnp.concatenate([vector.reshape(-1, 96) for vector in vectors], axis=0)
        held = jnp.pad(held, ((0, 4), (0, 32)))
        quarter_e = [half_of(pos, expand_weight), half_of(pos, output_weight), jnp.pad(held, ((0, 32), (0, 0)))]
        quarter_e = jnp.concatenate(quarter_e, axis=1)
        wide_e = quarter_e.shape[1] - 128
        chips_p = after(chips_p, sibling_p, quarter_e)
        mine_p = below(*chips_p)
        quarter_e = after(quarter_e, *chips_p)
        far_e = from_chip(quarter_e, 2)
        near_e = [from_chip(quarter_e, 1), from_chip(far_e, 1)]
        plane_p = from_plane(mine_p)
        plane_p = below(*after(plane_p, *near_e))
        other_p = [from_core(mine_p), from_core(plane_p)]

        def halves(shape, shard, sibling, group, at):
            copies = functools.partial(halves_copies, at=at, high=shard.shape[0], wide=shard.shape[1])
            return Weight(shape, [shard, sibling, *group], copies)

        project = halves(shapes[0], project_weight, sibling_p, (mine_p, plane_p, *other_p), 0)
        rows_s = shrink_weight.shape[0] // 8
        quarter_s = lax.dynamic_slice(
            shrink_weight, ((pos[2] * 2 + pos[3]) * 2 * rows_s, 0), (2 * rows_s, shrink_weight.shape[1])
        )
        quarter_s = jnp.concatenate([quarter_s[:rows_s], quarter_s[rows_s:]], axis=1)
        quarter_s = after(quarter_s, plane_p)
        far_s = from_chip(quarter_s, 2)
        mine_e = below(*near_e, far_e, wide=wide_e)
        plane_e = from_plane(mine_e)
        held = jnp.concatenate([held, *(chip[:16, wide_e:] for chip in (*near_e, far_e))], axis=0)
        held = after(held, mine_e)
        bias_full, hidden_bias, rows6 = spread(pos, [held, from_core(held)], width, expand_weight.shape[1])
        out_bias, gain1, shift1, down_bias, gain2, shift2 = (rows6[at : at + 1] for at in range(6))
    else:
        project, output, expand, shrink = (
            Weight(shape, [gather(shard)])
            for shape, shard in zip(shapes, (project_weight, output_weight, expand_weight, shrink_weight))
        )
        packed = gather(jnp.concatenate(vectors)[None, :])
        full, at = [], 0
        for size in widths:
            full.append(packed[:, at : at + size].reshape(1, parts * size).astype(F32))
            at += size
        bias_row, out_bias, gain1, shift1, hidden_bias, down_bias, gain2, shift2 = full
        bias_full = jnp.concatenate([bias_row[:, :width], jnp.zeros((1, width), F32), bias_row[:, width:]], axis=1)

    joined, project = join(pos, token_rows, project, bias_full)
    joined3 = joined.reshape(pairs, seq, 3 * width)
    if pieces:
        far_s = after(far_s, joined)
        joined3 = after(joined3, far_s)
        near_s = [from_chip(quarter_s, 1), from_chip(far_s, 1)]
    context, probs = attend(joined3, captions)
    context_rows = context.reshape(rows, width)
    if pieces:
        near_s = after(near_s, context)
        plane_e = below(*after(plane_e, *near_s))
        group_e = (mine_e, plane_e, from_core(mine_e), from_core(plane_e))
        sibling_e = from_core(after(expand_weight, context))
        sibling_o = from_core(after(output_weight, context))
        expand = halves(shapes[2], expand_weight, sibling_e, group_e, 0)
        output = halves(shapes[1], output_weight, sibling_o, group_e, expand_weight.shape[1] // 2)
        mine_s = below(*near_s, after(far_s, plane_e))
        plane_s = from_plane(mine_s)
        context_rows = after(context_rows, mine_s)
    unit1, scale1, normed_low, output = first_norm(pos, context_rows, output, out_bias, token_rows, gain1, shift1)
    active, slope, expand = expand_act(pos, normed_low, expand, hidden_bias)
    if pieces:
        plane_s = below(*after(plane_s, active))
        other_s = [from_core(mine_s), from_core(plane_s)]
        sibling_s = from_core(after(shrink_weight, active))
        shrink = Weight(
            shapes[3],
            [shrink_weight, sibling_s, mine_s, plane_s, *other_s],
            functools.partial(stacked_copies, high=shrink_weight.shape[0], wide=shrink_weight.shape[1]),
        )
    out_rows, shrink_low, second_grad, sums2, shrink = second_norm(
        pos, captions, active, shrink, down_bias, unit1, gain1, shift1, gain2, shift2, cot_rows, seq
    )
    if pieces:
        mine_s, theirs_s = stacked_grad(pos, active, shrink_low)
        theirs_s = from_core(theirs_s)
        shrink_low = after(shrink_low, mine_s)
    else:
        grad_shrink = weight_grad(active, shrink_low)
    expand_low, sums_hidden = hidden_back(shrink_low, shrink, slope)
    if pieces:
        keep_s, near_s = near_sum(mine_s, after(theirs_s, expand_low))
        expand_low = after(expand_low, near_s)
        near_s = from_chip(near_s, 1)
        mine_e, theirs_e = halves_grad(pos, normed_low, expand_low)
        theirs_e = from_core(theirs_e)
        expand_low = after(expand_low, mine_e)
    first_grad, branch_low, context_grad, sums1 = first_back(
        expand_low, expand, second_grad, unit1, scale1, gain1, output
    )
    if pieces:
        mine_o, theirs_o = halves_grad(pos, context_rows, branch_low)
        theirs_o = from_core(theirs_o)
        own_eo, *out_eo = core_sum([mine_e, mine_o], [theirs_e, theirs_o])
        plane_eo = from_plane(out_eo)
        keep_s, far_s = pair_sum(keep_s, after(near_s, own_eo))
        context_grad = after(context_grad, keep_s)
        far_s = from_chip(far_s, 2)
    else:
        grad_expand = weight_grad(normed_low, expand_low)
        grad_output = weight_grad(context_rows, branch_low)
    joined_grad, sums_joined = attend_back(joined3, probs, context_grad.reshape(pairs, seq, width))
    joined_grad_rows = joined_grad.reshape(rows, 3 * width)
    if pieces:
        extra = bundle(sums_joined, sums1, sums2, sums_hidden)
        mine_p, theirs_p = halves_grad(pos, token_rows, joined_grad_rows, extra, held=False)
        theirs_p = from_core(theirs_p)
        far_s = after(far_s, mine_p)
        keep_eo, near_eo = plane_sum([own_eo, *after(plane_eo, far_s)], flops=COVER)
        own_p, *out_p = core_sum([mine_p], [after(theirs_p, near_eo)], (keep_s, far_s))
        near_eo = from_chip(near_eo, 1)
        plane_p = from_plane(out_p)
        joined_grad_rows = after(joined_grad_rows, own_p)
    else:
        grad_project = weight_grad(token_rows, joined_grad_rows)

        def owned(grad):
            part = lax.psum_scatter(grad, "fsdp", scatter_dimension=0, tiled=True)
            return lax.psum(part, "dp").astype(F32)

        own_project, own_output, own_expand, own_shrink = (
            owned(grad) for grad in (grad_project, grad_output, grad_expand, grad_shrink)
        )
        small = (sums_joined[0], sums1[0], sums1[1], sums1[2], sums_hidden[0], sums2[0], sums2[1], sums2[2])
        packed_grad = jnp.concatenate([v.reshape(parts, -1) for v in small], axis=1)
        shard = lax.psum(lax.psum_scatter(packed_grad.reshape(-1), "fsdp", scatter_dimension=0, tiled=True), "dp")
    token_grad = token_back(joined_grad_rows, project, first_grad)
    if pieces:
        half_p, half_e, half_o = project_weight.shape[1] // 2, expand_weight.shape[1] // 2, width // 2
        keep_eo, far_eo = pair_sum(keep_eo, after(near_eo, token_grad))
        far_eo = from_chip(far_eo, 2)
        keep_p, near_p, total_s = plane_sum([own_p, *after(plane_p, keep_eo)], more=2 * width // 4)
        near_p = from_chip(near_p, 1)
        total_seo = last_sum(keep_eo, after(far_eo, keep_p), total_s)
        quarters_seo = from_plane(total_seo)
        keep_p, far_p = pair_sum(keep_p, after(near_p, total_seo))
        total_p = last_sum(keep_p, from_chip(far_p, 2))
        quarters_p = from_plane(total_p)
        own_shrink, own_expand, own_output = place(
            pos, [total_seo, *after(quarters_seo, total_p)], (("stacked", 2 * width), ("halves", half_e), ("halves", half_o))
        )
        own_project, shard = place(
            pos, [total_p, *after(quarters_p, own_expand)], (("halves", half_p), ("small", 128))
        )
        shard = shard[:12, :96].reshape(-1)

    smalls, at = [], 0
    for size in widths:
        smalls.append(shard[at : at + size])
        at += size
    return (
        out_rows.reshape(pairs, seq, width),
        token_grad.reshape(pairs, seq, width),
        own_project,
        smalls[0],
        own_output,
        smalls[1],
        smalls[2],
        smalls[3],
        own_expand,
        smalls[4],
        own_shrink,
        smalls[5],
        smalls[6],
        smalls[7],
    )


def solution(mesh):
    rows3 = P(("dp", "fsdp"), None, None)
    matrix, vector = P("fsdp", None), P("fsdp")
    pieces = mesh.shape["dp"] == 4 and mesh.shape["fsdp"] == 8
    return jax.shard_map(
        functools.partial(local, pieces),
        mesh=mesh,
        in_specs=(
            rows3, P(("dp", "fsdp")), rows3,
            matrix, vector, matrix, vector, vector, vector,
            matrix, vector, matrix, vector, vector, vector,
        ),
        out_specs=(
            rows3, rows3,
            matrix, vector, matrix, vector, vector, vector,
            matrix, vector, matrix, vector, vector, vector,
        ),
        check_vma=False,
    )
```

```python
import functools

import jax
import jax.numpy as jnp
from jax import lax
from jax.experimental import pallas as pl
from jax.experimental.pallas import tpu as pltpu
from jax.sharding import PartitionSpec as P

HEADS = 12
HEAD_DIM = 64
REGIONS = 36
BF16 = jnp.bfloat16
F32 = jnp.float32

COVER = 100 * 10**9

NN = (((1,), (0,)), ((), ()))
NT = (((1,), (1,)), ((), ()))
TN = (((0,), (0,)), ((), ()))


def dot(left, right, dims=NN):
    return lax.dot_general(left, right, dims, preferred_element_type=F32)


def params(mebibytes):
    return pltpu.CompilerParams(vmem_limit_bytes=mebibytes * 1024 * 1024)


def cost(flops=0):
    return pl.CostEstimate(flops=flops, bytes_accessed=0, transcendentals=0)


def whole(shape, buffers=None):
    mode = None if buffers is None else pl.Buffered(buffers)
    return pl.BlockSpec(shape, lambda *at: (0,) * len(shape), pipeline_mode=mode)


HELD = pl.BlockSpec(memory_space=pltpu.VMEM)


def inside(shape, dtype=BF16):
    return pltpu.VMEM(shape, dtype)


def outside(shape, dtype=BF16):
    return pltpu.HBM(shape, dtype)


def in_vmem(values):
    return pltpu.with_memory_space_constraint(values, pltpu.VMEM)


def in_hbm(values):
    return pltpu.with_memory_space_constraint(values, pltpu.HBM)


def tile_of(size, most):
    return max(t for t in range(128, most + 1, 128) if size % t == 0)


def rows_of(count, most):
    fits = [t for t in range(16, most + 1, 16) if count % t == 0]
    return max(fits) if fits else count


CHIPS = (1, 3, 2)


def halves_copies(refs, into, pos, at, high, wide):
    half = wide // 2
    rows = high // 2
    for side in range(2):
        core = pos[1] if side == 0 else 1 - pos[1]
        shard = pos[0] * 2 + core
        yield refs[side], into.at[pl.ds(pl.multiple_of(shard * high, 16), high), :]
        for flip in range(4):
            buffer, first = refs[2 + side * 2 + (flip > 0)], max(flip - 1, 0) * 3 * rows
            up = pos[2] ^ (flip // 2)
            along = pos[3] ^ (flip % 2)
            for place, chip in enumerate(CHIPS):
                shard = (pos[0] ^ chip) * 2 + core
                to_row = pl.multiple_of(shard * high + up * rows, 16)
                to_column = pl.multiple_of(along * half, 128)
                yield (
                    buffer.at[pl.ds(first + place * rows, rows), pl.ds(at, half)],
                    into.at[pl.ds(to_row, rows), pl.ds(to_column, half)],
                )


def stacked_copies(refs, into, pos, high, wide):
    rows = high // 8
    own = pos[2] * 2 + pos[3]
    for side in range(2):
        core = pos[1] if side == 0 else 1 - pos[1]
        shard = pos[0] * 2 + core
        yield refs[side], into.at[pl.ds(pl.multiple_of(shard * high, 16), high), :]
        for place, chip in enumerate(CHIPS):
            shard = (pos[0] ^ chip) * 2 + core
            for plane in range(2):
                for block in range(2):
                    for part in range(2):
                        flip = block * (2 if part == plane else 1)
                        if plane:
                            flip = (1, 3)[block] if part == 0 else (2, 3)[block]
                        to_row = pl.multiple_of(shard * high + ((own ^ flip) * 2 + part) * rows, 16)
                        yield (
                            refs[2 + side * 2 + plane].at[
                                pl.ds((place * 2 + block) * rows, rows), pl.ds(part * wide, wide)
                            ],
                            into.at[pl.ds(to_row, rows), :],
                        )


def natural_copies(refs, into, pos):
    yield refs[0], into


class Weight:
    def __init__(self, shape, arrays, copies=natural_copies):
        self.shape, self.copies = shape, copies
        self.arrays = [in_vmem(array) for array in arrays]

    def specs(self):
        return [HELD] * len(self.arrays)

    def out(self):
        return inside(self.shape)

    def split(self, refs):
        return refs[: len(self.arrays)], refs[len(self.arrays) : -1], refs[-1]

    def arrive(self, refs, full, pos):
        @pl.when(pl.program_id(0) == 0)
        def _():
            for source, target in self.copies(refs, full, pos):
                target[...] = source[...]


def spread_kernel(pos, own, other, bias, hidden, rows, held):
    part = held.shape[2] * 3 // 4
    for at, chip in enumerate((0, *CHIPS)):
        held[(pos[0] ^ chip) * 2 + pos[1]] = own[at * 16 : at * 16 + 16].astype(F32)
        held[(pos[0] ^ chip) * 2 + 1 - pos[1]] = other[at * 16 : at * 16 + 16].astype(F32)
    bias[...] = jnp.zeros_like(bias)
    width = rows.shape[1]
    for shard in range(8):
        for at in range(2):
            to = (shard * 2 + at) * part
            to += width if to >= width else 0
            bias[0:1, to : to + part] = held[shard, at : at + 1, :part]
        for at in range(4):
            to = (shard * 4 + at) * part
            hidden[0:1, to : to + part] = held[shard, 5 + at : 6 + at, :part]
        to = shard * part
        rows[0:3, to : to + part] = held[shard, 2:5, :part]
        rows[3:6, to : to + part] = held[shard, 9:12, :part]


def spread(pos, shards, width, hidden_width):
    shapes = [(1, 3 * width), (1, hidden_width), (8, width)]
    return pl.pallas_call(
        spread_kernel,
        grid_spec=pltpu.PrefetchScalarGridSpec(
            num_scalar_prefetch=1,
            grid=(1,),
            in_specs=[whole((64, 128))] * 2,
            out_specs=[whole(shape) for shape in shapes],
            scratch_shapes=[pltpu.VMEM((8, 16, 128), F32)],
        ),
        out_shape=[jax.ShapeDtypeStruct(shape, F32) for shape in shapes],
        compiler_params=params(4),
        cost_estimate=cost(COVER),
        name="spread",
    )(pos, *shards)


def bundle_kernel(joined, first, second, hidden, out):
    part = out.shape[2] * 3 // 4
    out[...] = jnp.zeros_like(out)
    for shard in range(8):
        for at in range(2):
            of = (shard * 2 + at) * part
            out[shard, at : at + 1, :part] = joined[0:1, of : of + part]
        for at in range(4):
            of = (shard * 4 + at) * part
            out[shard, 5 + at : 6 + at, :part] = hidden[0:1, of : of + part]
        of = shard * part
        out[shard, 2:5, :part] = first[0:3, of : of + part]
        out[shard, 9:12, :part] = second[0:3, of : of + part]


def bundle(joined, first, second, hidden):
    return pl.pallas_call(
        bundle_kernel,
        out_shape=jax.ShapeDtypeStruct((8, 16, 128), F32),
        compiler_params=params(4),
        cost_estimate=cost(),
        name="bundle",
    )(joined, first, second, hidden)


def step_of(size):
    return pl.ds(pl.multiple_of(pl.program_id(0) * size, 16), size)


def columns_of(size):
    return pl.ds(pl.multiple_of(pl.program_id(0) * size, 128), size)


def join_kernel(pos, tokens, bias, *rest, weight, tile):
    pieces, (out, kept), (full, sem) = rest[: len(weight.arrays)], rest[-4:-2], rest[-2:]
    weight.arrive(pieces, full, pos)
    write = pltpu.make_async_copy(full, kept, sem)

    @pl.when(pl.program_id(0) == 0)
    def _():
        write.start()

    out[...] = (dot(tokens[...], full[:, columns_of(tile)]) + bias[...]).astype(BF16)

    @pl.when(pl.program_id(0) == pl.num_programs(0) - 1)
    def _():
        write.wait()


def join(pos, token_rows, weight, bias):
    rows, width = token_rows.shape
    columns = weight.shape[1]
    tile = tile_of(columns, 768)
    return pl.pallas_call(
        functools.partial(join_kernel, weight=weight, tile=tile),
        grid_spec=pltpu.PrefetchScalarGridSpec(
            num_scalar_prefetch=1,
            grid=(columns // tile,),
            in_specs=[whole((rows, width), 1), pl.BlockSpec((1, tile), lambda i, p: (0, i))] + weight.specs(),
            out_specs=[pl.BlockSpec((rows, tile), lambda i, p: (0, i)), pl.BlockSpec(memory_space=pltpu.HBM)],
            scratch_shapes=[pltpu.VMEM(weight.shape, BF16), pltpu.SemaphoreType.DMA(())],
        ),
        out_shape=[outside((rows, columns)), outside(weight.shape)],
        compiler_params=params(15),
        cost_estimate=cost(),
        name="join",
    )(pos, token_rows, bias, *weight.arrays)


def head_stack(block, low_half, padded):
    rows = block.shape[0]
    filler = jnp.zeros((padded - rows, block.shape[1]), F32)
    first = jnp.where(low_half, block, 0.0)
    second = jnp.where(low_half, 0.0, block)
    return jnp.concatenate([first, filler, second, filler], axis=0).astype(BF16)


def attend_kernel(captions, joined, context, probs):
    seq = joined.shape[1]
    width = context.shape[2]
    padded = probs.shape[3] // 2
    valid = captions[pl.program_id(0)] + 2 + REGIONS
    keep = lax.broadcasted_iota(jnp.int32, (seq, 2 * padded), 0) < valid
    low_half = lax.broadcasted_iota(jnp.int32, (1, 2 * HEAD_DIM), 1) < HEAD_DIM
    places = [pair * 2 * HEAD_DIM for pair in range(HEADS // 2)]
    scores = []
    for at in places:
        query = joined[0, :, at : at + 2 * HEAD_DIM].astype(F32)
        keys = joined[0, :, width + at : width + at + 2 * HEAD_DIM]
        scores.append(dot(keys, head_stack(query, low_half, padded), NT) * HEAD_DIM ** (-0.5))
    probabilities = []
    for score in scores:
        score = jnp.where(keep, score, -1000000000.0)
        grown = jnp.exp(score - jnp.max(score, axis=0, keepdims=True))
        total = jnp.sum(grown, axis=0, keepdims=True)
        probabilities.append((grown * (1.0 / total)).astype(BF16))
    for pair, at in enumerate(places):
        values = joined[0, :, 2 * width + at : 2 * width + at + 2 * HEAD_DIM]
        mixed = dot(probabilities[pair], values, TN)
        probs[0, pair] = probabilities[pair]
        context[0, :, at : at + 2 * HEAD_DIM] = jnp.where(
            low_half, mixed[:seq], mixed[padded : padded + seq]
        ).astype(BF16)


def attend(joined, captions):
    pairs, seq, columns = joined.shape
    width = columns // 3
    padded = (seq + 127) // 128 * 128
    return pl.pallas_call(
        attend_kernel,
        grid_spec=pltpu.PrefetchScalarGridSpec(
            num_scalar_prefetch=1,
            grid=(pairs,),
            in_specs=[pl.BlockSpec((1, seq, columns), lambda i, c: (i, 0, 0))],
            out_specs=[
                pl.BlockSpec((1, seq, width), lambda i, c: (i, 0, 0)),
                pl.BlockSpec((1, HEADS // 2, seq, 2 * padded), lambda i, c: (i, 0, 0, 0)),
            ],
        ),
        out_shape=[
            inside((pairs, seq, width)),
            outside((pairs, HEADS // 2, seq, 2 * padded)),
        ],
        compiler_params=params(8),
        cost_estimate=cost(),
        name="attend",
    )(captions, in_hbm(joined))


def attend_back_kernel(joined, probs, grads, out, sums):
    seq = joined.shape[1]
    width = grads.shape[2]
    padded = probs.shape[3] // 2
    low_half = lax.broadcasted_iota(jnp.int32, (1, 2 * HEAD_DIM), 1) < HEAD_DIM

    @pl.when(pl.program_id(0) == 0)
    def _():
        sums[...] = jnp.zeros_like(sums)

    places = [pair * 2 * HEAD_DIM for pair in range(HEADS // 2)]
    prob_grads, grad_stacks = [], []
    for at in places:
        values = joined[0, :, 2 * width + at : 2 * width + at + 2 * HEAD_DIM]
        grad_stacks.append(head_stack(grads[0, :, at : at + 2 * HEAD_DIM].astype(F32), low_half, padded))
        prob_grads.append(dot(values, grad_stacks[-1], NT))
    score_grads = []
    for pair, prob_grad in enumerate(prob_grads):
        prob = probs[0, pair].astype(F32)
        row_dot = jnp.sum(prob * prob_grad, axis=0, keepdims=True)
        score_grads.append((prob * (prob_grad - row_dot) * HEAD_DIM ** (-0.5)).astype(BF16))
    results = []
    for pair, at in enumerate(places):
        query = joined[0, :, at : at + 2 * HEAD_DIM].astype(F32)
        keys = joined[0, :, width + at : width + at + 2 * HEAD_DIM]
        mixed = dot(score_grads[pair], keys, TN)
        query_grad = jnp.where(low_half, mixed[:seq], mixed[padded : padded + seq])
        keys_grad = dot(score_grads[pair], head_stack(query, low_half, padded))
        results.append((query_grad, keys_grad, dot(probs[0, pair], grad_stacks[pair])))
    for at, blocks in zip(places, results):
        for part, block in enumerate(blocks):
            out[0, :, part * width + at : part * width + at + 2 * HEAD_DIM] = block.astype(BF16)
            if part != 1:
                to = part // 2 * width + at
                sums[:, to : to + 2 * HEAD_DIM] += jnp.sum(block, axis=0, keepdims=True)


def attend_back(joined, probs, grads):
    pairs, seq, columns = joined.shape
    width = columns // 3
    padded = probs.shape[3] // 2
    return pl.pallas_call(
        attend_back_kernel,
        grid=(pairs,),
        in_specs=[
            pl.BlockSpec((1, seq, columns), lambda i: (i, 0, 0)),
            pl.BlockSpec((1, HEADS // 2, seq, 2 * padded), lambda i: (i, 0, 0, 0)),
            pl.BlockSpec((1, seq, width), lambda i: (i, 0, 0)),
        ],
        out_specs=[
            pl.BlockSpec((1, seq, columns), lambda i: (i, 0, 0)),
            pl.BlockSpec((1, 2 * width), lambda i: (0, 0)),
        ],
        out_shape=[
            inside((pairs, seq, columns)),
            jax.ShapeDtypeStruct((1, 2 * width), F32),
        ],
        compiler_params=params(10),
        cost_estimate=cost(),
        name="attend_back",
    )(in_hbm(joined), in_hbm(probs), in_vmem(grads))


def norm_parts(values):
    centred = values - jnp.mean(values, axis=-1, keepdims=True)
    spread = jnp.mean(centred * centred, axis=-1, keepdims=True)
    scale = lax.rsqrt(spread + 1e-05)
    return centred * scale, scale


def norm_back(upstream, unit, scale, gain):
    scaled = upstream * gain
    return scale * (
        scaled
        - jnp.mean(scaled, axis=-1, keepdims=True)
        - unit * jnp.mean(scaled * unit, axis=-1, keepdims=True)
    )


def add_sums(sums, rows):
    for at, values in enumerate(rows):
        sums[at : at + 1, :] += jnp.sum(values, axis=0, keepdims=True)


def chunked(count, load, use):
    ready = load(0)
    for at in range(count):
        following = load(at + 1) if at + 1 < count else None
        use(at, ready)
        ready = following


def chunk_slices(rows, most):
    tile = rows_of(rows, most)
    return [slice(at, at + tile) for at in range(0, rows, tile)]


def first_kernel(pos, context, bias, tokens, gain, shift, *rest, weight):
    pieces, (unit, scale, normed_low), full = weight.split(rest)
    weight.arrive(pieces, full, pos)
    chunks = chunk_slices(tokens.shape[0], 416)

    def normalise(at, branch):
        rows = chunks[at]
        unit_rows, scale_rows = norm_parts(tokens[rows, :].astype(F32) + (branch + bias[...]))
        unit[rows, :] = unit_rows
        scale[rows, :] = scale_rows
        normed_low[rows, :] = (unit_rows * gain[...] + shift[...]).astype(BF16)

    chunked(len(chunks), lambda at: dot(context[chunks[at], :], full[...]), normalise)


def first_norm(pos, context, weight, bias, token_rows, gain, shift):
    rows, width = token_rows.shape
    row = whole((1, width))
    return pl.pallas_call(
        functools.partial(first_kernel, weight=weight),
        grid_spec=pltpu.PrefetchScalarGridSpec(
            num_scalar_prefetch=1,
            grid=(1,),
            in_specs=[HELD, row, HELD, row, row] + weight.specs(),
            out_specs=[HELD] * 4,
        ),
        out_shape=[inside((rows, width), F32), inside((rows, 1), F32), inside((rows, width)), weight.out()],
        compiler_params=params(10),
        cost_estimate=cost(),
        name="first_norm",
    )(pos, in_vmem(context), bias, in_vmem(token_rows), gain, shift, *weight.arrays)


def expand_kernel(pos, normed_low, bias, *rest, weight, tile):
    pieces, (active, slope), full = weight.split(rest)
    weight.arrive(pieces, full, pos)
    at = columns_of(tile)
    expand = dot(normed_low[...], full[:, at]) + bias[...]
    half = 0.5 * (1.0 + lax.erf(expand * 0.7071067811865476))
    active[:, at] = (expand * half).astype(BF16)
    slope[:, at] = (half + expand * jnp.exp(-0.5 * expand * expand) * 0.3989422804014327).astype(BF16)


def expand_act(pos, normed_low, weight, bias):
    rows, width = normed_low.shape
    columns = weight.shape[1]
    tile = tile_of(columns, 768)
    return pl.pallas_call(
        functools.partial(expand_kernel, weight=weight, tile=tile),
        grid_spec=pltpu.PrefetchScalarGridSpec(
            num_scalar_prefetch=1,
            grid=(columns // tile,),
            in_specs=[HELD, pl.BlockSpec((1, tile), lambda i, p: (0, i))] + weight.specs(),
            out_specs=[HELD] * 3,
        ),
        out_shape=[inside((rows, columns))] * 2 + [weight.out()],
        compiler_params=params(12),
        cost_estimate=cost(),
        name="expand_act",
    )(pos, in_vmem(normed_low), bias, *weight.arrays)


def second_kernel(pos, captions, active, bias, unit, gain, shift, gain2, shift2, cotangent, *rest, weight, seq):
    pieces, (out, low, grad, sums), full, (held, sems) = *weight.split(rest[:-2]), rest[-2:]
    weight.arrive(pieces, full, pos)
    sums[...] = jnp.zeros_like(sums)
    chunks = chunk_slices(held.shape[0], 208)
    writes = [
        pltpu.make_async_copy(held.at[rows, :], out.at[rows, :], sems.at[at]) for at, rows in enumerate(chunks)
    ]

    def normalise(at, shrunk):
        rows = chunks[at]
        normed = unit[rows, :] * gain[...] + shift[...]
        unit2, scale2 = norm_parts(normed + (shrunk + bias[...]))
        held[rows, :] = (unit2 * gain2[...] + shift2[...]).astype(BF16)
        writes[at].start()
        row = lax.broadcasted_iota(jnp.int32, (rows.stop - rows.start, 1), 0) + rows.start
        live = jnp.zeros(row.shape, jnp.bool_)
        for pair in range(rows.start // seq, (rows.stop - 1) // seq + 1):
            live = live | ((row >= pair * seq) & (row < pair * seq + captions[pair] + 2 + REGIONS))
        upstream = jnp.where(live, cotangent[rows, :].astype(F32), 0.0)
        second = norm_back(upstream, unit2, scale2, gain2[...])
        grad[rows, :] = second
        low[rows, :] = second.astype(BF16)
        add_sums(sums, (second, upstream * unit2, upstream))

    chunked(len(chunks), lambda at: dot(active[chunks[at], :], full[...]), normalise)
    for write in writes:
        write.wait()


def second_norm(pos, captions, active, weight, bias, unit, gain, shift, gain2, shift2, cotangent, seq):
    rows, width = unit.shape
    row = whole((1, width))
    return pl.pallas_call(
        functools.partial(second_kernel, weight=weight, seq=seq),
        grid_spec=pltpu.PrefetchScalarGridSpec(
            num_scalar_prefetch=2,
            grid=(1,),
            in_specs=[HELD, row, HELD, row, row, row, row, HELD] + weight.specs(),
            out_specs=[pl.BlockSpec(memory_space=pltpu.HBM), HELD, HELD, whole((8, width)), HELD],
            scratch_shapes=[pltpu.VMEM((rows, width), BF16), pltpu.SemaphoreType.DMA((rows // 16,))],
        ),
        out_shape=[
            outside((rows, width)),
            inside((rows, width)),
            inside((rows, width), F32),
            jax.ShapeDtypeStruct((8, width), F32),
            weight.out(),
        ],
        compiler_params=params(12),
        cost_estimate=cost(),
        name="second_norm",
    )(pos, captions, in_vmem(active), bias, in_vmem(unit), gain, shift, gain2, shift2, in_vmem(cotangent), *weight.arrays)


def hidden_back_kernel(low, weight, slope, out, sums):
    at = columns_of(sums.shape[1])
    grad = dot(low[...], weight[at, :], NT) * slope[:, at].astype(F32)
    out[:, at] = grad.astype(BF16)
    sums[...] = jnp.sum(grad, axis=0, keepdims=True)


def hidden_back(low, weight, slope):
    rows, width = low.shape
    hidden = weight.shape[0]
    tile = tile_of(hidden, 768)
    return pl.pallas_call(
        hidden_back_kernel,
        grid=(hidden // tile,),
        in_specs=[HELD] * 3,
        out_specs=[HELD, pl.BlockSpec((1, tile), lambda i: (0, i))],
        out_shape=[inside((rows, hidden)), jax.ShapeDtypeStruct((1, hidden), F32)],
        compiler_params=params(10),
        cost_estimate=cost(),
        name="hidden_back",
    )(in_vmem(low), in_vmem(weight), in_vmem(slope))


def first_back_kernel(hidden, weight, second, unit, scale, gain, out_weight, grad, low, context_grad, sums):
    sums[...] = jnp.zeros_like(sums)
    chunks = chunk_slices(grad.shape[0], 416)
    waiting = []

    def pass_on():
        rows, first_low = waiting.pop()
        context_grad[rows, :] = dot(first_low, out_weight[...], NT).astype(BF16)

    def normalise(at, product):
        rows = chunks[at]
        unit_rows = unit[rows, :]
        normed_grad = product + second[rows, :]
        first = norm_back(normed_grad, unit_rows, scale[rows, :], gain[...])
        grad[rows, :] = first
        first_low = first.astype(BF16)
        low[rows, :] = first_low
        add_sums(sums, (first, normed_grad * unit_rows, normed_grad))
        if waiting:
            pass_on()
        waiting.append((rows, first_low))

    chunked(len(chunks), lambda at: dot(hidden[chunks[at], :], weight[...], NT), normalise)
    pass_on()


def first_back(hidden, weight, second, unit, scale, gain, out_weight):
    rows, width = second.shape
    return pl.pallas_call(
        first_back_kernel,
        grid=(1,),
        in_specs=[HELD] * 5 + [whole((1, width)), HELD],
        out_specs=[HELD, HELD, HELD, whole((8, width))],
        out_shape=[
            inside((rows, width), F32),
            inside((rows, width)),
            inside((rows, width)),
            jax.ShapeDtypeStruct((8, width), F32),
        ],
        compiler_params=params(13),
        cost_estimate=cost(COVER),
        name="first_back",
    )(in_vmem(hidden), in_vmem(weight), in_vmem(second), in_vmem(unit), in_vmem(scale), gain, in_vmem(out_weight))


def token_back_kernel(grads, weight, first, out):
    at = step_of(out.shape[0])
    out[...] = dot(grads[at, :], weight[...], NT) + first[at, :]


def token_back(grads, weight, first):
    rows, width = first.shape
    tile = rows_of(rows, 416)
    return pl.pallas_call(
        token_back_kernel,
        grid=(rows // tile,),
        in_specs=[HELD] * 3,
        out_specs=pl.BlockSpec((tile, width), lambda i: (i, 0)),
        out_shape=outside((rows, width), F32),
        compiler_params=params(9),
        cost_estimate=cost(),
        name="token_back",
    )(in_vmem(grads), in_vmem(weight), in_vmem(first))


def weight_grad_kernel(left, right, out):
    out[...] = dot(left[...], right[...], TN).astype(BF16)


def weight_grad(left, right):
    rows, height = left.shape
    columns = right.shape[1]
    tile = tile_of(columns, 768)
    high = tile_of(height, 768)
    return pl.pallas_call(
        weight_grad_kernel,
        grid=(height // high, columns // tile),
        in_specs=[
            pl.BlockSpec((rows, high), lambda i, j: (0, i)),
            pl.BlockSpec((rows, tile), lambda i, j: (0, j)),
        ],
        out_specs=pl.BlockSpec((high, tile), lambda i, j: (i, j)),
        out_shape=outside((height, columns)),
        compiler_params=params(24),
        cost_estimate=cost(),
        name="weight_grad",
    )(left, right)


def store_halves(out, core, grads, pos, along, extra):
    rows, wide = out.shape[3], grads.shape[1]
    for chip in range(4):
        for up in range(2):
            at = ((chip * 2 + core) * 2 + up) * rows
            to = (chip ^ pos[0], up ^ pos[2], along ^ pos[3])
            out[(*to, slice(None), slice(0, wide))] = grads[at : at + rows].astype(BF16)
            if extra is not None:
                out[(*to, slice(None), slice(wide, None))] = jnp.zeros((rows, 128), BF16)
                out[(*to, slice(0, 16), slice(wide, None))] = extra[chip * 2 + core].astype(BF16)


def store_stacked(out, core, grads, pos, chip):
    rows, wide = out.shape[3], grads.shape[1]
    for quarter in range(4):
        for part in range(2):
            at = ((core * 4 + quarter) * 2 + part) * rows
            to = (chip, (quarter // 2) ^ pos[2], (quarter % 2) ^ pos[3])
            out[(*to, slice(None), slice(part * wide, (part + 1) * wide))] = grads[at : at + rows].astype(BF16)


def by_core(pos, mine, theirs, store):
    for core in range(2):

        @pl.when(pos[1] == core)
        def _(core=core):
            store(mine, core)
            store(theirs, 1 - core)


def halves_grad_kernel(pos, left, right, *rest):
    extra, (mine, theirs) = (rest[0] if len(rest) == 3 else None), rest[-2:]
    along, half = pl.program_id(0), right.shape[1] // 2
    grads = dot(left[...], right[:, columns_of(half)], TN)
    by_core(pos, mine, theirs, lambda out, core: store_halves(out, core, grads, pos, along, extra))


def stacked_grad_kernel(pos, left, right, mine, theirs, *, odd):
    high = left.shape[1] // 4
    for part in range(2):
        chip = pos[0] ^ (2 * part + odd)
        columns = pl.ds(pl.multiple_of(chip * high, 128), high)
        grads = dot(left[:, columns], right[...], TN)
        by_core(pos, mine, theirs, lambda out, core: store_stacked(out, core, grads, pos, part))


def pieces_grad(kernel, name, pos, left, right, shape, extra=(), chips=4):
    out = inside((chips, 2, 2) + shape)
    return pl.pallas_call(
        kernel,
        grid_spec=pltpu.PrefetchScalarGridSpec(
            num_scalar_prefetch=1,
            grid=(chips // 2,),
            in_specs=[HELD, HELD] + [whole(array.shape) for array in extra],
            out_specs=[HELD, HELD],
        ),
        out_shape=[out, out],
        compiler_params=params(13),
        cost_estimate=cost(),
        name=name,
    )(pos, in_vmem(left), in_vmem(right), *extra)


def halves_grad(pos, left, right, extra=None):
    shape = (left.shape[1] // 16, right.shape[1] // 2 + (0 if extra is None else 128))
    more = () if extra is None else (extra,)
    return pieces_grad(halves_grad_kernel, "halves_grad", pos, left, right, shape, more)


def stacked_grad(pos, left, right, odd):
    shape = (left.shape[1] // 64, 2 * right.shape[1])
    kernel = functools.partial(stacked_grad_kernel, odd=odd)
    return pieces_grad(kernel, "stacked_grad", pos, left, right, shape, chips=2)


def held_call(kernel, name, outs, values, flops=0):
    return pl.pallas_call(
        kernel,
        in_specs=[HELD] * len(values),
        out_specs=[HELD] * len(outs),
        out_shape=[inside(out) for out in outs],
        compiler_params=params(4),
        cost_estimate=cost(flops),
        name=name,
    )(*map(in_vmem, values))


def add(*terms):
    total = terms[0].astype(F32)
    for term in terms[1:]:
        total += term.astype(F32)
    return total


def core_sum_kernel(*refs, count):
    outs = refs[-4:]
    for flip in range(4):
        at = 0
        for mine, theirs in zip(refs[:count], refs[count : 2 * count]):
            wide = mine.shape[4]
            for chip in range(4):
                pick = (chip, flip // 2, flip % 2)
                outs[flip][chip, :, at : at + wide] = add(mine[pick], theirs[pick]).astype(BF16)
            at += wide
        if len(refs) > 2 * count + 4:
            near, far = refs[2 * count : 2 * count + 2]
            total = add(near[flip], far[flip]).astype(BF16)
            wide = total.shape[1] // 4
            for part in range(4):
                outs[flip][part, :, at:] = total[:, part * wide : (part + 1) * wide]


def core_sum(mine, theirs, more=()):
    rows = mine[0].shape[3]
    wide = sum(m.shape[4] for m in mine) + sum(m.shape[2] // 8 for m in more)
    kernel = functools.partial(core_sum_kernel, count=len(mine))
    return held_call(kernel, "core_sum", [(4, rows, wide)] * 4, [*mine, *theirs, *more])


def both_sum_kernel(mine, theirs, out):
    for chip in range(2):
        for flip in range(4):
            pick = (chip, flip // 2, flip % 2)
            out[chip, flip] = add(mine[pick], theirs[pick]).astype(BF16)


def both_sum(mine, theirs, flops=0):
    return held_call(both_sum_kernel, "both_sum", [(2, 4) + mine.shape[3:]], [mine, theirs], flops)[0]


def plane_sum_kernel(own, one, two, three, keep, near, *more):
    wide = keep.shape[2]
    for chip in range(4):
        total = add(own[chip], one[chip], two[chip], three[chip]).astype(BF16)
        (keep, near)[chip % 2][chip // 2] = total[:, :wide]
        if more:
            part = total.shape[1] - wide
            more[0][:, chip * part : (chip + 1) * part] = total[:, wide:]


def plane_sum(parts, more=0, flops=0):
    _, rows, wide = parts[0].shape
    shape = (2, rows, wide - more)
    outs = [shape] * 2 + ([(rows, 4 * more)] if more else [])
    return held_call(plane_sum_kernel, "plane_sum", outs, parts, flops)


def pair_sum_kernel(keep, received, one, two):
    one[...] = add(keep[0], received[0]).astype(BF16)
    two[...] = add(keep[1], received[1]).astype(BF16)


def pair_sum(keep, received, flops=0):
    return held_call(pair_sum_kernel, "pair_sum", [keep.shape[1:]] * 2, [keep, received], flops)


def last_sum_kernel(*refs):
    out, at = refs[-1], refs[-1].shape[1] - refs[-2].shape[1]
    if at:
        out[:, :at] = refs[0][...]
    out[:, at:] = add(refs[-3][...], refs[-2][...]).astype(BF16)


def last_sum(one, two, beside=None):
    values = [one, two] if beside is None else [beside, one, two]
    rows, wide = one.shape[0], one.shape[1] + (0 if beside is None else beside.shape[1])
    return held_call(last_sum_kernel, "last_sum", [(rows, wide)], values)[0]


def place_kernel(pos, *refs, layout):
    parts, outs = refs[:4], refs[4:]
    rows = parts[0].shape[0]
    for flip, part in enumerate(parts):
        up, along = pos[2] ^ (flip // 2), pos[3] ^ (flip % 2)
        at = 0
        for (kind, wide), out in zip(layout, outs):
            if kind == "halves":
                to_row = pl.multiple_of(up * rows, 16)
                to_column = pl.multiple_of(along * wide, 128)
                out[pl.ds(to_row, rows), pl.ds(to_column, wide)] = part[:, at : at + wide].astype(F32)
            elif kind == "stacked":
                for side in range(2):
                    to_row = pl.multiple_of(((up * 2 + along) * 2 + side) * rows, 16)
                    from_column = at + side * (wide // 2)
                    out[pl.ds(to_row, rows), :] = part[:, from_column : from_column + wide // 2].astype(F32)
            else:

                @pl.when((up == 0) & (along == 0))
                def _(out=out, part=part, at=at, wide=wide):
                    out[...] = part[0:16, at : at + wide].astype(F32)

            at += wide


def place(pos, parts, layout):
    rows = parts[0].shape[0]
    shapes = {
        "halves": lambda wide: (2 * rows, 2 * wide),
        "stacked": lambda wide: (8 * rows, wide // 2),
        "small": lambda wide: (16, wide),
    }
    outs = [jax.ShapeDtypeStruct(shapes[kind](wide), F32) for kind, wide in layout]
    return pl.pallas_call(
        functools.partial(place_kernel, layout=layout),
        grid_spec=pltpu.PrefetchScalarGridSpec(
            num_scalar_prefetch=1,
            grid=(1,),
            in_specs=[HELD] * 4,
            out_specs=[whole(out.shape, 1) for out in outs],
        ),
        out_shape=outs,
        compiler_params=params(10),
        cost_estimate=cost(),
        name="place",
    )(pos, *map(in_vmem, parts))


def from_core(values):
    return lax.ppermute(values, "fsdp", [(i, i ^ 1) for i in range(8)])


def from_plane(values):
    parts = values if isinstance(values, (list, tuple)) else [values] * 3
    return [
        lax.ppermute(part, "dp", [(i, i ^ flip) for i in range(4)]) for flip, part in zip((1, 2, 3), parts)
    ]


def from_chips(values):
    return [from_chip(values, flip) for flip in CHIPS]


def from_chip(values, flip):
    return lax.ppermute(values, "fsdp", [(i, i ^ (2 * flip)) for i in range(8)])


def below_kernel(*refs):
    at = 0
    for ref in refs[:-1]:
        rows, wide = ref.shape[0], refs[-1].shape[1]
        refs[-1][at : at + rows] = ref[:, :wide]
        at += rows


def below(*parts, wide=None, flops=0):
    rows = sum(part.shape[0] for part in parts)
    return pl.pallas_call(
        below_kernel,
        in_specs=[HELD] * len(parts),
        out_specs=HELD,
        out_shape=inside((rows, wide or parts[0].shape[1])),
        compiler_params=params(4),
        cost_estimate=cost(flops),
        name="below",
    )(*map(in_vmem, parts))


def pick_kernel(pos, shard, out):
    rows, wide = out.shape[0] // 2, shard.shape[1]
    own = pos[2] * 2 + pos[3]
    for block, part, flip in ((0, 0, 0), (0, 1, 0), (1, 0, 2), (1, 1, 1)):
        from_row = pl.multiple_of(((own ^ flip) * 2 + part) * rows, 16)
        out[block * rows : (block + 1) * rows, part * wide : (part + 1) * wide] = shard[pl.ds(from_row, rows), :]


def pick(pos, shard):
    return pl.pallas_call(
        pick_kernel,
        grid_spec=pltpu.PrefetchScalarGridSpec(
            num_scalar_prefetch=1, grid=(1,), in_specs=[whole(shard.shape, 1)], out_specs=HELD
        ),
        out_shape=inside((shard.shape[0] // 4, 2 * shard.shape[1])),
        compiler_params=params(4),
        cost_estimate=cost(),
        name="pick",
    )(pos, shard)


def left_right_kernel(whole_ref, left, right):
    half = left.shape[1]
    left[...] = whole_ref[:, :half]
    right[...] = whole_ref[:, half:]


def left_right(values):
    rows, wide = values.shape
    return held_call(left_right_kernel, "left_right", [(rows, wide // 2)] * 2, [values])


def beside_kernel(left, right, out):
    half = left.shape[1]
    out[:, :half] = left[...]
    out[:, half:] = right[...]


def beside(left, right):
    rows, wide = left.shape
    return held_call(beside_kernel, "beside", [(rows, 2 * wide)], [left, right])[0]


def after(values, *others):
    return lax.optimization_barrier((values, others))[0]


def half_of(pos, shard):
    rows, wide = shard.shape[0] // 2, shard.shape[1] // 2
    return lax.dynamic_slice(shard, (pos[2] * rows, pos[3] * wide), (rows, wide))


def both_cores(pieces):
    return [*pieces, *(from_core(piece) for piece in pieces)]


def gather(values):
    return lax.all_gather(values, "fsdp", axis=0, tiled=True)


def local(
    pieces,
    tokens,
    captions,
    cotangent,
    project_weight,
    project_bias,
    output_weight,
    output_bias,
    first_gain,
    first_shift,
    expand_weight,
    expand_bias,
    shrink_weight,
    shrink_bias,
    second_gain,
    second_shift,
):
    pairs, seq, width = tokens.shape
    rows = pairs * seq
    parts = lax.axis_size("fsdp")
    token_rows = tokens.reshape(rows, width)
    cot_rows = cotangent.reshape(rows, width)

    vectors = (project_bias, output_bias, first_gain, first_shift, expand_bias, shrink_bias, second_gain, second_shift)
    widths = [vector.shape[0] for vector in vectors]
    replica, part = lax.axis_index("dp"), lax.axis_index("fsdp")
    pos = jnp.stack([part // 2, part % 2, replica // 2, replica % 2]).astype(jnp.int32)
    shapes = [(parts * shard.shape[0], shard.shape[1]) for shard in (project_weight, output_weight, expand_weight, shrink_weight)]
    if pieces:
        chips_p = from_chips(half_of(pos, project_weight))
        sibling_p = from_core(project_weight)
        held = jnp.concatenate([vector.reshape(-1, 96) for vector in vectors], axis=0)
        held = jnp.pad(held, ((0, 4), (0, 32)))
        quarter_e = [half_of(pos, expand_weight), half_of(pos, output_weight), jnp.pad(held, ((0, 32), (0, 0)))]
        quarter_e = jnp.concatenate(quarter_e, axis=1)
        wide_e = quarter_e.shape[1] - 128
        chips_p = after(chips_p, sibling_p, quarter_e)
        mine_p = below(*chips_p)
        quarter_e = after(quarter_e, *chips_p)
        far_e = from_chip(quarter_e, 2)
        near_e = [from_chip(quarter_e, 1), from_chip(far_e, 1)]
        plane_p = from_plane(mine_p)
        plane_p = below(*plane_p, flops=COVER)
        near_e = after(near_e, plane_p)
        other_p = [from_core(mine_p), from_core(plane_p)]

        def halves(shape, shard, sibling, group, at):
            copies = functools.partial(halves_copies, at=at, high=shard.shape[0], wide=shard.shape[1])
            return Weight(shape, [shard, sibling, *group], copies)

        project = halves(shapes[0], project_weight, sibling_p, (mine_p, plane_p, *other_p), 0)
        quarter_s = pick(pos, after(shrink_weight, quarter_e))
        quarter_s = after(quarter_s, plane_p)
        far_s = from_chip(quarter_s, 2)
        mine_e = below(*near_e, far_e, wide=wide_e)
        plane_e = from_plane(mine_e)
        held = jnp.concatenate([held, *(chip[:16, wide_e:] for chip in (*near_e, far_e))], axis=0)
        held = after(held, mine_e)
        bias_full, hidden_bias, rows6 = spread(pos, [held, from_core(held)], width, expand_weight.shape[1])
        out_bias, gain1, shift1, down_bias, gain2, shift2 = (rows6[at : at + 1] for at in range(6))
    else:
        project, output, expand, shrink = (
            Weight(shape, [gather(shard)])
            for shape, shard in zip(shapes, (project_weight, output_weight, expand_weight, shrink_weight))
        )
        packed = gather(jnp.concatenate(vectors)[None, :])
        full, at = [], 0
        for size in widths:
            full.append(packed[:, at : at + size].reshape(1, parts * size).astype(F32))
            at += size
        bias_row, out_bias, gain1, shift1, hidden_bias, down_bias, gain2, shift2 = full
        bias_full = jnp.concatenate([bias_row[:, :width], jnp.zeros((1, width), F32), bias_row[:, width:]], axis=1)

    joined, project = join(pos, token_rows, project, bias_full)
    joined3 = joined.reshape(pairs, seq, 3 * width)
    if pieces:
        near_s = from_chip(after(quarter_s, joined), 1)
    context, probs = attend(joined3, captions)
    context_rows = context.reshape(rows, width)
    if pieces:
        far_s = after(far_s, context)
        near_s = [near_s, from_chip(far_s, 1)]
        plane_e = below(*after(plane_e, far_s))
        mine_s = below(*after(near_s, plane_e), far_s, flops=COVER)
        left_s, right_s = left_right(mine_s)
        plane_s = [
            lax.ppermute(left_s, "dp", [(i, i ^ 1) for i in range(4)]),
            lax.ppermute(right_s, "dp", [(i, i ^ 2) for i in range(4)]),
        ]
        context_rows = after(context_rows, mine_s)
        group_e = (mine_e, plane_e, *after([from_core(mine_e), from_core(plane_e)], mine_s))
        sibling_e = from_core(after(expand_weight, joined))
        sibling_o = from_core(after(output_weight, joined))
        expand = halves(shapes[2], expand_weight, sibling_e, group_e, 0)
        output = halves(shapes[1], output_weight, sibling_o, group_e, expand_weight.shape[1] // 2)
    unit1, scale1, normed_low, output = first_norm(pos, context_rows, output, out_bias, token_rows, gain1, shift1)
    active, slope, expand = expand_act(pos, normed_low, expand, hidden_bias)
    if pieces:
        plane_s = beside(*after(plane_s, active))
        other_s = [from_core(mine_s), from_core(plane_s)]
        sibling_s = from_core(after(shrink_weight, active))
        shrink = Weight(
            shapes[3],
            [shrink_weight, sibling_s, mine_s, plane_s, *other_s],
            functools.partial(stacked_copies, high=shrink_weight.shape[0], wide=shrink_weight.shape[1]),
        )
    out_rows, shrink_low, second_grad, sums2, shrink = second_norm(
        pos, captions, active, shrink, down_bias, unit1, gain1, shift1, gain2, shift2, cot_rows, seq
    )
    if pieces:
        mine_s, theirs_s = stacked_grad(pos, active, shrink_low, 1)
        theirs_s = from_core(theirs_s)
        mine_z, theirs_z = stacked_grad(pos, active, after(shrink_low, mine_s), 0)
        theirs_z = from_core(theirs_z)
        near_s = both_sum(mine_s, after(theirs_s, mine_z))
        shrink_low = after(shrink_low, near_s)
        near_s = from_chip(near_s, 1)
    else:
        grad_shrink = weight_grad(active, shrink_low)
    expand_low, sums_hidden = hidden_back(shrink_low, shrink, slope)
    if pieces:
        keep_s = both_sum(mine_z, after(theirs_z, expand_low))
        expand_low = after(expand_low, keep_s)
        mine_e, theirs_e = halves_grad(pos, normed_low, expand_low)
        theirs_e = from_core(theirs_e)
        expand_low = after(expand_low, mine_e)
    first_grad, branch_low, context_grad, sums1 = first_back(
        expand_low, expand, second_grad, unit1, scale1, gain1, output
    )
    if pieces:
        mine_o, theirs_o = halves_grad(pos, context_rows, branch_low)
        theirs_o = from_core(theirs_o)
        own_eo, *out_eo = core_sum([mine_e, mine_o], [theirs_e, theirs_o])
        plane_eo = from_plane(out_eo)
        keep_s, far_s = pair_sum(keep_s, after(near_s, own_eo))
        context_grad = after(context_grad, keep_s)
        far_s = from_chip(far_s, 2)
    else:
        grad_expand = weight_grad(normed_low, expand_low)
        grad_output = weight_grad(context_rows, branch_low)
    joined_grad, sums_joined = attend_back(joined3, probs, context_grad.reshape(pairs, seq, width))
    joined_grad_rows = joined_grad.reshape(rows, 3 * width)
    if pieces:
        extra = bundle(sums_joined, sums1, sums2, sums_hidden)
        mine_p, theirs_p = halves_grad(pos, token_rows, joined_grad_rows, extra)
        theirs_p = from_core(theirs_p)
        far_s = after(far_s, mine_p)
        keep_eo, near_eo = plane_sum([own_eo, *after(plane_eo, far_s)], flops=COVER)
        own_p, *out_p = core_sum([mine_p], [after(theirs_p, near_eo)], (keep_s, far_s))
        near_eo = from_chip(near_eo, 1)
        plane_p = from_plane(out_p)
        joined_grad_rows = after(joined_grad_rows, own_p)
    else:
        grad_project = weight_grad(token_rows, joined_grad_rows)

        def owned(grad):
            part = lax.psum_scatter(grad, "fsdp", scatter_dimension=0, tiled=True)
            return lax.psum(part, "dp").astype(F32)

        own_project, own_output, own_expand, own_shrink = (
            owned(grad) for grad in (grad_project, grad_output, grad_expand, grad_shrink)
        )
        small = (sums_joined[0], sums1[0], sums1[1], sums1[2], sums_hidden[0], sums2[0], sums2[1], sums2[2])
        packed_grad = jnp.concatenate([v.reshape(parts, -1) for v in small], axis=1)
        shard = lax.psum(lax.psum_scatter(packed_grad.reshape(-1), "fsdp", scatter_dimension=0, tiled=True), "dp")
    token_grad = token_back(joined_grad_rows, project, first_grad)
    if pieces:
        half_p, half_e, half_o = project_weight.shape[1] // 2, expand_weight.shape[1] // 2, width // 2
        keep_eo, far_eo = pair_sum(keep_eo, after(near_eo, token_grad))
        far_eo = from_chip(far_eo, 2)
        keep_p, near_p, total_s = plane_sum([own_p, *after(plane_p, keep_eo)], more=2 * width // 4)
        near_p = from_chip(near_p, 1)
        total_seo = last_sum(keep_eo, after(far_eo, keep_p), total_s)
        quarters_seo = from_plane(total_seo)
        keep_p, far_p = pair_sum(keep_p, after(near_p, total_seo))
        total_p = last_sum(keep_p, from_chip(far_p, 2))
        quarters_p = from_plane(total_p)
        own_shrink, own_expand, own_output = place(
            pos, [total_seo, *after(quarters_seo, total_p)], (("stacked", 2 * width), ("halves", half_e), ("halves", half_o))
        )
        own_project, shard = place(
            pos, [total_p, *after(quarters_p, own_expand)], (("halves", half_p), ("small", 128))
        )
        shard = shard[:12, :96].reshape(-1)

    smalls, at = [], 0
    for size in widths:
        smalls.append(shard[at : at + size])
        at += size
    return (
        out_rows.reshape(pairs, seq, width),
        token_grad.reshape(pairs, seq, width),
        own_project,
        smalls[0],
        own_output,
        smalls[1],
        smalls[2],
        smalls[3],
        own_expand,
        smalls[4],
        own_shrink,
        smalls[5],
        smalls[6],
        smalls[7],
    )


def solution(mesh):
    rows3 = P(("dp", "fsdp"), None, None)
    matrix, vector = P("fsdp", None), P("fsdp")
    pieces = mesh.shape["dp"] == 4 and mesh.shape["fsdp"] == 8
    return jax.shard_map(
        functools.partial(local, pieces),
        mesh=mesh,
        in_specs=(
            rows3, P(("dp", "fsdp")), rows3,
            matrix, vector, matrix, vector, vector, vector,
            matrix, vector, matrix, vector, vector, vector,
        ),
        out_specs=(
            rows3, rows3,
            matrix, vector, matrix, vector, vector, vector,
            matrix, vector, matrix, vector, vector, vector,
        ),
        check_vma=False,
    )
```

```python
import functools

import jax
import jax.numpy as jnp
from jax import lax
from jax.experimental import pallas as pl
from jax.experimental.pallas import tpu as pltpu
from jax.sharding import PartitionSpec as P

HEADS = 12
HEAD_DIM = 64
REGIONS = 36
BF16 = jnp.bfloat16
F32 = jnp.float32

COVER = 100 * 10**9

NN = (((1,), (0,)), ((), ()))
NT = (((1,), (1,)), ((), ()))
TN = (((0,), (0,)), ((), ()))


def dot(left, right, dims=NN):
    return lax.dot_general(left, right, dims, preferred_element_type=F32)


def params(mebibytes):
    return pltpu.CompilerParams(vmem_limit_bytes=mebibytes * 1024 * 1024)


def cost(flops=0):
    return pl.CostEstimate(flops=flops, bytes_accessed=0, transcendentals=0)


def whole(shape, buffers=None):
    mode = None if buffers is None else pl.Buffered(buffers)
    return pl.BlockSpec(shape, lambda *at: (0,) * len(shape), pipeline_mode=mode)


HELD = pl.BlockSpec(memory_space=pltpu.VMEM)


def inside(shape, dtype=BF16):
    return pltpu.VMEM(shape, dtype)


def outside(shape, dtype=BF16):
    return pltpu.HBM(shape, dtype)


def in_vmem(values):
    return pltpu.with_memory_space_constraint(values, pltpu.VMEM)


def in_hbm(values):
    return pltpu.with_memory_space_constraint(values, pltpu.HBM)


def tile_of(size, most):
    return max(t for t in range(128, most + 1, 128) if size % t == 0)


def rows_of(count, most):
    fits = [t for t in range(16, most + 1, 16) if count % t == 0]
    return max(fits) if fits else count


CHIPS = (1, 3, 2)


def halves_copies(refs, into, pos, at, high, wide):
    half = wide // 2
    rows = high // 2
    for side in range(2):
        core = pos[1] if side == 0 else 1 - pos[1]
        shard = pos[0] * 2 + core
        yield refs[side], into.at[pl.ds(pl.multiple_of(shard * high, 16), high), :]
        for flip in range(4):
            buffer, first = refs[2 + side * 2 + (flip > 0)], max(flip - 1, 0) * 3 * rows
            up = pos[2] ^ (flip // 2)
            along = pos[3] ^ (flip % 2)
            for place, chip in enumerate(CHIPS):
                shard = (pos[0] ^ chip) * 2 + core
                to_row = pl.multiple_of(shard * high + up * rows, 16)
                to_column = pl.multiple_of(along * half, 128)
                yield (
                    buffer.at[pl.ds(first + place * rows, rows), pl.ds(at, half)],
                    into.at[pl.ds(to_row, rows), pl.ds(to_column, half)],
                )


def stacked_copies(refs, into, pos, high, wide):
    rows = high // 8
    own = pos[2] * 2 + pos[3]
    for side in range(2):
        core = pos[1] if side == 0 else 1 - pos[1]
        shard = pos[0] * 2 + core
        yield refs[side], into.at[pl.ds(pl.multiple_of(shard * high, 16), high), :]
        for place, chip in enumerate(CHIPS):
            shard = (pos[0] ^ chip) * 2 + core
            for plane in range(2):
                for block in range(2):
                    for part in range(2):
                        flip = block * (2 if part == plane else 1)
                        if plane:
                            flip = (1, 3)[block] if part == 0 else (2, 3)[block]
                        to_row = pl.multiple_of(shard * high + ((own ^ flip) * 2 + part) * rows, 16)
                        yield (
                            refs[2 + side * 2 + plane].at[
                                pl.ds((place * 2 + block) * rows, rows), pl.ds(part * wide, wide)
                            ],
                            into.at[pl.ds(to_row, rows), :],
                        )


def natural_copies(refs, into, pos):
    yield refs[0], into


class Weight:
    def __init__(self, shape, arrays, copies=natural_copies):
        self.shape, self.copies = shape, copies
        self.arrays = [in_vmem(array) for array in arrays]

    def specs(self):
        return [HELD] * len(self.arrays)

    def out(self):
        return inside(self.shape)

    def split(self, refs):
        return refs[: len(self.arrays)], refs[len(self.arrays) : -1], refs[-1]

    def arrive(self, refs, full, pos):
        @pl.when(pl.program_id(0) == 0)
        def _():
            for source, target in self.copies(refs, full, pos):
                target[...] = source[...]


def spread_kernel(pos, own, other, bias, hidden, rows, held):
    part = held.shape[2] * 3 // 4
    for at, chip in enumerate((0, *CHIPS)):
        held[(pos[0] ^ chip) * 2 + pos[1]] = own[at * 16 : at * 16 + 16].astype(F32)
        held[(pos[0] ^ chip) * 2 + 1 - pos[1]] = other[at * 16 : at * 16 + 16].astype(F32)
    bias[...] = jnp.zeros_like(bias)
    width = rows.shape[1]
    for shard in range(8):
        for at in range(2):
            to = (shard * 2 + at) * part
            to += width if to >= width else 0
            bias[0:1, to : to + part] = held[shard, at : at + 1, :part]
        for at in range(4):
            to = (shard * 4 + at) * part
            hidden[0:1, to : to + part] = held[shard, 5 + at : 6 + at, :part]
        to = shard * part
        rows[0:3, to : to + part] = held[shard, 2:5, :part]
        rows[3:6, to : to + part] = held[shard, 9:12, :part]


def spread(pos, shards, width, hidden_width):
    shapes = [(1, 3 * width), (1, hidden_width), (8, width)]
    return pl.pallas_call(
        spread_kernel,
        grid_spec=pltpu.PrefetchScalarGridSpec(
            num_scalar_prefetch=1,
            grid=(1,),
            in_specs=[whole((64, 128))] * 2,
            out_specs=[whole(shape) for shape in shapes],
            scratch_shapes=[pltpu.VMEM((8, 16, 128), F32)],
        ),
        out_shape=[jax.ShapeDtypeStruct(shape, F32) for shape in shapes],
        compiler_params=params(4),
        cost_estimate=cost(COVER),
        name="spread",
    )(pos, *shards)


def bundle_kernel(joined, first, second, hidden, out):
    part = out.shape[2] * 3 // 4
    out[...] = jnp.zeros_like(out)
    for shard in range(8):
        for at in range(2):
            of = (shard * 2 + at) * part
            out[shard, at : at + 1, :part] = joined[0:1, of : of + part]
        for at in range(4):
            of = (shard * 4 + at) * part
            out[shard, 5 + at : 6 + at, :part] = hidden[0:1, of : of + part]
        of = shard * part
        out[shard, 2:5, :part] = first[0:3, of : of + part]
        out[shard, 9:12, :part] = second[0:3, of : of + part]


def bundle(joined, first, second, hidden):
    return pl.pallas_call(
        bundle_kernel,
        out_shape=jax.ShapeDtypeStruct((8, 16, 128), F32),
        compiler_params=params(4),
        cost_estimate=cost(),
        name="bundle",
    )(joined, first, second, hidden)


def step_of(size):
    return pl.ds(pl.multiple_of(pl.program_id(0) * size, 16), size)


def columns_of(size):
    return pl.ds(pl.multiple_of(pl.program_id(0) * size, 128), size)


def join_kernel(pos, tokens, bias, *rest, weight, tile):
    pieces, (out, kept), (full, sem) = rest[: len(weight.arrays)], rest[-4:-2], rest[-2:]
    weight.arrive(pieces, full, pos)
    write = pltpu.make_async_copy(full, kept, sem)

    @pl.when(pl.program_id(0) == 0)
    def _():
        write.start()

    out[...] = (dot(tokens[...], full[:, columns_of(tile)]) + bias[...]).astype(BF16)

    @pl.when(pl.program_id(0) == pl.num_programs(0) - 1)
    def _():
        write.wait()


def join(pos, token_rows, weight, bias):
    rows, width = token_rows.shape
    columns = weight.shape[1]
    tile = tile_of(columns, 768)
    return pl.pallas_call(
        functools.partial(join_kernel, weight=weight, tile=tile),
        grid_spec=pltpu.PrefetchScalarGridSpec(
            num_scalar_prefetch=1,
            grid=(columns // tile,),
            in_specs=[whole((rows, width), 1), pl.BlockSpec((1, tile), lambda i, p: (0, i))] + weight.specs(),
            out_specs=[pl.BlockSpec((rows, tile), lambda i, p: (0, i)), pl.BlockSpec(memory_space=pltpu.HBM)],
            scratch_shapes=[pltpu.VMEM(weight.shape, BF16), pltpu.SemaphoreType.DMA(())],
        ),
        out_shape=[outside((rows, columns)), outside(weight.shape)],
        compiler_params=params(15),
        cost_estimate=cost(),
        name="join",
    )(pos, token_rows, bias, *weight.arrays)


def head_stack(block, low_half, padded):
    rows = block.shape[0]
    filler = jnp.zeros((padded - rows, block.shape[1]), F32)
    first = jnp.where(low_half, block, 0.0)
    second = jnp.where(low_half, 0.0, block)
    return jnp.concatenate([first, filler, second, filler], axis=0).astype(BF16)


def attend_kernel(captions, joined, context, probs):
    seq = joined.shape[1]
    width = context.shape[2]
    padded = probs.shape[3] // 2
    valid = captions[pl.program_id(0)] + 2 + REGIONS
    keep = lax.broadcasted_iota(jnp.int32, (seq, 2 * padded), 0) < valid
    low_half = lax.broadcasted_iota(jnp.int32, (1, 2 * HEAD_DIM), 1) < HEAD_DIM
    places = [pair * 2 * HEAD_DIM for pair in range(HEADS // 2)]
    scores = []
    for at in places:
        query = joined[0, :, at : at + 2 * HEAD_DIM].astype(F32)
        keys = joined[0, :, width + at : width + at + 2 * HEAD_DIM]
        scores.append(dot(keys, head_stack(query, low_half, padded), NT) * HEAD_DIM ** (-0.5))
    probabilities = []
    for score in scores:
        score = jnp.where(keep, score, -1000000000.0)
        grown = jnp.exp(score - jnp.max(score, axis=0, keepdims=True))
        total = jnp.sum(grown, axis=0, keepdims=True)
        probabilities.append((grown * (1.0 / total)).astype(BF16))
    for pair, at in enumerate(places):
        values = joined[0, :, 2 * width + at : 2 * width + at + 2 * HEAD_DIM]
        mixed = dot(probabilities[pair], values, TN)
        probs[0, pair] = probabilities[pair]
        context[0, :, at : at + 2 * HEAD_DIM] = jnp.where(
            low_half, mixed[:seq], mixed[padded : padded + seq]
        ).astype(BF16)


def attend(joined, captions):
    pairs, seq, columns = joined.shape
    width = columns // 3
    padded = (seq + 127) // 128 * 128
    return pl.pallas_call(
        attend_kernel,
        grid_spec=pltpu.PrefetchScalarGridSpec(
            num_scalar_prefetch=1,
            grid=(pairs,),
            in_specs=[pl.BlockSpec((1, seq, columns), lambda i, c: (i, 0, 0))],
            out_specs=[
                pl.BlockSpec((1, seq, width), lambda i, c: (i, 0, 0)),
                pl.BlockSpec((1, HEADS // 2, seq, 2 * padded), lambda i, c: (i, 0, 0, 0)),
            ],
        ),
        out_shape=[
            inside((pairs, seq, width)),
            outside((pairs, HEADS // 2, seq, 2 * padded)),
        ],
        compiler_params=params(8),
        cost_estimate=cost(),
        name="attend",
    )(captions, in_hbm(joined))


def attend_back_kernel(joined, probs, grads, out, sums):
    seq = joined.shape[1]
    width = grads.shape[2]
    padded = probs.shape[3] // 2
    low_half = lax.broadcasted_iota(jnp.int32, (1, 2 * HEAD_DIM), 1) < HEAD_DIM

    @pl.when(pl.program_id(0) == 0)
    def _():
        sums[...] = jnp.zeros_like(sums)

    places = [pair * 2 * HEAD_DIM for pair in range(HEADS // 2)]
    prob_grads, grad_stacks = [], []
    for at in places:
        values = joined[0, :, 2 * width + at : 2 * width + at + 2 * HEAD_DIM]
        grad_stacks.append(head_stack(grads[0, :, at : at + 2 * HEAD_DIM].astype(F32), low_half, padded))
        prob_grads.append(dot(values, grad_stacks[-1], NT))
    score_grads = []
    for pair, prob_grad in enumerate(prob_grads):
        prob = probs[0, pair].astype(F32)
        row_dot = jnp.sum(prob * prob_grad, axis=0, keepdims=True)
        score_grads.append((prob * (prob_grad - row_dot) * HEAD_DIM ** (-0.5)).astype(BF16))
    results = []
    for pair, at in enumerate(places):
        query = joined[0, :, at : at + 2 * HEAD_DIM].astype(F32)
        keys = joined[0, :, width + at : width + at + 2 * HEAD_DIM]
        mixed = dot(score_grads[pair], keys, TN)
        query_grad = jnp.where(low_half, mixed[:seq], mixed[padded : padded + seq])
        keys_grad = dot(score_grads[pair], head_stack(query, low_half, padded))
        results.append((query_grad, keys_grad, dot(probs[0, pair], grad_stacks[pair])))
    for at, blocks in zip(places, results):
        for part, block in enumerate(blocks):
            out[0, :, part * width + at : part * width + at + 2 * HEAD_DIM] = block.astype(BF16)
            if part != 1:
                to = part // 2 * width + at
                sums[:, to : to + 2 * HEAD_DIM] += jnp.sum(block, axis=0, keepdims=True)


def attend_back(joined, probs, grads):
    pairs, seq, columns = joined.shape
    width = columns // 3
    padded = probs.shape[3] // 2
    return pl.pallas_call(
        attend_back_kernel,
        grid=(pairs,),
        in_specs=[
            pl.BlockSpec((1, seq, columns), lambda i: (i, 0, 0)),
            pl.BlockSpec((1, HEADS // 2, seq, 2 * padded), lambda i: (i, 0, 0, 0)),
            pl.BlockSpec((1, seq, width), lambda i: (i, 0, 0)),
        ],
        out_specs=[
            pl.BlockSpec((1, seq, columns), lambda i: (i, 0, 0)),
            pl.BlockSpec((1, 2 * width), lambda i: (0, 0)),
        ],
        out_shape=[
            inside((pairs, seq, columns)),
            jax.ShapeDtypeStruct((1, 2 * width), F32),
        ],
        compiler_params=params(10),
        cost_estimate=cost(),
        name="attend_back",
    )(in_hbm(joined), in_hbm(probs), in_vmem(grads))


def norm_parts(values):
    centred = values - jnp.mean(values, axis=-1, keepdims=True)
    spread = jnp.mean(centred * centred, axis=-1, keepdims=True)
    scale = lax.rsqrt(spread + 1e-05)
    return centred * scale, scale


def norm_back(upstream, unit, scale, gain):
    scaled = upstream * gain
    return scale * (
        scaled
        - jnp.mean(scaled, axis=-1, keepdims=True)
        - unit * jnp.mean(scaled * unit, axis=-1, keepdims=True)
    )


def add_sums(sums, rows):
    for at, values in enumerate(rows):
        sums[at : at + 1, :] += jnp.sum(values, axis=0, keepdims=True)


def chunked(count, load, use):
    ready = load(0)
    for at in range(count):
        following = load(at + 1) if at + 1 < count else None
        use(at, ready)
        ready = following


def chunk_slices(rows, most):
    tile = rows_of(rows, most)
    return [slice(at, at + tile) for at in range(0, rows, tile)]


def first_kernel(pos, context, bias, tokens, gain, shift, *rest, weight):
    pieces, (unit, scale, normed_low), full = weight.split(rest)
    weight.arrive(pieces, full, pos)
    chunks = chunk_slices(tokens.shape[0], 416)

    def normalise(at, branch):
        rows = chunks[at]
        unit_rows, scale_rows = norm_parts(tokens[rows, :].astype(F32) + (branch + bias[...]))
        unit[rows, :] = unit_rows
        scale[rows, :] = scale_rows
        normed_low[rows, :] = (unit_rows * gain[...] + shift[...]).astype(BF16)

    chunked(len(chunks), lambda at: dot(context[chunks[at], :], full[...]), normalise)


def first_norm(pos, context, weight, bias, token_rows, gain, shift):
    rows, width = token_rows.shape
    row = whole((1, width))
    return pl.pallas_call(
        functools.partial(first_kernel, weight=weight),
        grid_spec=pltpu.PrefetchScalarGridSpec(
            num_scalar_prefetch=1,
            grid=(1,),
            in_specs=[HELD, row, HELD, row, row] + weight.specs(),
            out_specs=[HELD] * 4,
        ),
        out_shape=[inside((rows, width), F32), inside((rows, 1), F32), inside((rows, width)), weight.out()],
        compiler_params=params(10),
        cost_estimate=cost(),
        name="first_norm",
    )(pos, in_vmem(context), bias, in_vmem(token_rows), gain, shift, *weight.arrays)


def expand_kernel(pos, normed_low, bias, *rest, weight, tile):
    pieces, (active, slope), full = weight.split(rest)
    weight.arrive(pieces, full, pos)
    at = columns_of(tile)
    expand = dot(normed_low[...], full[:, at]) + bias[...]
    half = 0.5 * (1.0 + lax.erf(expand * 0.7071067811865476))
    active[:, at] = (expand * half).astype(BF16)
    slope[:, at] = (half + expand * jnp.exp(-0.5 * expand * expand) * 0.3989422804014327).astype(BF16)


def expand_act(pos, normed_low, weight, bias):
    rows, width = normed_low.shape
    columns = weight.shape[1]
    tile = tile_of(columns, 768)
    return pl.pallas_call(
        functools.partial(expand_kernel, weight=weight, tile=tile),
        grid_spec=pltpu.PrefetchScalarGridSpec(
            num_scalar_prefetch=1,
            grid=(columns // tile,),
            in_specs=[HELD, pl.BlockSpec((1, tile), lambda i, p: (0, i))] + weight.specs(),
            out_specs=[HELD] * 3,
        ),
        out_shape=[inside((rows, columns))] * 2 + [weight.out()],
        compiler_params=params(12),
        cost_estimate=cost(),
        name="expand_act",
    )(pos, in_vmem(normed_low), bias, *weight.arrays)


def second_kernel(pos, captions, active, bias, unit, gain, shift, gain2, shift2, cotangent, *rest, weight, seq):
    pieces, (out, low, grad, sums), full, (held, sems) = *weight.split(rest[:-2]), rest[-2:]
    weight.arrive(pieces, full, pos)
    sums[...] = jnp.zeros_like(sums)
    tile = rows_of(held.shape[0], 4 * seq)
    count = held.shape[0] // tile

    def write(at):
        rows = pl.ds(pl.multiple_of(at * tile, 16), tile)
        return pltpu.make_async_copy(held.at[rows, :], out.at[rows, :], sems.at[at])

    def chunk(at, carry):
        rows = pl.ds(pl.multiple_of(at * tile, 16), tile)
        normed = unit[rows, :] * gain[...] + shift[...]
        unit2, scale2 = norm_parts(normed + (dot(active[rows, :], full[...]) + bias[...]))
        held[rows, :] = (unit2 * gain2[...] + shift2[...]).astype(BF16)
        write(at).start()
        row = lax.broadcasted_iota(jnp.int32, (tile, 1), 0)
        live = jnp.zeros(row.shape, jnp.bool_)
        for pair in range(tile // seq):
            valid = captions[at * (tile // seq) + pair] + 2 + REGIONS
            live = live | ((row >= pair * seq) & (row < pair * seq + valid))
        upstream = jnp.where(live, cotangent[rows, :].astype(F32), 0.0)
        second = norm_back(upstream, unit2, scale2, gain2[...])
        grad[rows, :] = second
        low[rows, :] = second.astype(BF16)
        add_sums(sums, (second, upstream * unit2, upstream))
        return carry

    lax.fori_loop(0, count, chunk, 0)
    for at in range(count):
        write(at).wait()


def second_norm(pos, captions, active, weight, bias, unit, gain, shift, gain2, shift2, cotangent, seq):
    rows, width = unit.shape
    row = whole((1, width))
    return pl.pallas_call(
        functools.partial(second_kernel, weight=weight, seq=seq),
        grid_spec=pltpu.PrefetchScalarGridSpec(
            num_scalar_prefetch=2,
            grid=(1,),
            in_specs=[HELD, row, HELD, row, row, row, row, HELD] + weight.specs(),
            out_specs=[pl.BlockSpec(memory_space=pltpu.HBM), HELD, HELD, whole((8, width)), HELD],
            scratch_shapes=[pltpu.VMEM((rows, width), BF16), pltpu.SemaphoreType.DMA((rows // 16,))],
        ),
        out_shape=[
            outside((rows, width)),
            inside((rows, width)),
            inside((rows, width), F32),
            jax.ShapeDtypeStruct((8, width), F32),
            weight.out(),
        ],
        compiler_params=params(12),
        cost_estimate=cost(),
        name="second_norm",
    )(pos, captions, in_vmem(active), bias, in_vmem(unit), gain, shift, gain2, shift2, in_vmem(cotangent), *weight.arrays)


def hidden_back_kernel(low, weight, slope, out, sums):
    at = columns_of(sums.shape[1])
    grad = dot(low[...], weight[at, :], NT) * slope[:, at].astype(F32)
    out[:, at] = grad.astype(BF16)
    sums[...] = jnp.sum(grad, axis=0, keepdims=True)


def hidden_back(low, weight, slope):
    rows, width = low.shape
    hidden = weight.shape[0]
    tile = tile_of(hidden, 768)
    return pl.pallas_call(
        hidden_back_kernel,
        grid=(hidden // tile,),
        in_specs=[HELD] * 3,
        out_specs=[HELD, pl.BlockSpec((1, tile), lambda i: (0, i))],
        out_shape=[inside((rows, hidden)), jax.ShapeDtypeStruct((1, hidden), F32)],
        compiler_params=params(10),
        cost_estimate=cost(),
        name="hidden_back",
    )(in_vmem(low), in_vmem(weight), in_vmem(slope))


def first_back_kernel(hidden, weight, second, unit, scale, gain, out_weight, grad, low, context_grad, sums):
    sums[...] = jnp.zeros_like(sums)
    chunks = chunk_slices(grad.shape[0], 416)
    waiting = []

    def pass_on():
        rows, first_low = waiting.pop()
        context_grad[rows, :] = dot(first_low, out_weight[...], NT).astype(BF16)

    def normalise(at, product):
        rows = chunks[at]
        unit_rows = unit[rows, :]
        normed_grad = product + second[rows, :]
        first = norm_back(normed_grad, unit_rows, scale[rows, :], gain[...])
        grad[rows, :] = first
        first_low = first.astype(BF16)
        low[rows, :] = first_low
        add_sums(sums, (first, normed_grad * unit_rows, normed_grad))
        if waiting:
            pass_on()
        waiting.append((rows, first_low))

    chunked(len(chunks), lambda at: dot(hidden[chunks[at], :], weight[...], NT), normalise)
    pass_on()


def first_back(hidden, weight, second, unit, scale, gain, out_weight):
    rows, width = second.shape
    return pl.pallas_call(
        first_back_kernel,
        grid=(1,),
        in_specs=[HELD] * 5 + [whole((1, width)), HELD],
        out_specs=[HELD, HELD, HELD, whole((8, width))],
        out_shape=[
            inside((rows, width), F32),
            inside((rows, width)),
            inside((rows, width)),
            jax.ShapeDtypeStruct((8, width), F32),
        ],
        compiler_params=params(13),
        cost_estimate=cost(COVER),
        name="first_back",
    )(in_vmem(hidden), in_vmem(weight), in_vmem(second), in_vmem(unit), in_vmem(scale), gain, in_vmem(out_weight))


def token_back_kernel(grads, weight, first, out):
    at = step_of(out.shape[0])
    out[...] = dot(grads[at, :], weight[...], NT) + first[at, :]


def token_back(grads, weight, first):
    rows, width = first.shape
    tile = rows_of(rows, 416)
    return pl.pallas_call(
        token_back_kernel,
        grid=(rows // tile,),
        in_specs=[HELD] * 3,
        out_specs=pl.BlockSpec((tile, width), lambda i: (i, 0)),
        out_shape=outside((rows, width), F32),
        compiler_params=params(9),
        cost_estimate=cost(),
        name="token_back",
    )(in_vmem(grads), in_vmem(weight), in_vmem(first))


def weight_grad_kernel(left, right, out):
    out[...] = dot(left[...], right[...], TN).astype(BF16)


def weight_grad(left, right):
    rows, height = left.shape
    columns = right.shape[1]
    tile = tile_of(columns, 768)
    high = tile_of(height, 768)
    return pl.pallas_call(
        weight_grad_kernel,
        grid=(height // high, columns // tile),
        in_specs=[
            pl.BlockSpec((rows, high), lambda i, j: (0, i)),
            pl.BlockSpec((rows, tile), lambda i, j: (0, j)),
        ],
        out_specs=pl.BlockSpec((high, tile), lambda i, j: (i, j)),
        out_shape=outside((height, columns)),
        compiler_params=params(24),
        cost_estimate=cost(),
        name="weight_grad",
    )(left, right)


def store_halves(out, core, grads, pos, along, extra):
    rows, wide = out.shape[3], grads.shape[1]
    for chip in range(4):
        for up in range(2):
            at = ((chip * 2 + core) * 2 + up) * rows
            to = (chip ^ pos[0], up ^ pos[2], along ^ pos[3])
            out[(*to, slice(None), slice(0, wide))] = grads[at : at + rows].astype(BF16)
            if extra is not None:
                out[(*to, slice(None), slice(wide, None))] = jnp.zeros((rows, 128), BF16)
                out[(*to, slice(0, 16), slice(wide, None))] = extra[chip * 2 + core].astype(BF16)


def store_stacked(out, core, grads, pos, chip):
    rows, wide = out.shape[3], grads.shape[1]
    for quarter in range(4):
        for part in range(2):
            at = ((core * 4 + quarter) * 2 + part) * rows
            to = (chip ^ pos[0], (quarter // 2) ^ pos[2], (quarter % 2) ^ pos[3])
            out[(*to, slice(None), slice(part * wide, (part + 1) * wide))] = grads[at : at + rows].astype(BF16)


def by_core(pos, mine, theirs, store):
    for core in range(2):

        @pl.when(pos[1] == core)
        def _(core=core):
            store(mine, core)
            store(theirs, 1 - core)


def halves_grad_kernel(pos, left, right, *rest):
    extra, (mine, theirs) = (rest[0] if len(rest) == 3 else None), rest[-2:]
    along, half = pl.program_id(0), right.shape[1] // 2
    grads = dot(left[...], right[:, columns_of(half)], TN)
    by_core(pos, mine, theirs, lambda out, core: store_halves(out, core, grads, pos, along, extra))


def stacked_grad_kernel(pos, left, right, mine, theirs):
    high = left.shape[1] // 4
    grads = dot(left[:, columns_of(2 * high)], right[...], TN)
    for part in range(2):
        chip, block = pl.program_id(0) * 2 + part, grads[part * high : (part + 1) * high]
        by_core(pos, mine, theirs, lambda out, core: store_stacked(out, core, block, pos, chip))


def pieces_grad(kernel, name, pos, left, right, shape, extra=()):
    out = inside((4, 2, 2) + shape)
    return pl.pallas_call(
        kernel,
        grid_spec=pltpu.PrefetchScalarGridSpec(
            num_scalar_prefetch=1,
            grid=(2,),
            in_specs=[HELD, HELD] + [whole(array.shape) for array in extra],
            out_specs=[HELD, HELD],
        ),
        out_shape=[out, out],
        compiler_params=params(13),
        cost_estimate=cost(),
        name=name,
    )(pos, in_vmem(left), in_vmem(right), *extra)


def halves_grad(pos, left, right, extra=None):
    shape = (left.shape[1] // 16, right.shape[1] // 2 + (0 if extra is None else 128))
    more = () if extra is None else (extra,)
    return pieces_grad(halves_grad_kernel, "halves_grad", pos, left, right, shape, more)


def stacked_grad(pos, left, right):
    shape = (left.shape[1] // 64, 2 * right.shape[1])
    return pieces_grad(stacked_grad_kernel, "stacked_grad", pos, left, right, shape)


def held_call(kernel, name, outs, values, flops=0):
    return pl.pallas_call(
        kernel,
        in_specs=[HELD] * len(values),
        out_specs=[HELD] * len(outs),
        out_shape=[inside(out) for out in outs],
        compiler_params=params(4),
        cost_estimate=cost(flops),
        name=name,
    )(*map(in_vmem, values))


def add(*terms):
    total = terms[0].astype(F32)
    for term in terms[1:]:
        total += term.astype(F32)
    return total


FIRST = 1024


def shrink_sum_kernel(mine, theirs, keep, near, kept, send):
    for chip in range(4):
        for flip in range(4):
            pick = (chip, flip // 2, flip % 2)
            total = add(mine[pick], theirs[pick]).astype(BF16)
            (keep, near)[chip % 2][chip // 2, flip] = total[:, :FIRST]
            (kept, send)[flip % 2][flip // 2, chip] = total[:, FIRST:]


def shrink_sum(mine, theirs):
    rows, wide = mine.shape[3:]
    outs = [(2, 4, rows, FIRST)] * 2 + [(2, 4, rows, wide - FIRST)] * 2
    return held_call(shrink_sum_kernel, "shrink_sum", outs, [mine, theirs])


def core_split_kernel(*refs, count):
    outs = refs[-6:]
    for half in range(2):
        own, later, send = outs[3 * half : 3 * half + 3]
        first = 1 + half
        for flip, out in ((0, own), (3 - first, later), (first, send.at[0]), (3, send.at[1])):
            at = 0
            for mine, theirs in zip(refs[:count], refs[count : 2 * count]):
                wide = mine.shape[4]
                for chip in range(2):
                    pick = (2 * half + chip, flip // 2, flip % 2)
                    out[chip, :, at : at + wide] = add(mine[pick], theirs[pick]).astype(BF16)
                at += wide
            if len(refs) > 2 * count + 6:
                near, far = refs[2 * count : 2 * count + 2]
                wide = near.shape[2] // 4
                for chip in range(2):
                    columns = slice((2 * half + chip) * wide, (2 * half + chip + 1) * wide)
                    out[chip, :, at:] = add(near[flip, :, columns], far[flip, :, columns]).astype(BF16)


def core_split(mine, theirs, more=()):
    shape = (2, mine[0].shape[3], sum(m.shape[4] for m in mine) + sum(m.shape[2] // 8 for m in more))
    kernel = functools.partial(core_split_kernel, count=len(mine))
    return held_call(kernel, "core_split", [shape, shape, (2,) + shape] * 2, [*mine, *theirs, *more])


def middle_sum_kernel(*refs):
    for half in range(2):
        own, later, received = refs[3 * half : 3 * half + 3]
        refs[6 + 2 * half][...] = add(own[...], received[0]).astype(BF16)
        refs[7 + 2 * half][...] = add(later[...], received[1]).astype(BF16)


def middle_sum(parts):
    return held_call(middle_sum_kernel, "middle_sum", [parts[0].shape] * 4, parts)


def split_sum_kernel(own, received, own_too, received_too, keep, near, *rest):
    for chip in range(4):
        one, two = (own, received) if chip < 2 else (own_too, received_too)
        total = add(one[chip % 2], two[chip % 2]).astype(BF16)
        wide = keep.shape[2]
        (keep, near)[chip % 2][chip // 2] = total[:, :wide]
        if rest:
            part = total.shape[1] - wide
            rest[0][:, chip * part : (chip + 1) * part] = total[:, wide:]


def split_sum(parts, more=0, flops=0):
    _, rows, wide = parts[0].shape
    outs = [(2, rows, wide - more)] * 2 + ([(rows, 4 * more)] if more else [])
    return held_call(split_sum_kernel, "split_sum", outs, parts, flops)


def ahead_sum_kernel(one, two, keep, near, keep_out, near_out):
    wide = one.shape[2]
    for chip in range(4):
        source, out = (keep, keep_out) if chip % 2 == 0 else (near, near_out)
        out[chip // 2, :, :wide] = add(one[chip], two[chip]).astype(BF16)
        out[chip // 2, :, wide:] = source[chip // 2]


def ahead_sum(one, two, keep, near):
    shape = keep.shape[:2] + (keep.shape[2] + one.shape[2],)
    return held_call(ahead_sum_kernel, "ahead_sum", [shape] * 2, [one, two, keep, near])


def pair_sum_kernel(keep, received, one, two):
    one[...] = add(keep[0], received[0]).astype(BF16)
    two[...] = add(keep[1], received[1]).astype(BF16)


def pair_sum(keep, received, flops=0):
    return held_call(pair_sum_kernel, "pair_sum", [keep.shape[1:]] * 2, [keep, received], flops)


def last_sum_kernel(*refs, counts):
    out, at = refs[-1], 0
    for count in counts:
        terms, refs = refs[:count], refs[count:]
        wide = terms[0].shape[1]
        out[:, at : at + wide] = add(*(term[...] for term in terms)).astype(BF16)
        at += wide


def last_sum(*groups):
    kernel = functools.partial(last_sum_kernel, counts=[len(group) for group in groups])
    shape = (groups[0][0].shape[0], sum(group[0].shape[1] for group in groups))
    return held_call(kernel, "last_sum", [shape], [part for group in groups for part in group])[0]


def place_kernel(pos, *refs, layout):
    parts, outs = refs[:4], refs[4:]
    rows = parts[0].shape[0]
    for flip, part in enumerate(parts):
        up, along = pos[2] ^ (flip // 2), pos[3] ^ (flip % 2)
        at = 0
        for (kind, wide), out in zip(layout, outs):
            if kind == "halves":
                to_row = pl.multiple_of(up * rows, 16)
                to_column = pl.multiple_of(along * wide, 128)
                out[pl.ds(to_row, rows), pl.ds(to_column, wide)] = part[:, at : at + wide].astype(F32)
            elif kind == "stacked":
                for side in range(2):
                    to_row = pl.multiple_of(((up * 2 + along) * 2 + side) * rows, 16)
                    from_column = at + side * (wide // 2)
                    out[pl.ds(to_row, rows), :] = part[:, from_column : from_column + wide // 2].astype(F32)
            else:

                @pl.when((up == 0) & (along == 0))
                def _(part=part, at=at):
                    row = 0
                    for vector in outs[len(layout) - 1 :]:
                        for to in range(0, vector.shape[1], 96):
                            vector[:, to : to + 96] = part[row : row + 1, at : at + 96].astype(F32)
                            row += 1

            at += wide


def place(pos, parts, layout, sizes=()):
    rows = parts[0].shape[0]
    shapes = {
        "halves": lambda wide: (2 * rows, 2 * wide),
        "stacked": lambda wide: (8 * rows, wide // 2),
    }
    outs = [jax.ShapeDtypeStruct(shapes[kind](wide), F32) for kind, wide in layout if kind != "small"]
    outs += [jax.ShapeDtypeStruct((1, size), F32) for size in sizes]
    return pl.pallas_call(
        functools.partial(place_kernel, layout=layout),
        grid_spec=pltpu.PrefetchScalarGridSpec(
            num_scalar_prefetch=1,
            grid=(1,),
            in_specs=[HELD] * 4,
            out_specs=[whole(out.shape, 1) for out in outs],
        ),
        out_shape=outs,
        compiler_params=params(10),
        cost_estimate=cost(),
        name="place",
    )(pos, *map(in_vmem, parts))


def from_core(values):
    return lax.ppermute(values, "fsdp", [(i, i ^ 1) for i in range(8)])


def from_plane(values):
    parts = values if isinstance(values, (list, tuple)) else [values] * 3
    return [
        lax.ppermute(part, "dp", [(i, i ^ flip) for i in range(4)]) for flip, part in zip((1, 2, 3), parts)
    ]


def from_x(values):
    return lax.ppermute(values, "dp", [(i, i ^ 1) for i in range(4)])


def from_y(values):
    return lax.ppermute(values, "dp", [(i, i ^ 2) for i in range(4)])


def from_chips(values):
    return [from_chip(values, flip) for flip in CHIPS]


def from_chip(values, flip):
    return lax.ppermute(values, "fsdp", [(i, i ^ (2 * flip)) for i in range(8)])


def below_kernel(*refs):
    at = 0
    for ref in refs[:-1]:
        rows, wide = ref.shape[0], refs[-1].shape[1]
        refs[-1][at : at + rows] = ref[:, :wide]
        at += rows


def below(*parts, wide=None, flops=0):
    rows = sum(part.shape[0] for part in parts)
    return pl.pallas_call(
        below_kernel,
        in_specs=[HELD] * len(parts),
        out_specs=HELD,
        out_shape=inside((rows, wide or parts[0].shape[1])),
        compiler_params=params(4),
        cost_estimate=cost(flops),
        name="below",
    )(*map(in_vmem, parts))


def pick_kernel(pos, shard, out):
    rows, wide = out.shape[0] // 2, shard.shape[1]
    own = pos[2] * 2 + pos[3]
    for block, part, flip in ((0, 0, 0), (0, 1, 0), (1, 0, 2), (1, 1, 1)):
        from_row = pl.multiple_of(((own ^ flip) * 2 + part) * rows, 16)
        out[block * rows : (block + 1) * rows, part * wide : (part + 1) * wide] = shard[pl.ds(from_row, rows), :]


def pick(pos, shard):
    return pl.pallas_call(
        pick_kernel,
        grid_spec=pltpu.PrefetchScalarGridSpec(
            num_scalar_prefetch=1, grid=(1,), in_specs=[whole(shard.shape, 1)], out_specs=HELD
        ),
        out_shape=inside((shard.shape[0] // 4, 2 * shard.shape[1])),
        compiler_params=params(4),
        cost_estimate=cost(),
        name="pick",
    )(pos, shard)


def left_right_kernel(whole_ref, left, right):
    half = left.shape[1]
    left[...] = whole_ref[:, :half]
    right[...] = whole_ref[:, half:]


def left_right(values):
    rows, wide = values.shape
    return held_call(left_right_kernel, "left_right", [(rows, wide // 2)] * 2, [values])


def beside_kernel(left, right, out):
    half = left.shape[1]
    out[:, :half] = left[...]
    out[:, half:] = right[...]


def beside(left, right):
    rows, wide = left.shape
    return held_call(beside_kernel, "beside", [(rows, 2 * wide)], [left, right])[0]


def after(values, *others):
    return lax.optimization_barrier((values, others))[0]


def half_of(pos, shard):
    rows, wide = shard.shape[0] // 2, shard.shape[1] // 2
    return lax.dynamic_slice(shard, (pos[2] * rows, pos[3] * wide), (rows, wide))


def both_cores(pieces):
    return [*pieces, *(from_core(piece) for piece in pieces)]


def gather(values):
    return lax.all_gather(values, "fsdp", axis=0, tiled=True)


def local(
    pieces,
    tokens,
    captions,
    cotangent,
    project_weight,
    project_bias,
    output_weight,
    output_bias,
    first_gain,
    first_shift,
    expand_weight,
    expand_bias,
    shrink_weight,
    shrink_bias,
    second_gain,
    second_shift,
):
    pairs, seq, width = tokens.shape
    rows = pairs * seq
    parts = lax.axis_size("fsdp")
    token_rows = tokens.reshape(rows, width)
    cot_rows = cotangent.reshape(rows, width)

    vectors = (project_bias, output_bias, first_gain, first_shift, expand_bias, shrink_bias, second_gain, second_shift)
    widths = [vector.shape[0] for vector in vectors]
    replica, part = lax.axis_index("dp"), lax.axis_index("fsdp")
    pos = jnp.stack([part // 2, part % 2, replica // 2, replica % 2]).astype(jnp.int32)
    shapes = [(parts * shard.shape[0], shard.shape[1]) for shard in (project_weight, output_weight, expand_weight, shrink_weight)]
    if pieces:
        chips_p = from_chips(half_of(pos, project_weight))
        sibling_p = from_core(project_weight)
        held = jnp.concatenate([vector.reshape(-1, 96) for vector in vectors], axis=0)
        held = jnp.pad(held, ((0, 4), (0, 32)))
        quarter_e = [half_of(pos, expand_weight), half_of(pos, output_weight), jnp.pad(held, ((0, 32), (0, 0)))]
        quarter_e = jnp.concatenate(quarter_e, axis=1)
        wide_e = quarter_e.shape[1] - 128
        chips_p = after(chips_p, sibling_p, quarter_e)
        mine_p = below(*chips_p)
        quarter_e = after(quarter_e, *chips_p)
        far_e = from_chip(quarter_e, 2)
        near_e = [from_chip(quarter_e, 1), from_chip(far_e, 1)]
        plane_p = from_plane(mine_p)
        plane_p = below(*plane_p, flops=COVER)
        near_e = after(near_e, plane_p)
        other_p = [from_core(mine_p), from_core(plane_p)]

        def halves(shape, shard, sibling, group, at):
            copies = functools.partial(halves_copies, at=at, high=shard.shape[0], wide=shard.shape[1])
            return Weight(shape, [shard, sibling, *group], copies)

        project = halves(shapes[0], project_weight, sibling_p, (mine_p, plane_p, *other_p), 0)
        quarter_s = pick(pos, after(shrink_weight, quarter_e))
        quarter_s = after(quarter_s, plane_p)
        far_s = from_chip(quarter_s, 2)
        mine_e = below(*near_e, far_e, wide=wide_e)
        plane_e = from_plane(mine_e)
        held = jnp.concatenate([held, *(chip[:16, wide_e:] for chip in (*near_e, far_e))], axis=0)
        held = after(held, mine_e)
        bias_full, hidden_bias, rows6 = spread(pos, [held, from_core(held)], width, expand_weight.shape[1])
        out_bias, gain1, shift1, down_bias, gain2, shift2 = (rows6[at : at + 1] for at in range(6))
    else:
        project, output, expand, shrink = (
            Weight(shape, [gather(shard)])
            for shape, shard in zip(shapes, (project_weight, output_weight, expand_weight, shrink_weight))
        )
        packed = gather(jnp.concatenate(vectors)[None, :])
        full, at = [], 0
        for size in widths:
            full.append(packed[:, at : at + size].reshape(1, parts * size).astype(F32))
            at += size
        bias_row, out_bias, gain1, shift1, hidden_bias, down_bias, gain2, shift2 = full
        bias_full = jnp.concatenate([bias_row[:, :width], jnp.zeros((1, width), F32), bias_row[:, width:]], axis=1)

    joined, project = join(pos, token_rows, project, bias_full)
    joined3 = joined.reshape(pairs, seq, 3 * width)
    if pieces:
        near_s = from_chip(after(quarter_s, joined), 1)
    context, probs = attend(joined3, captions)
    context_rows = context.reshape(rows, width)
    if pieces:
        far_s = after(far_s, context)
        near_s = [near_s, from_chip(far_s, 1)]
        plane_e = below(*after(plane_e, far_s))
        mine_s = below(*after(near_s, plane_e), far_s, flops=COVER)
        left_s, right_s = left_right(mine_s)
        plane_s = [from_x(left_s), from_y(right_s)]
        context_rows = after(context_rows, mine_s)
        group_e = (mine_e, plane_e, *after([from_core(mine_e), from_core(plane_e)], mine_s))
        sibling_e = from_core(after(expand_weight, joined))
        sibling_o = from_core(after(output_weight, joined))
        expand = halves(shapes[2], expand_weight, sibling_e, group_e, 0)
        output = halves(shapes[1], output_weight, sibling_o, group_e, expand_weight.shape[1] // 2)
    unit1, scale1, normed_low, output = first_norm(pos, context_rows, output, out_bias, token_rows, gain1, shift1)
    active, slope, expand = expand_act(pos, normed_low, expand, hidden_bias)
    if pieces:
        plane_s = beside(*after(plane_s, active))
        other_s = [from_core(mine_s), from_core(plane_s)]
        sibling_s = from_core(after(shrink_weight, active))
        shrink = Weight(
            shapes[3],
            [shrink_weight, sibling_s, mine_s, plane_s, *other_s],
            functools.partial(stacked_copies, high=shrink_weight.shape[0], wide=shrink_weight.shape[1]),
        )
    out_rows, shrink_low, second_grad, sums2, shrink = second_norm(
        pos, captions, active, shrink, down_bias, unit1, gain1, shift1, gain2, shift2, cot_rows, seq
    )
    if pieces:
        mine_s, theirs_s = stacked_grad(pos, active, shrink_low)
        theirs_s = from_core(theirs_s)
        shrink_low = after(shrink_low, mine_s)
    else:
        grad_shrink = weight_grad(active, shrink_low)
    expand_low, sums_hidden = hidden_back(shrink_low, shrink, slope)
    if pieces:
        keep_s, near_s, kept_s, send_s = shrink_sum(mine_s, after(theirs_s, expand_low))
        expand_low = after(expand_low, kept_s)
        near_s, send_s = from_chip(near_s, 1), from_x(send_s)
        mine_e, theirs_e = halves_grad(pos, normed_low, expand_low)
        theirs_e = from_core(theirs_e)
        expand_low = after(expand_low, mine_e)
    first_grad, branch_low, context_grad, sums1 = first_back(
        expand_low, expand, second_grad, unit1, scale1, gain1, output
    )
    if pieces:
        own_s, later_s = pair_sum(kept_s, after(send_s, branch_low))
        mine_o, theirs_o = halves_grad(pos, context_rows, after(branch_low, own_s))
        theirs_o = from_core(theirs_o)
        later_s = from_y(later_s)
        keep_s, far_s = pair_sum(keep_s, after(near_s, mine_o))
        own_x, later_x, out_x, own_y, later_y, out_y = core_split(
            [mine_e, mine_o], after([theirs_e, theirs_o], keep_s)
        )
        far_s = from_chip(far_s, 2)
        out_x, out_y = from_x(out_x), from_y(out_y)
        context_grad = after(context_grad, own_x)
    else:
        grad_expand = weight_grad(normed_low, expand_low)
        grad_output = weight_grad(context_rows, branch_low)
    joined_grad, sums_joined = attend_back(joined3, probs, context_grad.reshape(pairs, seq, width))
    joined_grad_rows = joined_grad.reshape(rows, 3 * width)
    if pieces:
        extra = bundle(sums_joined, sums1, sums2, sums_hidden)
        mine_p, theirs_p = halves_grad(pos, token_rows, joined_grad_rows, extra)
        theirs_p = from_core(theirs_p)
        out_x, out_y = after((out_x, out_y), mine_p)
        own_x, later_x, own_y, later_y = middle_sum([own_x, later_x, out_x, own_y, later_y, out_y])
        later_x, later_y = after((from_y(later_x), from_x(later_y)), far_s)
        keep_eo, near_eo = split_sum([own_x, later_x, own_y, later_y], flops=COVER)
        keep_eo, near_eo = ahead_sum(own_s, after(later_s, keep_eo), keep_eo, near_eo)
        own_x, later_x, out_x, own_y, later_y, out_y = core_split(
            [mine_p], [after(theirs_p, near_eo)], (keep_s, far_s)
        )
        near_eo = from_chip(near_eo, 1)
        out_x, out_y = from_x(out_x), from_y(out_y)
        joined_grad_rows = after(joined_grad_rows, own_x)
    else:
        grad_project = weight_grad(token_rows, joined_grad_rows)

        def owned(grad):
            part = lax.psum_scatter(grad, "fsdp", scatter_dimension=0, tiled=True)
            return lax.psum(part, "dp").astype(F32)

        own_project, own_output, own_expand, own_shrink = (
            owned(grad) for grad in (grad_project, grad_output, grad_expand, grad_shrink)
        )
        small = (sums_joined[0], sums1[0], sums1[1], sums1[2], sums_hidden[0], sums2[0], sums2[1], sums2[2])
        packed_grad = jnp.concatenate([v.reshape(parts, -1) for v in small], axis=1)
        shard = lax.psum(lax.psum_scatter(packed_grad.reshape(-1), "fsdp", scatter_dimension=0, tiled=True), "dp")
    token_grad = token_back(joined_grad_rows, project, first_grad)
    if pieces:
        half_p, half_e, half_o = project_weight.shape[1] // 2, expand_weight.shape[1] // 2, width // 2
        out_x, out_y = after((out_x, out_y), token_grad)
        own_x, later_x, own_y, later_y = middle_sum([own_x, later_x, out_x, own_y, later_y, out_y])
        later_x, later_y = from_y(later_x), from_x(later_y)
        keep_eo, far_eo = pair_sum(keep_eo, after(near_eo, own_x))
        far_eo = from_chip(far_eo, 2)
        later_x, later_y = after((later_x, later_y), keep_eo)
        keep_p, near_p, total_s = split_sum([own_x, later_x, own_y, later_y], more=FIRST // 4)
        near_p = from_chip(near_p, 1)
        total_seo = last_sum((total_s,), (keep_eo, after(far_eo, keep_p)))
        quarters_seo = from_plane(total_seo)
        keep_p, far_p = pair_sum(keep_p, after(near_p, total_seo))
        total_p = last_sum((keep_p, from_chip(far_p, 2)))
        quarters_p = from_plane(total_p)
        own_shrink, own_expand, own_output = place(
            pos,
            [total_seo, *after(quarters_seo, total_p)],
            (("stacked", 2 * width), ("halves", half_e), ("halves", half_o)),
        )
        own_project, *smalls = place(
            pos, [total_p, *after(quarters_p, own_expand)], (("halves", half_p), ("small", 128)), widths
        )
        smalls = [vector.reshape(-1) for vector in smalls]

    if not pieces:
        smalls, at = [], 0
        for size in widths:
            smalls.append(shard[at : at + size])
            at += size
    return (
        out_rows.reshape(pairs, seq, width),
        token_grad.reshape(pairs, seq, width),
        own_project,
        smalls[0],
        own_output,
        smalls[1],
        smalls[2],
        smalls[3],
        own_expand,
        smalls[4],
        own_shrink,
        smalls[5],
        smalls[6],
        smalls[7],
    )


def solution(mesh):
    rows3 = P(("dp", "fsdp"), None, None)
    matrix, vector = P("fsdp", None), P("fsdp")
    pieces = mesh.shape["dp"] == 4 and mesh.shape["fsdp"] == 8
    return jax.shard_map(
        functools.partial(local, pieces),
        mesh=mesh,
        in_specs=(
            rows3, P(("dp", "fsdp")), rows3,
            matrix, vector, matrix, vector, vector, vector,
            matrix, vector, matrix, vector, vector, vector,
        ),
        out_specs=(
            rows3, rows3,
            matrix, vector, matrix, vector, vector, vector,
            matrix, vector, matrix, vector, vector, vector,
        ),
        check_vma=False,
    )
```

```python
import functools

import jax
import jax.numpy as jnp
from jax import lax
from jax.experimental import pallas as pl
from jax.experimental.pallas import tpu as pltpu
from jax.sharding import PartitionSpec as P

HEADS = 12
HEAD_DIM = 64
REGIONS = 36
BF16 = jnp.bfloat16
F32 = jnp.float32

COVER = 100 * 10**9

NN = (((1,), (0,)), ((), ()))
NT = (((1,), (1,)), ((), ()))
TN = (((0,), (0,)), ((), ()))


def dot(left, right, dims=NN):
    return lax.dot_general(left, right, dims, preferred_element_type=F32)


def params(mebibytes):
    return pltpu.CompilerParams(vmem_limit_bytes=mebibytes * 1024 * 1024)


def cost(flops=0):
    return pl.CostEstimate(flops=flops, bytes_accessed=0, transcendentals=0)


def whole(shape, buffers=None):
    mode = None if buffers is None else pl.Buffered(buffers)
    return pl.BlockSpec(shape, lambda *at: (0,) * len(shape), pipeline_mode=mode)


HELD = pl.BlockSpec(memory_space=pltpu.VMEM)


def inside(shape, dtype=BF16):
    return pltpu.VMEM(shape, dtype)


def outside(shape, dtype=BF16):
    return pltpu.HBM(shape, dtype)


def in_vmem(values):
    return pltpu.with_memory_space_constraint(values, pltpu.VMEM)


def in_hbm(values):
    return pltpu.with_memory_space_constraint(values, pltpu.HBM)


def tile_of(size, most):
    return max(t for t in range(128, most + 1, 128) if size % t == 0)


def rows_of(count, most):
    fits = [t for t in range(16, most + 1, 16) if count % t == 0]
    return max(fits) if fits else count


CHIPS = (1, 3, 2)


def halves_copies(refs, into, pos, at, high, wide):
    half = wide // 2
    rows = high // 2
    for side in range(2):
        core = pos[1] if side == 0 else 1 - pos[1]
        shard = pos[0] * 2 + core
        yield refs[side], into.at[pl.ds(pl.multiple_of(shard * high, 16), high), :]
        for flip in range(4):
            buffer, first = refs[2 + side * 2 + (flip > 0)], max(flip - 1, 0) * 3 * rows
            up = pos[2] ^ (flip // 2)
            along = pos[3] ^ (flip % 2)
            for place, chip in enumerate(CHIPS):
                shard = (pos[0] ^ chip) * 2 + core
                to_row = pl.multiple_of(shard * high + up * rows, 16)
                to_column = pl.multiple_of(along * half, 128)
                yield (
                    buffer.at[pl.ds(first + place * rows, rows), pl.ds(at, half)],
                    into.at[pl.ds(to_row, rows), pl.ds(to_column, half)],
                )


def stacked_copies(refs, into, pos, high, wide):
    rows = high // 8
    own = pos[2] * 2 + pos[3]
    for side in range(2):
        core = pos[1] if side == 0 else 1 - pos[1]
        shard = pos[0] * 2 + core
        yield refs[side], into.at[pl.ds(pl.multiple_of(shard * high, 16), high), :]
        for place, chip in enumerate(CHIPS):
            shard = (pos[0] ^ chip) * 2 + core
            for plane in range(2):
                for block in range(2):
                    for part in range(2):
                        flip = block * (2 if part == plane else 1)
                        if plane:
                            flip = (1, 3)[block] if part == 0 else (2, 3)[block]
                        to_row = pl.multiple_of(shard * high + ((own ^ flip) * 2 + part) * rows, 16)
                        yield (
                            refs[2 + side * 2 + plane].at[
                                pl.ds((place * 2 + block) * rows, rows), pl.ds(part * wide, wide)
                            ],
                            into.at[pl.ds(to_row, rows), :],
                        )


def natural_copies(refs, into, pos):
    yield refs[0], into


class Weight:
    def __init__(self, shape, arrays, copies=natural_copies):
        self.shape, self.copies = shape, copies
        self.arrays = [in_vmem(array) for array in arrays]

    def specs(self):
        return [HELD] * len(self.arrays)

    def out(self):
        return inside(self.shape)

    def split(self, refs):
        return refs[: len(self.arrays)], refs[len(self.arrays) : -1], refs[-1]

    def arrive(self, refs, full, pos):
        @pl.when(pl.program_id(0) == 0)
        def _():
            for source, target in self.copies(refs, full, pos):
                target[...] = source[...]


def spread_kernel(pos, own, other, bias, hidden, rows, held):
    part = held.shape[2] * 3 // 4
    for at, chip in enumerate((0, *CHIPS)):
        held[(pos[0] ^ chip) * 2 + pos[1]] = own[at * 16 : at * 16 + 16].astype(F32)
        held[(pos[0] ^ chip) * 2 + 1 - pos[1]] = other[at * 16 : at * 16 + 16].astype(F32)
    bias[...] = jnp.zeros_like(bias)
    width = rows.shape[1]
    for shard in range(8):
        for at in range(2):
            to = (shard * 2 + at) * part
            to += width if to >= width else 0
            bias[0:1, to : to + part] = held[shard, at : at + 1, :part]
        for at in range(4):
            to = (shard * 4 + at) * part
            hidden[0:1, to : to + part] = held[shard, 5 + at : 6 + at, :part]
        to = shard * part
        rows[0:3, to : to + part] = held[shard, 2:5, :part]
        rows[3:6, to : to + part] = held[shard, 9:12, :part]


def spread(pos, shards, width, hidden_width):
    shapes = [(1, 3 * width), (1, hidden_width), (8, width)]
    return pl.pallas_call(
        spread_kernel,
        grid_spec=pltpu.PrefetchScalarGridSpec(
            num_scalar_prefetch=1,
            grid=(1,),
            in_specs=[whole((64, 128))] * 2,
            out_specs=[whole(shape) for shape in shapes],
            scratch_shapes=[pltpu.VMEM((8, 16, 128), F32)],
        ),
        out_shape=[jax.ShapeDtypeStruct(shape, F32) for shape in shapes],
        compiler_params=params(4),
        cost_estimate=cost(COVER),
        name="spread",
    )(pos, *shards)


def bundle_kernel(joined, first, second, hidden, out):
    part = out.shape[2] * 3 // 4
    out[...] = jnp.zeros_like(out)
    for shard in range(8):
        for at in range(2):
            of = (shard * 2 + at) * part
            out[shard, at : at + 1, :part] = joined[0:1, of : of + part]
        for at in range(4):
            of = (shard * 4 + at) * part
            out[shard, 5 + at : 6 + at, :part] = hidden[0:1, of : of + part]
        of = shard * part
        out[shard, 2:5, :part] = first[0:3, of : of + part]
        out[shard, 9:12, :part] = second[0:3, of : of + part]


def bundle(joined, first, second, hidden):
    return pl.pallas_call(
        bundle_kernel,
        out_shape=jax.ShapeDtypeStruct((8, 16, 128), F32),
        compiler_params=params(4),
        cost_estimate=cost(),
        name="bundle",
    )(joined, first, second, hidden)


def step_of(size):
    return pl.ds(pl.multiple_of(pl.program_id(0) * size, 16), size)


def columns_of(size):
    return pl.ds(pl.multiple_of(pl.program_id(0) * size, 128), size)


def join_kernel(pos, tokens, bias, *rest, weight, tile):
    pieces, (out, kept), (full, sem) = rest[: len(weight.arrays)], rest[-4:-2], rest[-2:]
    weight.arrive(pieces, full, pos)
    write = pltpu.make_async_copy(full, kept, sem)

    @pl.when(pl.program_id(0) == 0)
    def _():
        write.start()

    out[...] = (dot(tokens[...], full[:, columns_of(tile)]) + bias[...]).astype(BF16)

    @pl.when(pl.program_id(0) == pl.num_programs(0) - 1)
    def _():
        write.wait()


def join(pos, token_rows, weight, bias):
    rows, width = token_rows.shape
    columns = weight.shape[1]
    tile = tile_of(columns, 768)
    return pl.pallas_call(
        functools.partial(join_kernel, weight=weight, tile=tile),
        grid_spec=pltpu.PrefetchScalarGridSpec(
            num_scalar_prefetch=1,
            grid=(columns // tile,),
            in_specs=[whole((rows, width), 1), pl.BlockSpec((1, tile), lambda i, p: (0, i))] + weight.specs(),
            out_specs=[pl.BlockSpec((rows, tile), lambda i, p: (0, i)), pl.BlockSpec(memory_space=pltpu.HBM)],
            scratch_shapes=[pltpu.VMEM(weight.shape, BF16), pltpu.SemaphoreType.DMA(())],
        ),
        out_shape=[outside((rows, columns)), outside(weight.shape)],
        compiler_params=params(15),
        cost_estimate=cost(),
        name="join",
    )(pos, token_rows, bias, *weight.arrays)


def head_stack(block, low_half, padded):
    rows = block.shape[0]
    filler = jnp.zeros((padded - rows, block.shape[1]), F32)
    first = jnp.where(low_half, block, 0.0)
    second = jnp.where(low_half, 0.0, block)
    return jnp.concatenate([first, filler, second, filler], axis=0).astype(BF16)


def attend_kernel(captions, joined, context, probs):
    seq = joined.shape[1]
    width = context.shape[2]
    padded = probs.shape[3] // 2
    valid = captions[pl.program_id(0)] + 2 + REGIONS
    keep = lax.broadcasted_iota(jnp.int32, (seq, 2 * padded), 0) < valid
    low_half = lax.broadcasted_iota(jnp.int32, (1, 2 * HEAD_DIM), 1) < HEAD_DIM
    places = [pair * 2 * HEAD_DIM for pair in range(HEADS // 2)]
    scores = []
    for at in places:
        query = joined[0, :, at : at + 2 * HEAD_DIM].astype(F32)
        keys = joined[0, :, width + at : width + at + 2 * HEAD_DIM]
        scores.append(dot(keys, head_stack(query, low_half, padded), NT) * HEAD_DIM ** (-0.5))
    probabilities = []
    for score in scores:
        score = jnp.where(keep, score, -1000000000.0)
        grown = jnp.exp(score - jnp.max(score, axis=0, keepdims=True))
        total = jnp.sum(grown, axis=0, keepdims=True)
        probabilities.append((grown * (1.0 / total)).astype(BF16))
    for pair, at in enumerate(places):
        values = joined[0, :, 2 * width + at : 2 * width + at + 2 * HEAD_DIM]
        mixed = dot(probabilities[pair], values, TN)
        probs[0, pair] = probabilities[pair]
        context[0, :, at : at + 2 * HEAD_DIM] = jnp.where(
            low_half, mixed[:seq], mixed[padded : padded + seq]
        ).astype(BF16)


def attend(joined, captions):
    pairs, seq, columns = joined.shape
    width = columns // 3
    padded = (seq + 127) // 128 * 128
    return pl.pallas_call(
        attend_kernel,
        grid_spec=pltpu.PrefetchScalarGridSpec(
            num_scalar_prefetch=1,
            grid=(pairs,),
            in_specs=[pl.BlockSpec((1, seq, columns), lambda i, c: (i, 0, 0))],
            out_specs=[
                pl.BlockSpec((1, seq, width), lambda i, c: (i, 0, 0)),
                pl.BlockSpec((1, HEADS // 2, seq, 2 * padded), lambda i, c: (i, 0, 0, 0)),
            ],
        ),
        out_shape=[
            inside((pairs, seq, width)),
            outside((pairs, HEADS // 2, seq, 2 * padded)),
        ],
        compiler_params=params(8),
        cost_estimate=cost(),
        name="attend",
    )(captions, in_hbm(joined))


def attend_back_kernel(joined, probs, grads, out, sums):
    seq = joined.shape[1]
    width = grads.shape[2]
    padded = probs.shape[3] // 2
    low_half = lax.broadcasted_iota(jnp.int32, (1, 2 * HEAD_DIM), 1) < HEAD_DIM

    @pl.when(pl.program_id(0) == 0)
    def _():
        sums[...] = jnp.zeros_like(sums)

    places = [pair * 2 * HEAD_DIM for pair in range(HEADS // 2)]
    prob_grads, grad_stacks = [], []
    for at in places:
        values = joined[0, :, 2 * width + at : 2 * width + at + 2 * HEAD_DIM]
        grad_stacks.append(head_stack(grads[0, :, at : at + 2 * HEAD_DIM].astype(F32), low_half, padded))
        prob_grads.append(dot(values, grad_stacks[-1], NT))
    score_grads = []
    for pair, prob_grad in enumerate(prob_grads):
        prob = probs[0, pair].astype(F32)
        row_dot = jnp.sum(prob * prob_grad, axis=0, keepdims=True)
        score_grads.append((prob * (prob_grad - row_dot) * HEAD_DIM ** (-0.5)).astype(BF16))
    results = []
    for pair, at in enumerate(places):
        query = joined[0, :, at : at + 2 * HEAD_DIM].astype(F32)
        keys = joined[0, :, width + at : width + at + 2 * HEAD_DIM]
        mixed = dot(score_grads[pair], keys, TN)
        query_grad = jnp.where(low_half, mixed[:seq], mixed[padded : padded + seq])
        keys_grad = dot(score_grads[pair], head_stack(query, low_half, padded))
        results.append((query_grad, keys_grad, dot(probs[0, pair], grad_stacks[pair])))
    for at, blocks in zip(places, results):
        for part, block in enumerate(blocks):
            out[0, :, part * width + at : part * width + at + 2 * HEAD_DIM] = block.astype(BF16)
            if part != 1:
                to = part // 2 * width + at
                sums[:, to : to + 2 * HEAD_DIM] += jnp.sum(block, axis=0, keepdims=True)


def attend_back(joined, probs, grads):
    pairs, seq, columns = joined.shape
    width = columns // 3
    padded = probs.shape[3] // 2
    return pl.pallas_call(
        attend_back_kernel,
        grid=(pairs,),
        in_specs=[
            pl.BlockSpec((1, seq, columns), lambda i: (i, 0, 0)),
            pl.BlockSpec((1, HEADS // 2, seq, 2 * padded), lambda i: (i, 0, 0, 0)),
            pl.BlockSpec((1, seq, width), lambda i: (i, 0, 0)),
        ],
        out_specs=[
            pl.BlockSpec((1, seq, columns), lambda i: (i, 0, 0)),
            pl.BlockSpec((1, 2 * width), lambda i: (0, 0)),
        ],
        out_shape=[
            inside((pairs, seq, columns)),
            jax.ShapeDtypeStruct((1, 2 * width), F32),
        ],
        compiler_params=params(10),
        cost_estimate=cost(),
        name="attend_back",
    )(in_hbm(joined), in_hbm(probs), in_vmem(grads))


def norm_parts(values):
    centred = values - jnp.mean(values, axis=-1, keepdims=True)
    spread = jnp.mean(centred * centred, axis=-1, keepdims=True)
    scale = lax.rsqrt(spread + 1e-05)
    return centred * scale, scale


def norm_back(upstream, unit, scale, gain):
    scaled = upstream * gain
    return scale * (
        scaled
        - jnp.mean(scaled, axis=-1, keepdims=True)
        - unit * jnp.mean(scaled * unit, axis=-1, keepdims=True)
    )


def add_sums(sums, rows):
    for at, values in enumerate(rows):
        sums[at : at + 1, :] += jnp.sum(values, axis=0, keepdims=True)


def chunked(count, load, use):
    ready = load(0)
    for at in range(count):
        following = load(at + 1) if at + 1 < count else None
        use(at, ready)
        ready = following


def chunk_slices(rows, most):
    tile = rows_of(rows, most)
    return [slice(at, at + tile) for at in range(0, rows, tile)]


def first_kernel(pos, context, bias, tokens, gain, shift, *rest, weight):
    pieces, (unit, scale, normed_low), full = weight.split(rest)
    weight.arrive(pieces, full, pos)
    chunks = chunk_slices(tokens.shape[0], 416)

    def normalise(at, branch):
        rows = chunks[at]
        unit_rows, scale_rows = norm_parts(tokens[rows, :].astype(F32) + (branch + bias[...]))
        unit[rows, :] = unit_rows
        scale[rows, :] = scale_rows
        normed_low[rows, :] = (unit_rows * gain[...] + shift[...]).astype(BF16)

    chunked(len(chunks), lambda at: dot(context[chunks[at], :], full[...]), normalise)


def first_norm(pos, context, weight, bias, token_rows, gain, shift):
    rows, width = token_rows.shape
    row = whole((1, width))
    return pl.pallas_call(
        functools.partial(first_kernel, weight=weight),
        grid_spec=pltpu.PrefetchScalarGridSpec(
            num_scalar_prefetch=1,
            grid=(1,),
            in_specs=[HELD, row, HELD, row, row] + weight.specs(),
            out_specs=[HELD] * 4,
        ),
        out_shape=[inside((rows, width), F32), inside((rows, 1), F32), inside((rows, width)), weight.out()],
        compiler_params=params(10),
        cost_estimate=cost(),
        name="first_norm",
    )(pos, in_vmem(context), bias, in_vmem(token_rows), gain, shift, *weight.arrays)


def expand_kernel(pos, normed_low, bias, *rest, weight, tile):
    pieces, (active, slope), full = weight.split(rest)
    weight.arrive(pieces, full, pos)
    at = columns_of(tile)
    expand = dot(normed_low[...], full[:, at]) + bias[...]
    half = 0.5 * (1.0 + lax.erf(expand * 0.7071067811865476))
    active[:, at] = (expand * half).astype(BF16)
    slope[:, at] = (half + expand * jnp.exp(-0.5 * expand * expand) * 0.3989422804014327).astype(BF16)


def expand_act(pos, normed_low, weight, bias):
    rows, width = normed_low.shape
    columns = weight.shape[1]
    tile = tile_of(columns, 768)
    return pl.pallas_call(
        functools.partial(expand_kernel, weight=weight, tile=tile),
        grid_spec=pltpu.PrefetchScalarGridSpec(
            num_scalar_prefetch=1,
            grid=(columns // tile,),
            in_specs=[HELD, pl.BlockSpec((1, tile), lambda i, p: (0, i))] + weight.specs(),
            out_specs=[HELD] * 3,
        ),
        out_shape=[inside((rows, columns))] * 2 + [weight.out()],
        compiler_params=params(12),
        cost_estimate=cost(),
        name="expand_act",
    )(pos, in_vmem(normed_low), bias, *weight.arrays)


def second_kernel(pos, captions, active, bias, unit, gain, shift, gain2, shift2, cotangent, *rest, weight, seq):
    pieces, (out, low, grad, sums), full, (held, sems) = *weight.split(rest[:-2]), rest[-2:]
    weight.arrive(pieces, full, pos)
    sums[...] = jnp.zeros_like(sums)
    tile = rows_of(held.shape[0], 4 * seq)
    count = held.shape[0] // tile

    def write(at):
        rows = pl.ds(pl.multiple_of(at * tile, 16), tile)
        return pltpu.make_async_copy(held.at[rows, :], out.at[rows, :], sems.at[at])

    def chunk(at, carry):
        rows = pl.ds(pl.multiple_of(at * tile, 16), tile)
        normed = unit[rows, :] * gain[...] + shift[...]
        unit2, scale2 = norm_parts(normed + (dot(active[rows, :], full[...]) + bias[...]))
        held[rows, :] = (unit2 * gain2[...] + shift2[...]).astype(BF16)
        write(at).start()
        row = lax.broadcasted_iota(jnp.int32, (tile, 1), 0)
        live = jnp.zeros(row.shape, jnp.bool_)
        for pair in range(tile // seq):
            valid = captions[at * (tile // seq) + pair] + 2 + REGIONS
            live = live | ((row >= pair * seq) & (row < pair * seq + valid))
        upstream = jnp.where(live, cotangent[rows, :].astype(F32), 0.0)
        second = norm_back(upstream, unit2, scale2, gain2[...])
        grad[rows, :] = second
        low[rows, :] = second.astype(BF16)
        add_sums(sums, (second, upstream * unit2, upstream))
        return carry

    lax.fori_loop(0, count, chunk, 0)
    for at in range(count):
        write(at).wait()


def second_norm(pos, captions, active, weight, bias, unit, gain, shift, gain2, shift2, cotangent, seq):
    rows, width = unit.shape
    row = whole((1, width))
    return pl.pallas_call(
        functools.partial(second_kernel, weight=weight, seq=seq),
        grid_spec=pltpu.PrefetchScalarGridSpec(
            num_scalar_prefetch=2,
            grid=(1,),
            in_specs=[HELD, row, HELD, row, row, row, row, HELD] + weight.specs(),
            out_specs=[pl.BlockSpec(memory_space=pltpu.HBM), HELD, HELD, whole((8, width)), HELD],
            scratch_shapes=[pltpu.VMEM((rows, width), BF16), pltpu.SemaphoreType.DMA((rows // 16,))],
        ),
        out_shape=[
            outside((rows, width)),
            inside((rows, width)),
            inside((rows, width), F32),
            jax.ShapeDtypeStruct((8, width), F32),
            weight.out(),
        ],
        compiler_params=params(12),
        cost_estimate=cost(),
        name="second_norm",
    )(pos, captions, in_vmem(active), bias, in_vmem(unit), gain, shift, gain2, shift2, in_vmem(cotangent), *weight.arrays)


def hidden_back_kernel(low, weight, slope, out, sums):
    at = columns_of(sums.shape[1])
    grad = dot(low[...], weight[at, :], NT) * slope[:, at].astype(F32)
    out[:, at] = grad.astype(BF16)
    sums[...] = jnp.sum(grad, axis=0, keepdims=True)


def hidden_back(low, weight, slope):
    rows, width = low.shape
    hidden = weight.shape[0]
    tile = tile_of(hidden, 768)
    return pl.pallas_call(
        hidden_back_kernel,
        grid=(hidden // tile,),
        in_specs=[HELD] * 3,
        out_specs=[HELD, pl.BlockSpec((1, tile), lambda i: (0, i))],
        out_shape=[inside((rows, hidden)), jax.ShapeDtypeStruct((1, hidden), F32)],
        compiler_params=params(10),
        cost_estimate=cost(),
        name="hidden_back",
    )(in_vmem(low), in_vmem(weight), in_vmem(slope))


def first_back_kernel(hidden, weight, second, unit, scale, gain, out_weight, grad, low, context_grad, sums):
    sums[...] = jnp.zeros_like(sums)
    chunks = chunk_slices(grad.shape[0], 416)
    waiting = []

    def pass_on():
        rows, first_low = waiting.pop()
        context_grad[rows, :] = dot(first_low, out_weight[...], NT).astype(BF16)

    def normalise(at, product):
        rows = chunks[at]
        unit_rows = unit[rows, :]
        normed_grad = product + second[rows, :]
        first = norm_back(normed_grad, unit_rows, scale[rows, :], gain[...])
        grad[rows, :] = first
        first_low = first.astype(BF16)
        low[rows, :] = first_low
        add_sums(sums, (first, normed_grad * unit_rows, normed_grad))
        if waiting:
            pass_on()
        waiting.append((rows, first_low))

    chunked(len(chunks), lambda at: dot(hidden[chunks[at], :], weight[...], NT), normalise)
    pass_on()


def first_back(hidden, weight, second, unit, scale, gain, out_weight):
    rows, width = second.shape
    return pl.pallas_call(
        first_back_kernel,
        grid=(1,),
        in_specs=[HELD] * 5 + [whole((1, width)), HELD],
        out_specs=[HELD, HELD, HELD, whole((8, width))],
        out_shape=[
            inside((rows, width), F32),
            inside((rows, width)),
            inside((rows, width)),
            jax.ShapeDtypeStruct((8, width), F32),
        ],
        compiler_params=params(13),
        cost_estimate=cost(COVER),
        name="first_back",
    )(in_vmem(hidden), in_vmem(weight), in_vmem(second), in_vmem(unit), in_vmem(scale), gain, in_vmem(out_weight))


def token_back_kernel(grads, weight, first, out):
    at = step_of(out.shape[0])
    out[...] = dot(grads[at, :], weight[...], NT) + first[at, :]


def token_back(grads, weight, first):
    rows, width = first.shape
    tile = rows_of(rows, 416)
    return pl.pallas_call(
        token_back_kernel,
        grid=(rows // tile,),
        in_specs=[HELD] * 3,
        out_specs=pl.BlockSpec((tile, width), lambda i: (i, 0)),
        out_shape=outside((rows, width), F32),
        compiler_params=params(9),
        cost_estimate=cost(),
        name="token_back",
    )(in_vmem(grads), in_vmem(weight), in_vmem(first))


def weight_grad_kernel(left, right, out):
    out[...] = dot(left[...], right[...], TN).astype(BF16)


def weight_grad(left, right):
    rows, height = left.shape
    columns = right.shape[1]
    tile = tile_of(columns, 768)
    high = tile_of(height, 768)
    return pl.pallas_call(
        weight_grad_kernel,
        grid=(height // high, columns // tile),
        in_specs=[
            pl.BlockSpec((rows, high), lambda i, j: (0, i)),
            pl.BlockSpec((rows, tile), lambda i, j: (0, j)),
        ],
        out_specs=pl.BlockSpec((high, tile), lambda i, j: (i, j)),
        out_shape=outside((height, columns)),
        compiler_params=params(24),
        cost_estimate=cost(),
        name="weight_grad",
    )(left, right)


def regroup_kernel(values, out):
    part = values.shape[1] // 8
    blocks = [values[:, shard * part : (shard + 1) * part] for shard in (0, 2, 4, 6, 1, 3, 5, 7)]
    out[...] = jnp.concatenate(blocks, axis=1)


def regroup(values):
    return held_call(regroup_kernel, "regroup", [values.shape], [values])[0]


def by_core(pos, mine, theirs, store):
    store(mine, pos[1])
    store(theirs, 1 - pos[1])


def halves_grad_kernel(pos, left, right, *rest):
    extra, (mine, theirs) = (rest[0] if len(rest) == 3 else None), rest[-2:]
    along, half = pl.program_id(0), right.shape[1] // 2
    columns, high, rows = right[:, columns_of(half)], left.shape[1] // 2, mine.shape[3]

    def store(out, core):
        grads = dot(left[:, pl.ds(pl.multiple_of(core * high, 128), high)], columns, TN)
        for chip in range(4):
            for up in range(2):
                at = (chip * 2 + up) * rows
                to = (chip ^ pos[0], up ^ pos[2], along ^ pos[3])
                out[(*to, slice(None), slice(0, half))] = grads[at : at + rows].astype(BF16)
                if extra is not None:
                    out[(*to, slice(None), slice(half, None))] = jnp.zeros((rows, 128), BF16)
                    out[(*to, slice(0, 16), slice(half, None))] = extra[chip * 2 + core].astype(BF16)

    by_core(pos, mine, theirs, store)


def stacked_grad_kernel(pos, left, right, mine, theirs):
    high, rows, wide = left.shape[1] // 8, mine.shape[3], right.shape[1]

    def store(out, core):
        for part in range(2):
            chip = pl.program_id(0) * 2 + part
            columns = pl.ds(pl.multiple_of((chip * 2 + core) * high, 128), high)
            grads = dot(left[:, columns], right[...], TN)
            for quarter in range(4):
                for side in range(2):
                    at = (quarter * 2 + side) * rows
                    to = (chip ^ pos[0], (quarter // 2) ^ pos[2], (quarter % 2) ^ pos[3])
                    block = grads[at : at + rows].astype(BF16)
                    out[(*to, slice(None), slice(side * wide, (side + 1) * wide))] = block

    by_core(pos, mine, theirs, store)


def pieces_grad(kernel, name, pos, left, right, shape, extra=()):
    out = inside((4, 2, 2) + shape)
    return pl.pallas_call(
        kernel,
        grid_spec=pltpu.PrefetchScalarGridSpec(
            num_scalar_prefetch=1,
            grid=(2,),
            in_specs=[HELD, HELD] + [whole(array.shape) for array in extra],
            out_specs=[HELD, HELD],
        ),
        out_shape=[out, out],
        compiler_params=params(13),
        cost_estimate=cost(),
        name=name,
    )(pos, in_vmem(left), in_vmem(right), *extra)


def halves_grad(pos, left, right, extra=None):
    shape = (left.shape[1] // 16, right.shape[1] // 2 + (0 if extra is None else 128))
    more = () if extra is None else (extra,)
    return pieces_grad(halves_grad_kernel, "halves_grad", pos, left, right, shape, more)


def stacked_grad(pos, left, right):
    shape = (left.shape[1] // 64, 2 * right.shape[1])
    return pieces_grad(stacked_grad_kernel, "stacked_grad", pos, left, right, shape)


def held_call(kernel, name, outs, values, flops=0):
    return pl.pallas_call(
        kernel,
        in_specs=[HELD] * len(values),
        out_specs=[HELD] * len(outs),
        out_shape=[inside(out) for out in outs],
        compiler_params=params(4),
        cost_estimate=cost(flops),
        name=name,
    )(*map(in_vmem, values))


def add(*terms):
    total = terms[0].astype(F32)
    for term in terms[1:]:
        total += term.astype(F32)
    return total


FIRST = 1024


def shrink_sum_kernel(mine, theirs, keep, near, kept, send):
    for chip in range(4):
        for flip in range(4):
            pick = (chip, flip // 2, flip % 2)
            total = add(mine[pick], theirs[pick]).astype(BF16)
            (keep, near)[chip % 2][chip // 2, flip] = total[:, :FIRST]
            (kept, send)[flip % 2][flip // 2, chip] = total[:, FIRST:]


def shrink_sum(mine, theirs):
    rows, wide = mine.shape[3:]
    outs = [(2, 4, rows, FIRST)] * 2 + [(2, 4, rows, wide - FIRST)] * 2
    return held_call(shrink_sum_kernel, "shrink_sum", outs, [mine, theirs])


def core_split_kernel(*refs, count):
    outs = refs[-6:]
    for half in range(2):
        own, later, send = outs[3 * half : 3 * half + 3]
        first = 1 + half
        for flip, out in ((0, own), (3 - first, later), (first, send.at[0]), (3, send.at[1])):
            at = 0
            for mine, theirs in zip(refs[:count], refs[count : 2 * count]):
                wide = mine.shape[4]
                for chip in range(2):
                    pick = (2 * half + chip, flip // 2, flip % 2)
                    out[chip, :, at : at + wide] = add(mine[pick], theirs[pick]).astype(BF16)
                at += wide
            if len(refs) > 2 * count + 6:
                near, far = refs[2 * count : 2 * count + 2]
                wide = near.shape[2] // 4
                for chip in range(2):
                    columns = slice((2 * half + chip) * wide, (2 * half + chip + 1) * wide)
                    out[chip, :, at:] = add(near[flip, :, columns], far[flip, :, columns]).astype(BF16)


def core_split(mine, theirs, more=()):
    shape = (2, mine[0].shape[3], sum(m.shape[4] for m in mine) + sum(m.shape[2] // 8 for m in more))
    kernel = functools.partial(core_split_kernel, count=len(mine))
    return held_call(kernel, "core_split", [shape, shape, (2,) + shape] * 2, [*mine, *theirs, *more])


def middle_sum_kernel(*refs):
    for half in range(2):
        own, later, received = refs[3 * half : 3 * half + 3]
        refs[6 + 2 * half][...] = add(own[...], received[0]).astype(BF16)
        refs[7 + 2 * half][...] = add(later[...], received[1]).astype(BF16)


def middle_sum(parts):
    return held_call(middle_sum_kernel, "middle_sum", [parts[0].shape] * 4, parts)


def split_sum_kernel(own, received, own_too, received_too, keep, near, *rest):
    for chip in range(4):
        one, two = (own, received) if chip < 2 else (own_too, received_too)
        total = add(one[chip % 2], two[chip % 2]).astype(BF16)
        wide = keep.shape[2]
        (keep, near)[chip % 2][chip // 2] = total[:, :wide]
        if rest:
            part = total.shape[1] - wide
            rest[0][:, chip * part : (chip + 1) * part] = total[:, wide:]


def split_sum(parts, more=0, flops=0):
    _, rows, wide = parts[0].shape
    outs = [(2, rows, wide - more)] * 2 + ([(rows, 4 * more)] if more else [])
    return held_call(split_sum_kernel, "split_sum", outs, parts, flops)


def ahead_sum_kernel(one, two, keep, near, keep_out, near_out):
    wide = one.shape[2]
    for chip in range(4):
        source, out = (keep, keep_out) if chip % 2 == 0 else (near, near_out)
        out[chip // 2, :, :wide] = add(one[chip], two[chip]).astype(BF16)
        out[chip // 2, :, wide:] = source[chip // 2]


def ahead_sum(one, two, keep, near):
    shape = keep.shape[:2] + (keep.shape[2] + one.shape[2],)
    return held_call(ahead_sum_kernel, "ahead_sum", [shape] * 2, [one, two, keep, near])


def pair_sum_kernel(keep, received, one, two):
    one[...] = add(keep[0], received[0]).astype(BF16)
    two[...] = add(keep[1], received[1]).astype(BF16)


def pair_sum(keep, received, flops=0):
    return held_call(pair_sum_kernel, "pair_sum", [keep.shape[1:]] * 2, [keep, received], flops)


def last_sum_kernel(*refs, counts):
    out, at = refs[-1], 0
    for count in counts:
        terms, refs = refs[:count], refs[count:]
        wide = terms[0].shape[1]
        out[:, at : at + wide] = add(*(term[...] for term in terms)).astype(BF16)
        at += wide


def last_sum(*groups):
    kernel = functools.partial(last_sum_kernel, counts=[len(group) for group in groups])
    shape = (groups[0][0].shape[0], sum(group[0].shape[1] for group in groups))
    return held_call(kernel, "last_sum", [shape], [part for group in groups for part in group])[0]


def place_kernel(pos, *refs, layout):
    parts, outs = refs[:4], refs[4:]
    rows = parts[0].shape[0]
    for flip, part in enumerate(parts):
        up, along = pos[2] ^ (flip // 2), pos[3] ^ (flip % 2)
        at = 0
        for (kind, wide), out in zip(layout, outs):
            if kind == "halves":
                to_row = pl.multiple_of(up * rows, 16)
                to_column = pl.multiple_of(along * wide, 128)
                out[pl.ds(to_row, rows), pl.ds(to_column, wide)] = part[:, at : at + wide].astype(F32)
            elif kind == "stacked":
                for side in range(2):
                    to_row = pl.multiple_of(((up * 2 + along) * 2 + side) * rows, 16)
                    from_column = at + side * (wide // 2)
                    out[pl.ds(to_row, rows), :] = part[:, from_column : from_column + wide // 2].astype(F32)
            else:

                @pl.when((up == 0) & (along == 0))
                def _(part=part, at=at):
                    row = 0
                    for vector in outs[len(layout) - 1 :]:
                        for to in range(0, vector.shape[1], 96):
                            vector[:, to : to + 96] = part[row : row + 1, at : at + 96].astype(F32)
                            row += 1

            at += wide


def place(pos, parts, layout, sizes=()):
    rows = parts[0].shape[0]
    shapes = {
        "halves": lambda wide: (2 * rows, 2 * wide),
        "stacked": lambda wide: (8 * rows, wide // 2),
    }
    outs = [jax.ShapeDtypeStruct(shapes[kind](wide), F32) for kind, wide in layout if kind != "small"]
    outs += [jax.ShapeDtypeStruct((1, size), F32) for size in sizes]
    return pl.pallas_call(
        functools.partial(place_kernel, layout=layout),
        grid_spec=pltpu.PrefetchScalarGridSpec(
            num_scalar_prefetch=1,
            grid=(1,),
            in_specs=[HELD] * 4,
            out_specs=[whole(out.shape, 1) for out in outs],
        ),
        out_shape=outs,
        compiler_params=params(10),
        cost_estimate=cost(),
        name="place",
    )(pos, *map(in_vmem, parts))


def from_core(values):
    return lax.ppermute(values, "fsdp", [(i, i ^ 1) for i in range(8)])


def from_plane(values):
    parts = values if isinstance(values, (list, tuple)) else [values] * 3
    return [
        lax.ppermute(part, "dp", [(i, i ^ flip) for i in range(4)]) for flip, part in zip((1, 2, 3), parts)
    ]


def from_x(values):
    return lax.ppermute(values, "dp", [(i, i ^ 1) for i in range(4)])


def from_y(values):
    return lax.ppermute(values, "dp", [(i, i ^ 2) for i in range(4)])


def from_chips(values):
    return [from_chip(values, flip) for flip in CHIPS]


def from_chip(values, flip):
    return lax.ppermute(values, "fsdp", [(i, i ^ (2 * flip)) for i in range(8)])


def below_kernel(*refs):
    at = 0
    for ref in refs[:-1]:
        rows, wide = ref.shape[0], refs[-1].shape[1]
        refs[-1][at : at + rows] = ref[:, :wide]
        at += rows


def below(*parts, wide=None, flops=0):
    rows = sum(part.shape[0] for part in parts)
    return pl.pallas_call(
        below_kernel,
        in_specs=[HELD] * len(parts),
        out_specs=HELD,
        out_shape=inside((rows, wide or parts[0].shape[1])),
        compiler_params=params(4),
        cost_estimate=cost(flops),
        name="below",
    )(*map(in_vmem, parts))


def pick_kernel(pos, shard, out):
    rows, wide = out.shape[0] // 2, shard.shape[1]
    own = pos[2] * 2 + pos[3]
    for block, part, flip in ((0, 0, 0), (0, 1, 0), (1, 0, 2), (1, 1, 1)):
        from_row = pl.multiple_of(((own ^ flip) * 2 + part) * rows, 16)
        out[block * rows : (block + 1) * rows, part * wide : (part + 1) * wide] = shard[pl.ds(from_row, rows), :]


def pick(pos, shard):
    return pl.pallas_call(
        pick_kernel,
        grid_spec=pltpu.PrefetchScalarGridSpec(
            num_scalar_prefetch=1, grid=(1,), in_specs=[whole(shard.shape, 1)], out_specs=HELD
        ),
        out_shape=inside((shard.shape[0] // 4, 2 * shard.shape[1])),
        compiler_params=params(4),
        cost_estimate=cost(),
        name="pick",
    )(pos, shard)


def left_right_kernel(whole_ref, left, right):
    half = left.shape[1]
    left[...] = whole_ref[:, :half]
    right[...] = whole_ref[:, half:]


def left_right(values):
    rows, wide = values.shape
    return held_call(left_right_kernel, "left_right", [(rows, wide // 2)] * 2, [values])


def beside_kernel(left, right, out):
    half = left.shape[1]
    out[:, :half] = left[...]
    out[:, half:] = right[...]


def beside(left, right):
    rows, wide = left.shape
    return held_call(beside_kernel, "beside", [(rows, 2 * wide)], [left, right])[0]


def after(values, *others):
    return lax.optimization_barrier((values, others))[0]


def half_of(pos, shard):
    rows, wide = shard.shape[0] // 2, shard.shape[1] // 2
    return lax.dynamic_slice(shard, (pos[2] * rows, pos[3] * wide), (rows, wide))


def both_cores(pieces):
    return [*pieces, *(from_core(piece) for piece in pieces)]


def gather(values):
    return lax.all_gather(values, "fsdp", axis=0, tiled=True)


def local(
    pieces,
    tokens,
    captions,
    cotangent,
    project_weight,
    project_bias,
    output_weight,
    output_bias,
    first_gain,
    first_shift,
    expand_weight,
    expand_bias,
    shrink_weight,
    shrink_bias,
    second_gain,
    second_shift,
):
    pairs, seq, width = tokens.shape
    rows = pairs * seq
    parts = lax.axis_size("fsdp")
    token_rows = tokens.reshape(rows, width)
    cot_rows = cotangent.reshape(rows, width)

    vectors = (project_bias, output_bias, first_gain, first_shift, expand_bias, shrink_bias, second_gain, second_shift)
    widths = [vector.shape[0] for vector in vectors]
    replica, part = lax.axis_index("dp"), lax.axis_index("fsdp")
    pos = jnp.stack([part // 2, part % 2, replica // 2, replica % 2]).astype(jnp.int32)
    shapes = [(parts * shard.shape[0], shard.shape[1]) for shard in (project_weight, output_weight, expand_weight, shrink_weight)]
    if pieces:
        chips_p = from_chips(half_of(pos, project_weight))
        sibling_p = from_core(project_weight)
        held = jnp.concatenate([vector.reshape(-1, 96) for vector in vectors], axis=0)
        held = jnp.pad(held, ((0, 4), (0, 32)))
        quarter_e = [half_of(pos, expand_weight), half_of(pos, output_weight), jnp.pad(held, ((0, 32), (0, 0)))]
        quarter_e = jnp.concatenate(quarter_e, axis=1)
        wide_e = quarter_e.shape[1] - 128
        chips_p = after(chips_p, sibling_p, quarter_e)
        mine_p = below(*chips_p)
        quarter_e = after(quarter_e, *chips_p)
        far_e = from_chip(quarter_e, 2)
        near_e = [from_chip(quarter_e, 1), from_chip(far_e, 1)]
        plane_p = from_plane(mine_p)
        plane_p = below(*plane_p, flops=COVER)
        near_e = after(near_e, plane_p)
        other_p = [from_core(mine_p), from_core(plane_p)]

        def halves(shape, shard, sibling, group, at):
            copies = functools.partial(halves_copies, at=at, high=shard.shape[0], wide=shard.shape[1])
            return Weight(shape, [shard, sibling, *group], copies)

        project = halves(shapes[0], project_weight, sibling_p, (mine_p, plane_p, *other_p), 0)
        quarter_s = pick(pos, after(shrink_weight, quarter_e))
        quarter_s = after(quarter_s, plane_p)
        far_s = from_chip(quarter_s, 2)
        mine_e = below(*near_e, far_e, wide=wide_e)
        plane_e = from_plane(mine_e)
        held = jnp.concatenate([held, *(chip[:16, wide_e:] for chip in (*near_e, far_e))], axis=0)
        token_group = regroup(after(token_rows, plane_p))
        held = after(held, mine_e, token_group)
        bias_full, hidden_bias, rows6 = spread(pos, [held, from_core(held)], width, expand_weight.shape[1])
        out_bias, gain1, shift1, down_bias, gain2, shift2 = (rows6[at : at + 1] for at in range(6))
    else:
        project, output, expand, shrink = (
            Weight(shape, [gather(shard)])
            for shape, shard in zip(shapes, (project_weight, output_weight, expand_weight, shrink_weight))
        )
        packed = gather(jnp.concatenate(vectors)[None, :])
        full, at = [], 0
        for size in widths:
            full.append(packed[:, at : at + size].reshape(1, parts * size).astype(F32))
            at += size
        bias_row, out_bias, gain1, shift1, hidden_bias, down_bias, gain2, shift2 = full
        bias_full = jnp.concatenate([bias_row[:, :width], jnp.zeros((1, width), F32), bias_row[:, width:]], axis=1)

    joined, project = join(pos, token_rows, project, bias_full)
    joined3 = joined.reshape(pairs, seq, 3 * width)
    if pieces:
        near_s = from_chip(after(quarter_s, joined), 1)
    context, probs = attend(joined3, captions)
    context_rows = context.reshape(rows, width)
    if pieces:
        far_s = after(far_s, context)
        near_s = [near_s, from_chip(far_s, 1)]
        context_group = regroup(context_rows)
        plane_e = below(*after(plane_e, far_s, context_group))
        mine_s = below(*after(near_s, plane_e), far_s, flops=COVER)
        left_s, right_s = left_right(mine_s)
        plane_s = [from_x(left_s), from_y(right_s)]
        context_rows = after(context_rows, mine_s)
        group_e = (mine_e, plane_e, *after([from_core(mine_e), from_core(plane_e)], mine_s))
        sibling_e = from_core(after(expand_weight, joined))
        sibling_o = from_core(after(output_weight, joined))
        expand = halves(shapes[2], expand_weight, sibling_e, group_e, 0)
        output = halves(shapes[1], output_weight, sibling_o, group_e, expand_weight.shape[1] // 2)
    unit1, scale1, normed_low, output = first_norm(pos, context_rows, output, out_bias, token_rows, gain1, shift1)
    active, slope, expand = expand_act(pos, normed_low, expand, hidden_bias)
    if pieces:
        plane_s = beside(*after(plane_s, active))
        normed_group = regroup(after(normed_low, plane_s))
        other_s = [from_core(mine_s), from_core(plane_s)]
        sibling_s = from_core(after(shrink_weight, active))
        shrink = Weight(
            shapes[3],
            [shrink_weight, sibling_s, mine_s, plane_s, *after(other_s, normed_group)],
            functools.partial(stacked_copies, high=shrink_weight.shape[0], wide=shrink_weight.shape[1]),
        )
    out_rows, shrink_low, second_grad, sums2, shrink = second_norm(
        pos, captions, active, shrink, down_bias, unit1, gain1, shift1, gain2, shift2, cot_rows, seq
    )
    if pieces:
        mine_s, theirs_s = stacked_grad(pos, active, shrink_low)
        theirs_s = from_core(theirs_s)
        shrink_low = after(shrink_low, mine_s)
    else:
        grad_shrink = weight_grad(active, shrink_low)
    expand_low, sums_hidden = hidden_back(shrink_low, shrink, slope)
    if pieces:
        keep_s, near_s, kept_s, send_s = shrink_sum(mine_s, after(theirs_s, expand_low))
        expand_low = after(expand_low, kept_s)
        near_s, send_s = from_chip(near_s, 1), from_x(send_s)
        mine_e, theirs_e = halves_grad(pos, normed_group, expand_low)
        theirs_e = from_core(theirs_e)
        expand_low = after(expand_low, mine_e)
    first_grad, branch_low, context_grad, sums1 = first_back(
        expand_low, expand, second_grad, unit1, scale1, gain1, output
    )
    if pieces:
        own_s, later_s = pair_sum(kept_s, after(send_s, branch_low))
        mine_o, theirs_o = halves_grad(pos, context_group, after(branch_low, own_s))
        theirs_o = from_core(theirs_o)
        later_s = from_y(later_s)
        keep_s, far_s = pair_sum(keep_s, after(near_s, mine_o))
        own_x, later_x, out_x, own_y, later_y, out_y = core_split(
            [mine_e, mine_o], after([theirs_e, theirs_o], keep_s)
        )
        far_s = from_chip(far_s, 2)
        out_x, out_y = from_x(out_x), from_y(out_y)
        context_grad = after(context_grad, own_x)
    else:
        grad_expand = weight_grad(normed_low, expand_low)
        grad_output = weight_grad(context_rows, branch_low)
    joined_grad, sums_joined = attend_back(joined3, probs, context_grad.reshape(pairs, seq, width))
    joined_grad_rows = joined_grad.reshape(rows, 3 * width)
    if pieces:
        extra = bundle(sums_joined, sums1, sums2, sums_hidden)
        mine_p, theirs_p = halves_grad(pos, token_group, joined_grad_rows, extra)
        theirs_p = from_core(theirs_p)
        out_x, out_y = after((out_x, out_y), mine_p)
        own_x, later_x, own_y, later_y = middle_sum([own_x, later_x, out_x, own_y, later_y, out_y])
        later_x, later_y = after((from_y(later_x), from_x(later_y)), far_s)
        keep_eo, near_eo = split_sum([own_x, later_x, own_y, later_y], flops=COVER)
        keep_eo, near_eo = ahead_sum(own_s, after(later_s, keep_eo), keep_eo, near_eo)
        own_x, later_x, out_x, own_y, later_y, out_y = core_split(
            [mine_p], [after(theirs_p, near_eo)], (keep_s, far_s)
        )
        near_eo = from_chip(near_eo, 1)
        out_x, out_y = from_x(out_x), from_y(out_y)
        joined_grad_rows = after(joined_grad_rows, own_x)
    else:
        grad_project = weight_grad(token_rows, joined_grad_rows)

        def owned(grad):
            part = lax.psum_scatter(grad, "fsdp", scatter_dimension=0, tiled=True)
            return lax.psum(part, "dp").astype(F32)

        own_project, own_output, own_expand, own_shrink = (
            owned(grad) for grad in (grad_project, grad_output, grad_expand, grad_shrink)
        )
        small = (sums_joined[0], sums1[0], sums1[1], sums1[2], sums_hidden[0], sums2[0], sums2[1], sums2[2])
        packed_grad = jnp.concatenate([v.reshape(parts, -1) for v in small], axis=1)
        shard = lax.psum(lax.psum_scatter(packed_grad.reshape(-1), "fsdp", scatter_dimension=0, tiled=True), "dp")
    token_grad = token_back(joined_grad_rows, project, first_grad)
    if pieces:
        half_p, half_e, half_o = project_weight.shape[1] // 2, expand_weight.shape[1] // 2, width // 2
        out_x, out_y = after((out_x, out_y), token_grad)
        own_x, later_x, own_y, later_y = middle_sum([own_x, later_x, out_x, own_y, later_y, out_y])
        later_x, later_y = from_y(later_x), from_x(later_y)
        keep_eo, far_eo = pair_sum(keep_eo, after(near_eo, own_x))
        far_eo = from_chip(far_eo, 2)
        later_x, later_y = after((later_x, later_y), keep_eo)
        keep_p, near_p, total_s = split_sum([own_x, later_x, own_y, later_y], more=FIRST // 4)
        near_p = from_chip(near_p, 1)
        total_seo = last_sum((total_s,), (keep_eo, after(far_eo, keep_p)))
        quarters_seo = from_plane(total_seo)
        keep_p, far_p = pair_sum(keep_p, after(near_p, total_seo))
        total_p = last_sum((keep_p, from_chip(far_p, 2)))
        quarters_p = from_plane(total_p)
        own_shrink, own_expand, own_output = place(
            pos,
            [total_seo, *after(quarters_seo, total_p)],
            (("stacked", 2 * width), ("halves", half_e), ("halves", half_o)),
        )
        own_project, *smalls = place(
            pos, [total_p, *after(quarters_p, own_expand)], (("halves", half_p), ("small", 128)), widths
        )
        smalls = [vector.reshape(-1) for vector in smalls]

    if not pieces:
        smalls, at = [], 0
        for size in widths:
            smalls.append(shard[at : at + size])
            at += size
    return (
        out_rows.reshape(pairs, seq, width),
        token_grad.reshape(pairs, seq, width),
        own_project,
        smalls[0],
        own_output,
        smalls[1],
        smalls[2],
        smalls[3],
        own_expand,
        smalls[4],
        own_shrink,
        smalls[5],
        smalls[6],
        smalls[7],
    )


def solution(mesh):
    rows3 = P(("dp", "fsdp"), None, None)
    matrix, vector = P("fsdp", None), P("fsdp")
    pieces = mesh.shape["dp"] == 4 and mesh.shape["fsdp"] == 8
    return jax.shard_map(
        functools.partial(local, pieces),
        mesh=mesh,
        in_specs=(
            rows3, P(("dp", "fsdp")), rows3,
            matrix, vector, matrix, vector, vector, vector,
            matrix, vector, matrix, vector, vector, vector,
        ),
        out_specs=(
            rows3, rows3,
            matrix, vector, matrix, vector, vector, vector,
            matrix, vector, matrix, vector, vector, vector,
        ),
        check_vma=False,
    )
```

```python
import functools

import jax
import jax.numpy as jnp
from jax import lax
from jax.experimental import pallas as pl
from jax.experimental.pallas import tpu as pltpu
from jax.sharding import PartitionSpec as P

HEADS = 12
HEAD_DIM = 64
REGIONS = 36
BF16 = jnp.bfloat16
F32 = jnp.float32

COVER = 100 * 10**9

NN = (((1,), (0,)), ((), ()))
NT = (((1,), (1,)), ((), ()))
TN = (((0,), (0,)), ((), ()))


def dot(left, right, dims=NN):
    return lax.dot_general(left, right, dims, preferred_element_type=F32)


def params(mebibytes):
    return pltpu.CompilerParams(vmem_limit_bytes=mebibytes * 1024 * 1024)


def cost(flops=0):
    return pl.CostEstimate(flops=flops, bytes_accessed=0, transcendentals=0)


def whole(shape, buffers=None):
    mode = None if buffers is None else pl.Buffered(buffers)
    return pl.BlockSpec(shape, lambda *at: (0,) * len(shape), pipeline_mode=mode)


HELD = pl.BlockSpec(memory_space=pltpu.VMEM)


def inside(shape, dtype=BF16):
    return pltpu.VMEM(shape, dtype)


def outside(shape, dtype=BF16):
    return pltpu.HBM(shape, dtype)


def in_vmem(values):
    return pltpu.with_memory_space_constraint(values, pltpu.VMEM)


def in_hbm(values):
    return pltpu.with_memory_space_constraint(values, pltpu.HBM)


def tile_of(size, most):
    return max(t for t in range(128, most + 1, 128) if size % t == 0)


def rows_of(count, most):
    fits = [t for t in range(16, most + 1, 16) if count % t == 0]
    return max(fits) if fits else count


CHIPS = (1, 3, 2)


def halves_copies(refs, into, pos, at, high, wide):
    half = wide // 2
    rows = high // 2
    for side in range(2):
        core = pos[1] if side == 0 else 1 - pos[1]
        shard = pos[0] * 2 + core
        yield refs[side], into.at[pl.ds(pl.multiple_of(shard * high, 16), high), :]
        for flip in range(4):
            buffer, first = refs[2 + side * 2 + (flip > 0)], max(flip - 1, 0) * 3 * rows
            up = pos[2] ^ (flip // 2)
            along = pos[3] ^ (flip % 2)
            for place, chip in enumerate(CHIPS):
                shard = (pos[0] ^ chip) * 2 + core
                to_row = pl.multiple_of(shard * high + up * rows, 16)
                to_column = pl.multiple_of(along * half, 128)
                yield (
                    buffer.at[pl.ds(first + place * rows, rows), pl.ds(at, half)],
                    into.at[pl.ds(to_row, rows), pl.ds(to_column, half)],
                )


def stacked_copies(refs, into, pos, high, wide):
    rows = high // 8
    own = pos[2] * 2 + pos[3]
    for side in range(2):
        core = pos[1] if side == 0 else 1 - pos[1]
        shard = pos[0] * 2 + core
        yield refs[side], into.at[pl.ds(pl.multiple_of(shard * high, 16), high), :]
        for place, chip in enumerate(CHIPS):
            shard = (pos[0] ^ chip) * 2 + core
            for plane in range(2):
                for block in range(2):
                    for part in range(2):
                        flip = block * (2 if part == plane else 1)
                        if plane:
                            flip = (1, 3)[block] if part == 0 else (2, 3)[block]
                        to_row = pl.multiple_of(shard * high + ((own ^ flip) * 2 + part) * rows, 16)
                        yield (
                            refs[2 + side * 2 + plane].at[
                                pl.ds((place * 2 + block) * rows, rows), pl.ds(part * wide, wide)
                            ],
                            into.at[pl.ds(to_row, rows), :],
                        )


def natural_copies(refs, into, pos):
    yield refs[0], into


class Weight:
    def __init__(self, shape, arrays, copies=natural_copies):
        self.shape, self.copies = shape, copies
        self.arrays = [in_vmem(array) for array in arrays]

    def specs(self):
        return [HELD] * len(self.arrays)

    def out(self):
        return inside(self.shape)

    def split(self, refs):
        return refs[: len(self.arrays)], refs[len(self.arrays) : -1], refs[-1]

    def arrive(self, refs, full, pos):
        @pl.when(pl.program_id(0) == 0)
        def _():
            for source, target in self.copies(refs, full, pos):
                target[...] = source[...]


def spread_kernel(pos, own, other, bias, hidden, rows, held):
    part = held.shape[2] * 3 // 4
    for at, chip in enumerate((0, *CHIPS)):
        held[(pos[0] ^ chip) * 2 + pos[1]] = own[at * 16 : at * 16 + 16].astype(F32)
        held[(pos[0] ^ chip) * 2 + 1 - pos[1]] = other[at * 16 : at * 16 + 16].astype(F32)
    bias[...] = jnp.zeros_like(bias)
    width = rows.shape[1]
    for shard in range(8):
        for at in range(2):
            to = (shard * 2 + at) * part
            to += width if to >= width else 0
            bias[0:1, to : to + part] = held[shard, at : at + 1, :part]
        for at in range(4):
            to = (shard * 4 + at) * part
            hidden[0:1, to : to + part] = held[shard, 5 + at : 6 + at, :part]
        to = shard * part
        rows[0:3, to : to + part] = held[shard, 2:5, :part]
        rows[3:6, to : to + part] = held[shard, 9:12, :part]


def spread(pos, shards, width, hidden_width):
    shapes = [(1, 3 * width), (1, hidden_width), (8, width)]
    return pl.pallas_call(
        spread_kernel,
        grid_spec=pltpu.PrefetchScalarGridSpec(
            num_scalar_prefetch=1,
            grid=(1,),
            in_specs=[whole((64, 128))] * 2,
            out_specs=[whole(shape) for shape in shapes],
            scratch_shapes=[pltpu.VMEM((8, 16, 128), F32)],
        ),
        out_shape=[jax.ShapeDtypeStruct(shape, F32) for shape in shapes],
        compiler_params=params(4),
        cost_estimate=cost(COVER),
        name="spread",
    )(pos, *shards)


def bundle_kernel(joined, first, second, hidden, out):
    part = out.shape[2] * 3 // 4
    out[...] = jnp.zeros_like(out)
    for shard in range(8):
        for at in range(2):
            of = (shard * 2 + at) * part
            out[shard, at : at + 1, :part] = joined[0:1, of : of + part]
        for at in range(4):
            of = (shard * 4 + at) * part
            out[shard, 5 + at : 6 + at, :part] = hidden[0:1, of : of + part]
        of = shard * part
        out[shard, 2:5, :part] = first[0:3, of : of + part]
        out[shard, 9:12, :part] = second[0:3, of : of + part]


def bundle(joined, first, second, hidden):
    return pl.pallas_call(
        bundle_kernel,
        out_shape=jax.ShapeDtypeStruct((8, 16, 128), F32),
        compiler_params=params(4),
        cost_estimate=cost(),
        name="bundle",
    )(joined, first, second, hidden)


def step_of(size):
    return pl.ds(pl.multiple_of(pl.program_id(0) * size, 16), size)


def columns_of(size):
    return pl.ds(pl.multiple_of(pl.program_id(0) * size, 128), size)


def join_kernel(pos, tokens, bias, *rest, weight, tile):
    pieces, (out, kept), (full, sem) = rest[: len(weight.arrays)], rest[-4:-2], rest[-2:]
    weight.arrive(pieces, full, pos)
    write = pltpu.make_async_copy(full, kept, sem)

    @pl.when(pl.program_id(0) == 0)
    def _():
        write.start()

    out[...] = (dot(tokens[...], full[:, columns_of(tile)]) + bias[...]).astype(BF16)

    @pl.when(pl.program_id(0) == pl.num_programs(0) - 1)
    def _():
        write.wait()


def join(pos, token_rows, weight, bias):
    rows, width = token_rows.shape
    columns = weight.shape[1]
    tile = tile_of(columns, 768)
    return pl.pallas_call(
        functools.partial(join_kernel, weight=weight, tile=tile),
        grid_spec=pltpu.PrefetchScalarGridSpec(
            num_scalar_prefetch=1,
            grid=(columns // tile,),
            in_specs=[whole((rows, width), 1), pl.BlockSpec((1, tile), lambda i, p: (0, i))] + weight.specs(),
            out_specs=[pl.BlockSpec((rows, tile), lambda i, p: (0, i)), pl.BlockSpec(memory_space=pltpu.HBM)],
            scratch_shapes=[pltpu.VMEM(weight.shape, BF16), pltpu.SemaphoreType.DMA(())],
        ),
        out_shape=[outside((rows, columns)), outside(weight.shape)],
        compiler_params=params(15),
        cost_estimate=cost(),
        name="join",
    )(pos, token_rows, bias, *weight.arrays)


def head_stack(block, low_half, padded):
    rows = block.shape[0]
    filler = jnp.zeros((padded - rows, block.shape[1]), F32)
    first = jnp.where(low_half, block, 0.0)
    second = jnp.where(low_half, 0.0, block)
    return jnp.concatenate([first, filler, second, filler], axis=0).astype(BF16)


def attend_kernel(captions, joined, context, probs):
    seq = joined.shape[1]
    width = context.shape[2]
    padded = probs.shape[3] // 2
    valid = captions[pl.program_id(0)] + 2 + REGIONS
    keep = lax.broadcasted_iota(jnp.int32, (seq, 2 * padded), 0) < valid
    low_half = lax.broadcasted_iota(jnp.int32, (1, 2 * HEAD_DIM), 1) < HEAD_DIM
    places = [pair * 2 * HEAD_DIM for pair in range(HEADS // 2)]
    scores = []
    for at in places:
        query = joined[0, :, at : at + 2 * HEAD_DIM].astype(F32)
        keys = joined[0, :, width + at : width + at + 2 * HEAD_DIM]
        scores.append(dot(keys, head_stack(query, low_half, padded), NT) * HEAD_DIM ** (-0.5))
    probabilities = []
    for score in scores:
        score = jnp.where(keep, score, -1000000000.0)
        grown = jnp.exp(score - jnp.max(score, axis=0, keepdims=True))
        total = jnp.sum(grown, axis=0, keepdims=True)
        probabilities.append((grown * (1.0 / total)).astype(BF16))
    for pair, at in enumerate(places):
        values = joined[0, :, 2 * width + at : 2 * width + at + 2 * HEAD_DIM]
        mixed = dot(probabilities[pair], values, TN)
        probs[0, pair] = probabilities[pair]
        context[0, :, at : at + 2 * HEAD_DIM] = jnp.where(
            low_half, mixed[:seq], mixed[padded : padded + seq]
        ).astype(BF16)


def attend(joined, captions):
    pairs, seq, columns = joined.shape
    width = columns // 3
    padded = (seq + 127) // 128 * 128
    return pl.pallas_call(
        attend_kernel,
        grid_spec=pltpu.PrefetchScalarGridSpec(
            num_scalar_prefetch=1,
            grid=(pairs,),
            in_specs=[pl.BlockSpec((1, seq, columns), lambda i, c: (i, 0, 0))],
            out_specs=[
                pl.BlockSpec((1, seq, width), lambda i, c: (i, 0, 0)),
                pl.BlockSpec((1, HEADS // 2, seq, 2 * padded), lambda i, c: (i, 0, 0, 0)),
            ],
        ),
        out_shape=[
            inside((pairs, seq, width)),
            outside((pairs, HEADS // 2, seq, 2 * padded)),
        ],
        compiler_params=params(8),
        cost_estimate=cost(),
        name="attend",
    )(captions, in_hbm(joined))


def attend_back_kernel(joined, probs, grads, out, sums):
    seq = joined.shape[1]
    width = grads.shape[2]
    padded = probs.shape[3] // 2
    low_half = lax.broadcasted_iota(jnp.int32, (1, 2 * HEAD_DIM), 1) < HEAD_DIM

    @pl.when(pl.program_id(0) == 0)
    def _():
        sums[...] = jnp.zeros_like(sums)

    places = [pair * 2 * HEAD_DIM for pair in range(HEADS // 2)]
    prob_grads, grad_stacks = [], []
    for at in places:
        values = joined[0, :, 2 * width + at : 2 * width + at + 2 * HEAD_DIM]
        grad_stacks.append(head_stack(grads[0, :, at : at + 2 * HEAD_DIM].astype(F32), low_half, padded))
        prob_grads.append(dot(values, grad_stacks[-1], NT))
    score_grads = []
    for pair, prob_grad in enumerate(prob_grads):
        prob = probs[0, pair].astype(F32)
        row_dot = jnp.sum(prob * prob_grad, axis=0, keepdims=True)
        score_grads.append((prob * (prob_grad - row_dot) * HEAD_DIM ** (-0.5)).astype(BF16))
    results = []
    for pair, at in enumerate(places):
        query = joined[0, :, at : at + 2 * HEAD_DIM].astype(F32)
        keys = joined[0, :, width + at : width + at + 2 * HEAD_DIM]
        mixed = dot(score_grads[pair], keys, TN)
        query_grad = jnp.where(low_half, mixed[:seq], mixed[padded : padded + seq])
        keys_grad = dot(score_grads[pair], head_stack(query, low_half, padded))
        results.append((query_grad, keys_grad, dot(probs[0, pair], grad_stacks[pair])))
    for at, blocks in zip(places, results):
        for part, block in enumerate(blocks):
            out[0, :, part * width + at : part * width + at + 2 * HEAD_DIM] = block.astype(BF16)
            if part != 1:
                to = part // 2 * width + at
                sums[:, to : to + 2 * HEAD_DIM] += jnp.sum(block, axis=0, keepdims=True)


def attend_back(joined, probs, grads):
    pairs, seq, columns = joined.shape
    width = columns // 3
    padded = probs.shape[3] // 2
    return pl.pallas_call(
        attend_back_kernel,
        grid=(pairs,),
        in_specs=[
            pl.BlockSpec((1, seq, columns), lambda i: (i, 0, 0)),
            pl.BlockSpec((1, HEADS // 2, seq, 2 * padded), lambda i: (i, 0, 0, 0)),
            pl.BlockSpec((1, seq, width), lambda i: (i, 0, 0)),
        ],
        out_specs=[
            pl.BlockSpec((1, seq, columns), lambda i: (i, 0, 0)),
            pl.BlockSpec((1, 2 * width), lambda i: (0, 0)),
        ],
        out_shape=[
            inside((pairs, seq, columns)),
            jax.ShapeDtypeStruct((1, 2 * width), F32),
        ],
        compiler_params=params(10),
        cost_estimate=cost(),
        name="attend_back",
    )(in_hbm(joined), in_hbm(probs), in_vmem(grads))


def norm_parts(values):
    centred = values - jnp.mean(values, axis=-1, keepdims=True)
    spread = jnp.mean(centred * centred, axis=-1, keepdims=True)
    scale = lax.rsqrt(spread + 1e-05)
    return centred * scale, scale


def norm_back(upstream, unit, scale, gain):
    scaled = upstream * gain
    return scale * (
        scaled
        - jnp.mean(scaled, axis=-1, keepdims=True)
        - unit * jnp.mean(scaled * unit, axis=-1, keepdims=True)
    )


def add_sums(sums, rows):
    for at, values in enumerate(rows):
        sums[at : at + 1, :] += jnp.sum(values, axis=0, keepdims=True)


def chunked(count, load, use):
    ready = load(0)
    for at in range(count):
        following = load(at + 1) if at + 1 < count else None
        use(at, ready)
        ready = following


def chunk_slices(rows, most):
    tile = rows_of(rows, most)
    return [slice(at, at + tile) for at in range(0, rows, tile)]


def first_kernel(pos, context, bias, tokens, gain, shift, *rest, weight):
    pieces, (unit, scale, normed_low), full = weight.split(rest)
    weight.arrive(pieces, full, pos)
    chunks = chunk_slices(tokens.shape[0], 416)

    def normalise(at, branch):
        rows = chunks[at]
        unit_rows, scale_rows = norm_parts(tokens[rows, :].astype(F32) + (branch + bias[...]))
        unit[rows, :] = unit_rows
        scale[rows, :] = scale_rows
        normed_low[rows, :] = (unit_rows * gain[...] + shift[...]).astype(BF16)

    chunked(len(chunks), lambda at: dot(context[chunks[at], :], full[...]), normalise)


def first_norm(pos, context, weight, bias, token_rows, gain, shift):
    rows, width = token_rows.shape
    row = whole((1, width))
    return pl.pallas_call(
        functools.partial(first_kernel, weight=weight),
        grid_spec=pltpu.PrefetchScalarGridSpec(
            num_scalar_prefetch=1,
            grid=(1,),
            in_specs=[HELD, row, HELD, row, row] + weight.specs(),
            out_specs=[HELD] * 4,
        ),
        out_shape=[inside((rows, width), F32), inside((rows, 1), F32), inside((rows, width)), weight.out()],
        compiler_params=params(10),
        cost_estimate=cost(),
        name="first_norm",
    )(pos, in_vmem(context), bias, in_vmem(token_rows), gain, shift, *weight.arrays)


def expand_kernel(pos, normed_low, bias, *rest, weight, tile):
    pieces, (active, slope), full = weight.split(rest)
    weight.arrive(pieces, full, pos)
    at = columns_of(tile)
    expand = dot(normed_low[...], full[:, at]) + bias[...]
    half = 0.5 * (1.0 + lax.erf(expand * 0.7071067811865476))
    active[:, at] = (expand * half).astype(BF16)
    slope[:, at] = (half + expand * jnp.exp(-0.5 * expand * expand) * 0.3989422804014327).astype(BF16)


def expand_act(pos, normed_low, weight, bias):
    rows, width = normed_low.shape
    columns = weight.shape[1]
    tile = tile_of(columns, 768)
    return pl.pallas_call(
        functools.partial(expand_kernel, weight=weight, tile=tile),
        grid_spec=pltpu.PrefetchScalarGridSpec(
            num_scalar_prefetch=1,
            grid=(columns // tile,),
            in_specs=[HELD, pl.BlockSpec((1, tile), lambda i, p: (0, i))] + weight.specs(),
            out_specs=[HELD] * 3,
        ),
        out_shape=[inside((rows, columns))] * 2 + [weight.out()],
        compiler_params=params(12),
        cost_estimate=cost(),
        name="expand_act",
    )(pos, in_vmem(normed_low), bias, *weight.arrays)


def second_kernel(pos, captions, active, bias, unit, gain, shift, gain2, shift2, cotangent, *rest, weight, seq):
    pieces, (out, low, grad, sums), full, (held, sems) = *weight.split(rest[:-2]), rest[-2:]
    weight.arrive(pieces, full, pos)
    sums[...] = jnp.zeros_like(sums)
    tile = rows_of(held.shape[0], 4 * seq)
    count = held.shape[0] // tile

    def write(at):
        rows = pl.ds(pl.multiple_of(at * tile, 16), tile)
        return pltpu.make_async_copy(held.at[rows, :], out.at[rows, :], sems.at[at])

    def chunk(at, carry):
        rows = pl.ds(pl.multiple_of(at * tile, 16), tile)
        normed = unit[rows, :] * gain[...] + shift[...]
        unit2, scale2 = norm_parts(normed + (dot(active[rows, :], full[...]) + bias[...]))
        held[rows, :] = (unit2 * gain2[...] + shift2[...]).astype(BF16)
        write(at).start()
        row = lax.broadcasted_iota(jnp.int32, (tile, 1), 0)
        live = jnp.zeros(row.shape, jnp.bool_)
        for pair in range(tile // seq):
            valid = captions[at * (tile // seq) + pair] + 2 + REGIONS
            live = live | ((row >= pair * seq) & (row < pair * seq + valid))
        upstream = jnp.where(live, cotangent[rows, :].astype(F32), 0.0)
        second = norm_back(upstream, unit2, scale2, gain2[...])
        grad[rows, :] = second
        low[rows, :] = second.astype(BF16)
        add_sums(sums, (second, upstream * unit2, upstream))
        return carry

    lax.fori_loop(0, count, chunk, 0)
    for at in range(count):
        write(at).wait()


def second_norm(pos, captions, active, weight, bias, unit, gain, shift, gain2, shift2, cotangent, seq):
    rows, width = unit.shape
    row = whole((1, width))
    return pl.pallas_call(
        functools.partial(second_kernel, weight=weight, seq=seq),
        grid_spec=pltpu.PrefetchScalarGridSpec(
            num_scalar_prefetch=2,
            grid=(1,),
            in_specs=[HELD, row, HELD, row, row, row, row, HELD] + weight.specs(),
            out_specs=[pl.BlockSpec(memory_space=pltpu.HBM), HELD, HELD, whole((8, width)), HELD],
            scratch_shapes=[pltpu.VMEM((rows, width), BF16), pltpu.SemaphoreType.DMA((rows // 16,))],
        ),
        out_shape=[
            outside((rows, width)),
            inside((rows, width)),
            inside((rows, width), F32),
            jax.ShapeDtypeStruct((8, width), F32),
            weight.out(),
        ],
        compiler_params=params(12),
        cost_estimate=cost(),
        name="second_norm",
    )(pos, captions, in_vmem(active), bias, in_vmem(unit), gain, shift, gain2, shift2, in_vmem(cotangent), *weight.arrays)


def hidden_back_kernel(low, weight, slope, out, sums):
    at = columns_of(sums.shape[1])
    grad = dot(low[...], weight[at, :], NT) * slope[:, at].astype(F32)
    out[:, at] = grad.astype(BF16)
    sums[...] = jnp.sum(grad, axis=0, keepdims=True)


def hidden_back(low, weight, slope):
    rows, width = low.shape
    hidden = weight.shape[0]
    tile = tile_of(hidden, 768)
    return pl.pallas_call(
        hidden_back_kernel,
        grid=(hidden // tile,),
        in_specs=[HELD] * 3,
        out_specs=[HELD, pl.BlockSpec((1, tile), lambda i: (0, i))],
        out_shape=[inside((rows, hidden)), jax.ShapeDtypeStruct((1, hidden), F32)],
        compiler_params=params(10),
        cost_estimate=cost(),
        name="hidden_back",
    )(in_vmem(low), in_vmem(weight), in_vmem(slope))


def first_back_kernel(hidden, weight, second, unit, scale, gain, out_weight, grad, low, context_grad, sums):
    sums[...] = jnp.zeros_like(sums)
    chunks = chunk_slices(grad.shape[0], 416)
    waiting = []

    def pass_on():
        rows, first_low = waiting.pop()
        context_grad[rows, :] = dot(first_low, out_weight[...], NT).astype(BF16)

    def normalise(at, product):
        rows = chunks[at]
        unit_rows = unit[rows, :]
        normed_grad = product + second[rows, :]
        first = norm_back(normed_grad, unit_rows, scale[rows, :], gain[...])
        grad[rows, :] = first
        first_low = first.astype(BF16)
        low[rows, :] = first_low
        add_sums(sums, (first, normed_grad * unit_rows, normed_grad))
        if waiting:
            pass_on()
        waiting.append((rows, first_low))

    chunked(len(chunks), lambda at: dot(hidden[chunks[at], :], weight[...], NT), normalise)
    pass_on()


def first_back(hidden, weight, second, unit, scale, gain, out_weight):
    rows, width = second.shape
    return pl.pallas_call(
        first_back_kernel,
        grid=(1,),
        in_specs=[HELD] * 5 + [whole((1, width)), HELD],
        out_specs=[HELD, HELD, HELD, whole((8, width))],
        out_shape=[
            inside((rows, width), F32),
            inside((rows, width)),
            inside((rows, width)),
            jax.ShapeDtypeStruct((8, width), F32),
        ],
        compiler_params=params(13),
        cost_estimate=cost(COVER),
        name="first_back",
    )(in_vmem(hidden), in_vmem(weight), in_vmem(second), in_vmem(unit), in_vmem(scale), gain, in_vmem(out_weight))


def token_back_kernel(grads, weight, first, out):
    at = step_of(out.shape[0])
    out[...] = dot(grads[at, :], weight[...], NT) + first[at, :]


def token_back(grads, weight, first):
    rows, width = first.shape
    tile = rows_of(rows, 416)
    return pl.pallas_call(
        token_back_kernel,
        grid=(rows // tile,),
        in_specs=[HELD] * 3,
        out_specs=pl.BlockSpec((tile, width), lambda i: (i, 0)),
        out_shape=outside((rows, width), F32),
        compiler_params=params(9),
        cost_estimate=cost(),
        name="token_back",
    )(in_vmem(grads), in_vmem(weight), in_vmem(first))


def weight_grad_kernel(left, right, out):
    out[...] = dot(left[...], right[...], TN).astype(BF16)


def weight_grad(left, right):
    rows, height = left.shape
    columns = right.shape[1]
    tile = tile_of(columns, 768)
    high = tile_of(height, 768)
    return pl.pallas_call(
        weight_grad_kernel,
        grid=(height // high, columns // tile),
        in_specs=[
            pl.BlockSpec((rows, high), lambda i, j: (0, i)),
            pl.BlockSpec((rows, tile), lambda i, j: (0, j)),
        ],
        out_specs=pl.BlockSpec((high, tile), lambda i, j: (i, j)),
        out_shape=outside((height, columns)),
        compiler_params=params(24),
        cost_estimate=cost(),
        name="weight_grad",
    )(left, right)


def regroup_kernel(values, out):
    part = values.shape[1] // 8
    blocks = [values[:, shard * part : (shard + 1) * part] for shard in (0, 2, 4, 6, 1, 3, 5, 7)]
    out[...] = jnp.concatenate(blocks, axis=1)


def regroup(values):
    return held_call(regroup_kernel, "regroup", [values.shape], [values])[0]


def by_core(pos, mine, theirs, store):
    store(mine, pos[1])
    store(theirs, 1 - pos[1])


def halves_grad_kernel(pos, left, right, *rest):
    extra, (mine, theirs) = (rest[0] if len(rest) == 3 else None), rest[-2:]
    along, half = pl.program_id(0), right.shape[1] // 2
    columns, high, rows = right[:, columns_of(half)], left.shape[1] // 2, mine.shape[3]

    def store(out, core):
        grads = dot(left[:, pl.ds(pl.multiple_of(core * high, 128), high)], columns, TN)
        for chip in range(4):
            for up in range(2):
                at = (chip * 2 + up) * rows
                to = (chip ^ pos[0], up ^ pos[2], along ^ pos[3])
                out[(*to, slice(None), slice(0, half))] = grads[at : at + rows].astype(BF16)
                if extra is not None:
                    out[(*to, slice(None), slice(half, None))] = jnp.zeros((rows, 128), BF16)
                    out[(*to, slice(0, 16), slice(half, None))] = extra[chip * 2 + core].astype(BF16)

    by_core(pos, mine, theirs, store)


def stacked_grad_kernel(pos, left, right, mine, theirs):
    high, rows, wide = left.shape[1] // 8, mine.shape[3], right.shape[1]

    def store(out, core):
        for part in range(2):
            chip = pl.program_id(0) * 2 + part
            columns = pl.ds(pl.multiple_of((chip * 2 + core) * high, 128), high)
            grads = dot(left[:, columns], right[...], TN)
            for quarter in range(4):
                for side in range(2):
                    at = (quarter * 2 + side) * rows
                    to = (chip ^ pos[0], (quarter // 2) ^ pos[2], (quarter % 2) ^ pos[3])
                    block = grads[at : at + rows].astype(BF16)
                    out[(*to, slice(None), slice(side * wide, (side + 1) * wide))] = block

    by_core(pos, mine, theirs, store)


def pieces_grad(kernel, name, pos, left, right, shape, extra=()):
    out = inside((4, 2, 2) + shape)
    return pl.pallas_call(
        kernel,
        grid_spec=pltpu.PrefetchScalarGridSpec(
            num_scalar_prefetch=1,
            grid=(2,),
            in_specs=[HELD, HELD] + [whole(array.shape) for array in extra],
            out_specs=[HELD, HELD],
        ),
        out_shape=[out, out],
        compiler_params=params(13),
        cost_estimate=cost(),
        name=name,
    )(pos, in_vmem(left), in_vmem(right), *extra)


def halves_grad(pos, left, right, extra=None):
    shape = (left.shape[1] // 16, right.shape[1] // 2 + (0 if extra is None else 128))
    more = () if extra is None else (extra,)
    return pieces_grad(halves_grad_kernel, "halves_grad", pos, left, right, shape, more)


def stacked_grad(pos, left, right):
    shape = (left.shape[1] // 64, 2 * right.shape[1])
    return pieces_grad(stacked_grad_kernel, "stacked_grad", pos, left, right, shape)


def held_call(kernel, name, outs, values, flops=0):
    return pl.pallas_call(
        kernel,
        in_specs=[HELD] * len(values),
        out_specs=[HELD] * len(outs),
        out_shape=[inside(out) for out in outs],
        compiler_params=params(4),
        cost_estimate=cost(flops),
        name=name,
    )(*map(in_vmem, values))


def add(*terms):
    total = terms[0].astype(F32)
    for term in terms[1:]:
        total += term.astype(F32)
    return total


FIRST = 1024


def shrink_sum_kernel(mine, theirs, keep, near, kept, send):
    for chip in range(4):
        for flip in range(4):
            pick = (chip, flip // 2, flip % 2)
            total = add(mine[pick], theirs[pick]).astype(BF16)
            (keep, near)[chip % 2][chip // 2, flip] = total[:, :FIRST]
            (kept, send)[flip % 2][flip // 2, chip] = total[:, FIRST:]


def shrink_sum(mine, theirs):
    rows, wide = mine.shape[3:]
    outs = [(2, 4, rows, FIRST)] * 2 + [(2, 4, rows, wide - FIRST)] * 2
    return held_call(shrink_sum_kernel, "shrink_sum", outs, [mine, theirs])


def core_split_kernel(*refs, count):
    outs = refs[-6:]
    for half in range(2):
        own, later, send = outs[3 * half : 3 * half + 3]
        first = 1 + half
        for flip, out in ((0, own), (3 - first, later), (first, send.at[0]), (3, send.at[1])):
            at = 0
            for mine, theirs in zip(refs[:count], refs[count : 2 * count]):
                wide = mine.shape[4]
                for chip in range(2):
                    pick = (2 * half + chip, flip // 2, flip % 2)
                    out[chip, :, at : at + wide] = add(mine[pick], theirs[pick]).astype(BF16)
                at += wide
            if len(refs) > 2 * count + 6:
                near, far = refs[2 * count : 2 * count + 2]
                wide = near.shape[2] // 4
                for chip in range(2):
                    columns = slice((2 * half + chip) * wide, (2 * half + chip + 1) * wide)
                    out[chip, :, at:] = add(near[flip, :, columns], far[flip, :, columns]).astype(BF16)


def core_split(mine, theirs, more=()):
    shape = (2, mine[0].shape[3], sum(m.shape[4] for m in mine) + sum(m.shape[2] // 8 for m in more))
    kernel = functools.partial(core_split_kernel, count=len(mine))
    return held_call(kernel, "core_split", [shape, shape, (2,) + shape] * 2, [*mine, *theirs, *more])


def middle_sum_kernel(*refs):
    for half in range(2):
        own, later, received = refs[3 * half : 3 * half + 3]
        refs[6 + 2 * half][...] = add(own[...], received[0]).astype(BF16)
        refs[7 + 2 * half][...] = add(later[...], received[1]).astype(BF16)


def middle_sum(parts):
    return held_call(middle_sum_kernel, "middle_sum", [parts[0].shape] * 4, parts)


def split_sum_kernel(own, received, own_too, received_too, keep, near, *rest):
    for chip in range(4):
        one, two = (own, received) if chip < 2 else (own_too, received_too)
        total = add(one[chip % 2], two[chip % 2]).astype(BF16)
        wide = keep.shape[2]
        (keep, near)[chip % 2][chip // 2] = total[:, :wide]
        if rest:
            part = total.shape[1] - wide
            rest[0][:, chip * part : (chip + 1) * part] = total[:, wide:]


def split_sum(parts, more=0, flops=0):
    _, rows, wide = parts[0].shape
    outs = [(2, rows, wide - more)] * 2 + ([(rows, 4 * more)] if more else [])
    return held_call(split_sum_kernel, "split_sum", outs, parts, flops)


def ahead_sum_kernel(one, two, keep, near, keep_out, near_out):
    wide = one.shape[2]
    for chip in range(4):
        source, out = (keep, keep_out) if chip % 2 == 0 else (near, near_out)
        out[chip // 2, :, :wide] = add(one[chip], two[chip]).astype(BF16)
        out[chip // 2, :, wide:] = source[chip // 2]


def ahead_sum(one, two, keep, near):
    shape = keep.shape[:2] + (keep.shape[2] + one.shape[2],)
    return held_call(ahead_sum_kernel, "ahead_sum", [shape] * 2, [one, two, keep, near])


def pair_sum_kernel(keep, received, one, two):
    one[...] = add(keep[0], received[0]).astype(BF16)
    two[...] = add(keep[1], received[1]).astype(BF16)


def pair_sum(keep, received, flops=0):
    return held_call(pair_sum_kernel, "pair_sum", [keep.shape[1:]] * 2, [keep, received], flops)


def last_sum_kernel(*refs, counts):
    out, at = refs[-1], 0
    for count in counts:
        terms, refs = refs[:count], refs[count:]
        wide = terms[0].shape[1]
        out[:, at : at + wide] = add(*(term[...] for term in terms)).astype(BF16)
        at += wide


def last_sum(*groups):
    kernel = functools.partial(last_sum_kernel, counts=[len(group) for group in groups])
    shape = (groups[0][0].shape[0], sum(group[0].shape[1] for group in groups))
    return held_call(kernel, "last_sum", [shape], [part for group in groups for part in group])[0]


def place_kernel(pos, *refs, layout):
    parts, outs = refs[:4], refs[4:]
    rows = parts[0].shape[0]
    for flip, part in enumerate(parts):
        up, along = pos[2] ^ (flip // 2), pos[3] ^ (flip % 2)
        at = 0
        for (kind, wide), out in zip(layout, outs):
            if kind == "halves":
                to_row = pl.multiple_of(up * rows, 16)
                to_column = pl.multiple_of(along * wide, 128)
                out[pl.ds(to_row, rows), pl.ds(to_column, wide)] = part[:, at : at + wide].astype(F32)
            elif kind == "stacked":
                for side in range(2):
                    to_row = pl.multiple_of(((up * 2 + along) * 2 + side) * rows, 16)
                    from_column = at + side * (wide // 2)
                    out[pl.ds(to_row, rows), :] = part[:, from_column : from_column + wide // 2].astype(F32)
            else:

                @pl.when((up == 0) & (along == 0))
                def _(part=part, at=at):
                    row = 0
                    for vector in outs[len(layout) - 1 :]:
                        for to in range(0, vector.shape[1], 96):
                            vector[:, to : to + 96] = part[row : row + 1, at : at + 96].astype(F32)
                            row += 1

            at += wide


def place(pos, parts, layout, sizes=()):
    rows = parts[0].shape[0]
    shapes = {
        "halves": lambda wide: (2 * rows, 2 * wide),
        "stacked": lambda wide: (8 * rows, wide // 2),
    }
    outs = [jax.ShapeDtypeStruct(shapes[kind](wide), F32) for kind, wide in layout if kind != "small"]
    outs += [jax.ShapeDtypeStruct((1, size), F32) for size in sizes]
    return pl.pallas_call(
        functools.partial(place_kernel, layout=layout),
        grid_spec=pltpu.PrefetchScalarGridSpec(
            num_scalar_prefetch=1,
            grid=(1,),
            in_specs=[HELD] * 4,
            out_specs=[whole(out.shape, 1) for out in outs],
        ),
        out_shape=outs,
        compiler_params=params(10),
        cost_estimate=cost(),
        name="place",
    )(pos, *map(in_vmem, parts))


def from_core(values):
    return lax.ppermute(values, "fsdp", [(i, i ^ 1) for i in range(8)])


def from_plane(values):
    parts = values if isinstance(values, (list, tuple)) else [values] * 3
    return [
        lax.ppermute(part, "dp", [(i, i ^ flip) for i in range(4)]) for flip, part in zip((1, 2, 3), parts)
    ]


def from_x(values):
    return lax.ppermute(values, "dp", [(i, i ^ 1) for i in range(4)])


def from_y(values):
    return lax.ppermute(values, "dp", [(i, i ^ 2) for i in range(4)])


def from_chips(values):
    return [from_chip(values, flip) for flip in CHIPS]


def from_chip(values, flip):
    return lax.ppermute(values, "fsdp", [(i, i ^ (2 * flip)) for i in range(8)])


def below_kernel(*refs):
    at = 0
    for ref in refs[:-1]:
        rows, wide = ref.shape[0], refs[-1].shape[1]
        refs[-1][at : at + rows] = ref[:, :wide]
        at += rows


def below(*parts, wide=None, flops=0):
    rows = sum(part.shape[0] for part in parts)
    return pl.pallas_call(
        below_kernel,
        in_specs=[HELD] * len(parts),
        out_specs=HELD,
        out_shape=inside((rows, wide or parts[0].shape[1])),
        compiler_params=params(4),
        cost_estimate=cost(flops),
        name="below",
    )(*map(in_vmem, parts))


def pick_kernel(pos, shard, out):
    rows, wide = out.shape[0] // 2, shard.shape[1]
    own = pos[2] * 2 + pos[3]
    for block, part, flip in ((0, 0, 0), (0, 1, 0), (1, 0, 2), (1, 1, 1)):
        from_row = pl.multiple_of(((own ^ flip) * 2 + part) * rows, 16)
        out[block * rows : (block + 1) * rows, part * wide : (part + 1) * wide] = shard[pl.ds(from_row, rows), :]


def pick(pos, shard):
    return pl.pallas_call(
        pick_kernel,
        grid_spec=pltpu.PrefetchScalarGridSpec(
            num_scalar_prefetch=1, grid=(1,), in_specs=[whole(shard.shape, 1)], out_specs=HELD
        ),
        out_shape=inside((shard.shape[0] // 4, 2 * shard.shape[1])),
        compiler_params=params(4),
        cost_estimate=cost(),
        name="pick",
    )(pos, shard)


def left_right_kernel(whole_ref, left, right):
    half = left.shape[1]
    left[...] = whole_ref[:, :half]
    right[...] = whole_ref[:, half:]


def left_right(values):
    rows, wide = values.shape
    return held_call(left_right_kernel, "left_right", [(rows, wide // 2)] * 2, [values])


def beside_kernel(left, right, out):
    half = left.shape[1]
    out[:, :half] = left[...]
    out[:, half:] = right[...]


def beside(left, right):
    rows, wide = left.shape
    return held_call(beside_kernel, "beside", [(rows, 2 * wide)], [left, right])[0]


def after(values, *others):
    return lax.optimization_barrier((values, others))[0]


def half_of(pos, shard):
    rows, wide = shard.shape[0] // 2, shard.shape[1] // 2
    return lax.dynamic_slice(shard, (pos[2] * rows, pos[3] * wide), (rows, wide))


def both_cores(pieces):
    return [*pieces, *(from_core(piece) for piece in pieces)]


def gather(values):
    return lax.all_gather(values, "fsdp", axis=0, tiled=True)


def local(
    pieces,
    tokens,
    captions,
    cotangent,
    project_weight,
    project_bias,
    output_weight,
    output_bias,
    first_gain,
    first_shift,
    expand_weight,
    expand_bias,
    shrink_weight,
    shrink_bias,
    second_gain,
    second_shift,
):
    pairs, seq, width = tokens.shape
    rows = pairs * seq
    parts = lax.axis_size("fsdp")
    token_rows = tokens.reshape(rows, width)
    cot_rows = cotangent.reshape(rows, width)

    vectors = (project_bias, output_bias, first_gain, first_shift, expand_bias, shrink_bias, second_gain, second_shift)
    widths = [vector.shape[0] for vector in vectors]
    replica, part = lax.axis_index("dp"), lax.axis_index("fsdp")
    pos = jnp.stack([part // 2, part % 2, replica // 2, replica % 2]).astype(jnp.int32)
    shapes = [(parts * shard.shape[0], shard.shape[1]) for shard in (project_weight, output_weight, expand_weight, shrink_weight)]
    if pieces:
        chips_p = from_chips(half_of(pos, project_weight))
        sibling_p = from_core(project_weight)
        held = jnp.concatenate([vector.reshape(-1, 96) for vector in vectors], axis=0)
        held = jnp.pad(held, ((0, 4), (0, 32)))
        quarter_e = [half_of(pos, expand_weight), half_of(pos, output_weight), jnp.pad(held, ((0, 32), (0, 0)))]
        quarter_e = jnp.concatenate(quarter_e, axis=1)
        wide_e = quarter_e.shape[1] - 128
        quarter_s, token_group = pick(pos, shrink_weight), regroup(token_rows)
        chips_p = after(chips_p, sibling_p, quarter_e, quarter_s, token_group)
        mine_p = below(*chips_p)
        quarter_e = after(quarter_e, *chips_p)
        far_e = from_chip(quarter_e, 2)
        near_e = [from_chip(quarter_e, 1), from_chip(far_e, 1)]
        plane_p = from_plane(mine_p)
        plane_p = below(*plane_p, flops=COVER)
        near_e = after(near_e, plane_p)
        other_p = [from_core(mine_p), from_core(plane_p)]

        def halves(shape, shard, sibling, group, at):
            copies = functools.partial(halves_copies, at=at, high=shard.shape[0], wide=shard.shape[1])
            return Weight(shape, [shard, sibling, *group], copies)

        project = halves(shapes[0], project_weight, sibling_p, (mine_p, plane_p, *other_p), 0)
        quarter_s = after(quarter_s, plane_p)
        far_s = from_chip(quarter_s, 2)
        mine_e = below(*near_e, far_e, wide=wide_e)
        plane_e = from_plane(mine_e)
        held = jnp.concatenate([held, *(chip[:16, wide_e:] for chip in (*near_e, far_e))], axis=0)
        held = after(held, mine_e)
        bias_full, hidden_bias, rows6 = spread(pos, [held, from_core(held)], width, expand_weight.shape[1])
        out_bias, gain1, shift1, down_bias, gain2, shift2 = (rows6[at : at + 1] for at in range(6))
    else:
        project, output, expand, shrink = (
            Weight(shape, [gather(shard)])
            for shape, shard in zip(shapes, (project_weight, output_weight, expand_weight, shrink_weight))
        )
        packed = gather(jnp.concatenate(vectors)[None, :])
        full, at = [], 0
        for size in widths:
            full.append(packed[:, at : at + size].reshape(1, parts * size).astype(F32))
            at += size
        bias_row, out_bias, gain1, shift1, hidden_bias, down_bias, gain2, shift2 = full
        bias_full = jnp.concatenate([bias_row[:, :width], jnp.zeros((1, width), F32), bias_row[:, width:]], axis=1)

    joined, project = join(pos, token_rows, project, bias_full)
    joined3 = joined.reshape(pairs, seq, 3 * width)
    if pieces:
        near_s = from_chip(after(quarter_s, joined), 1)
    context, probs = attend(joined3, captions)
    context_rows = context.reshape(rows, width)
    if pieces:
        far_s = after(far_s, context)
        near_s = [near_s, from_chip(far_s, 1)]
        context_group = regroup(context_rows)
        plane_e = below(*after(plane_e, far_s, context_group))
        mine_s = below(*after(near_s, plane_e), far_s, flops=COVER)
        left_s, right_s = left_right(mine_s)
        plane_s = [from_x(left_s), from_y(right_s)]
        context_rows = after(context_rows, mine_s)
        group_e = (mine_e, plane_e, *after([from_core(mine_e), from_core(plane_e)], mine_s))
        sibling_e = from_core(after(expand_weight, joined))
        sibling_o = from_core(after(output_weight, joined))
        expand = halves(shapes[2], expand_weight, sibling_e, group_e, 0)
        output = halves(shapes[1], output_weight, sibling_o, group_e, expand_weight.shape[1] // 2)
    unit1, scale1, normed_low, output = first_norm(pos, context_rows, output, out_bias, token_rows, gain1, shift1)
    active, slope, expand = expand_act(pos, normed_low, expand, hidden_bias)
    if pieces:
        plane_s = beside(*after(plane_s, active))
        normed_group = regroup(after(normed_low, plane_s))
        other_s = [from_core(mine_s), from_core(plane_s)]
        sibling_s = from_core(after(shrink_weight, active))
        shrink = Weight(
            shapes[3],
            [shrink_weight, sibling_s, mine_s, plane_s, *after(other_s, normed_group)],
            functools.partial(stacked_copies, high=shrink_weight.shape[0], wide=shrink_weight.shape[1]),
        )
    out_rows, shrink_low, second_grad, sums2, shrink = second_norm(
        pos, captions, active, shrink, down_bias, unit1, gain1, shift1, gain2, shift2, cot_rows, seq
    )
    if pieces:
        mine_s, theirs_s = stacked_grad(pos, active, shrink_low)
        theirs_s = from_core(theirs_s)
        shrink_low = after(shrink_low, mine_s)
    else:
        grad_shrink = weight_grad(active, shrink_low)
    expand_low, sums_hidden = hidden_back(shrink_low, shrink, slope)
    if pieces:
        keep_s, near_s, kept_s, send_s = shrink_sum(mine_s, after(theirs_s, expand_low))
        expand_low = after(expand_low, kept_s)
        near_s, send_s = from_chip(near_s, 1), from_x(send_s)
        mine_e, theirs_e = halves_grad(pos, normed_group, expand_low)
        theirs_e = from_core(theirs_e)
        expand_low = after(expand_low, mine_e)
    first_grad, branch_low, context_grad, sums1 = first_back(
        expand_low, expand, second_grad, unit1, scale1, gain1, output
    )
    if pieces:
        own_s, later_s = pair_sum(kept_s, after(send_s, branch_low))
        mine_o, theirs_o = halves_grad(pos, context_group, after(branch_low, own_s))
        theirs_o = from_core(theirs_o)
        later_s = from_y(later_s)
        keep_s, far_s = pair_sum(keep_s, after(near_s, mine_o))
        own_x, later_x, out_x, own_y, later_y, out_y = core_split(
            [mine_e, mine_o], after([theirs_e, theirs_o], keep_s)
        )
        far_s = from_chip(far_s, 2)
        out_x, out_y = from_x(out_x), from_y(out_y)
        context_grad = after(context_grad, own_x)
    else:
        grad_expand = weight_grad(normed_low, expand_low)
        grad_output = weight_grad(context_rows, branch_low)
    joined_grad, sums_joined = attend_back(joined3, probs, context_grad.reshape(pairs, seq, width))
    joined_grad_rows = joined_grad.reshape(rows, 3 * width)
    if pieces:
        extra = bundle(sums_joined, sums1, sums2, sums_hidden)
        mine_p, theirs_p = halves_grad(pos, token_group, joined_grad_rows, extra)
        theirs_p = from_core(theirs_p)
        out_x, out_y = after((out_x, out_y), mine_p)
        own_x, later_x, own_y, later_y = middle_sum([own_x, later_x, out_x, own_y, later_y, out_y])
        later_x, later_y = after((from_y(later_x), from_x(later_y)), far_s)
        keep_eo, near_eo = split_sum([own_x, later_x, own_y, later_y], flops=COVER)
        keep_eo, near_eo = ahead_sum(own_s, after(later_s, keep_eo), keep_eo, near_eo)
        own_x, later_x, out_x, own_y, later_y, out_y = core_split(
            [mine_p], [after(theirs_p, near_eo)], (keep_s, far_s)
        )
        near_eo = from_chip(near_eo, 1)
        out_x, out_y = from_x(out_x), from_y(out_y)
        joined_grad_rows = after(joined_grad_rows, own_x)
    else:
        grad_project = weight_grad(token_rows, joined_grad_rows)

        def owned(grad):
            part = lax.psum_scatter(grad, "fsdp", scatter_dimension=0, tiled=True)
            return lax.psum(part, "dp").astype(F32)

        own_project, own_output, own_expand, own_shrink = (
            owned(grad) for grad in (grad_project, grad_output, grad_expand, grad_shrink)
        )
        small = (sums_joined[0], sums1[0], sums1[1], sums1[2], sums_hidden[0], sums2[0], sums2[1], sums2[2])
        packed_grad = jnp.concatenate([v.reshape(parts, -1) for v in small], axis=1)
        shard = lax.psum(lax.psum_scatter(packed_grad.reshape(-1), "fsdp", scatter_dimension=0, tiled=True), "dp")
    token_grad = token_back(joined_grad_rows, project, first_grad)
    if pieces:
        half_p, half_e, half_o = project_weight.shape[1] // 2, expand_weight.shape[1] // 2, width // 2
        out_x, out_y = after((out_x, out_y), token_grad)
        own_x, later_x, own_y, later_y = middle_sum([own_x, later_x, out_x, own_y, later_y, out_y])
        later_x, later_y = from_y(later_x), from_x(later_y)
        keep_eo, far_eo = pair_sum(keep_eo, after(near_eo, own_x))
        far_eo = from_chip(far_eo, 2)
        later_x, later_y = after((later_x, later_y), keep_eo)
        keep_p, near_p, total_s = split_sum([own_x, later_x, own_y, later_y], more=FIRST // 4)
        near_p = from_chip(near_p, 1)
        total_seo = last_sum((total_s,), (keep_eo, after(far_eo, keep_p)))
        quarters_seo = from_plane(total_seo)
        keep_p, far_p = pair_sum(keep_p, after(near_p, total_seo))
        total_p = last_sum((keep_p, from_chip(far_p, 2)))
        quarters_p = from_plane(total_p)
        own_shrink, own_expand, own_output = place(
            pos,
            [total_seo, *after(quarters_seo, total_p)],
            (("stacked", 2 * width), ("halves", half_e), ("halves", half_o)),
        )
        own_project, *smalls = place(
            pos, [total_p, *after(quarters_p, own_expand)], (("halves", half_p), ("small", 128)), widths
        )
        smalls = [vector.reshape(-1) for vector in smalls]

    if not pieces:
        smalls, at = [], 0
        for size in widths:
            smalls.append(shard[at : at + size])
            at += size
    return (
        out_rows.reshape(pairs, seq, width),
        token_grad.reshape(pairs, seq, width),
        own_project,
        smalls[0],
        own_output,
        smalls[1],
        smalls[2],
        smalls[3],
        own_expand,
        smalls[4],
        own_shrink,
        smalls[5],
        smalls[6],
        smalls[7],
    )


def solution(mesh):
    rows3 = P(("dp", "fsdp"), None, None)
    matrix, vector = P("fsdp", None), P("fsdp")
    pieces = mesh.shape["dp"] == 4 and mesh.shape["fsdp"] == 8
    return jax.shard_map(
        functools.partial(local, pieces),
        mesh=mesh,
        in_specs=(
            rows3, P(("dp", "fsdp")), rows3,
            matrix, vector, matrix, vector, vector, vector,
            matrix, vector, matrix, vector, vector, vector,
        ),
        out_specs=(
            rows3, rows3,
            matrix, vector, matrix, vector, vector, vector,
            matrix, vector, matrix, vector, vector, vector,
        ),
        check_vma=False,
    )
```

```python
import functools

import jax
import jax.numpy as jnp
from jax import lax
from jax.experimental import pallas as pl
from jax.experimental.pallas import tpu as pltpu
from jax.sharding import PartitionSpec as P

HEADS = 12
HEAD_DIM = 64
REGIONS = 36
BF16 = jnp.bfloat16
F32 = jnp.float32

COVER = 100 * 10**9

NN = (((1,), (0,)), ((), ()))
NT = (((1,), (1,)), ((), ()))
TN = (((0,), (0,)), ((), ()))


def dot(left, right, dims=NN):
    return lax.dot_general(left, right, dims, preferred_element_type=F32)


def params(mebibytes):
    return pltpu.CompilerParams(vmem_limit_bytes=mebibytes * 1024 * 1024)


def cost(flops=0):
    return pl.CostEstimate(flops=flops, bytes_accessed=0, transcendentals=0)


def whole(shape, buffers=None):
    mode = None if buffers is None else pl.Buffered(buffers)
    return pl.BlockSpec(shape, lambda *at: (0,) * len(shape), pipeline_mode=mode)


HELD = pl.BlockSpec(memory_space=pltpu.VMEM)


def inside(shape, dtype=BF16):
    return pltpu.VMEM(shape, dtype)


def outside(shape, dtype=BF16):
    return pltpu.HBM(shape, dtype)


def in_vmem(values):
    return pltpu.with_memory_space_constraint(values, pltpu.VMEM)


def in_hbm(values):
    return pltpu.with_memory_space_constraint(values, pltpu.HBM)


def tile_of(size, most):
    return max(t for t in range(128, most + 1, 128) if size % t == 0)


def rows_of(count, most):
    fits = [t for t in range(16, most + 1, 16) if count % t == 0]
    return max(fits) if fits else count


CHIPS = (1, 3, 2)


def halves_copies(refs, into, pos, at, high, wide):
    half = wide // 2
    rows = high // 2
    for side in range(2):
        core = pos[1] if side == 0 else 1 - pos[1]
        shard = pos[0] * 2 + core
        yield refs[side], into.at[pl.ds(pl.multiple_of(shard * high, 16), high), :]
        for flip in range(4):
            buffer, first = refs[2 + side * 2 + (flip > 0)], max(flip - 1, 0) * 3 * rows
            up = pos[2] ^ (flip // 2)
            along = pos[3] ^ (flip % 2)
            for place, chip in enumerate(CHIPS):
                shard = (pos[0] ^ chip) * 2 + core
                to_row = pl.multiple_of(shard * high + up * rows, 16)
                to_column = pl.multiple_of(along * half, 128)
                yield (
                    buffer.at[pl.ds(first + place * rows, rows), pl.ds(at, half)],
                    into.at[pl.ds(to_row, rows), pl.ds(to_column, half)],
                )


def stacked_copies(refs, into, pos, high, wide):
    rows = high // 8
    own = pos[2] * 2 + pos[3]
    for side in range(2):
        core = pos[1] if side == 0 else 1 - pos[1]
        shard = pos[0] * 2 + core
        yield refs[side], into.at[pl.ds(pl.multiple_of(shard * high, 16), high), :]
        for place, chip in enumerate(CHIPS):
            shard = (pos[0] ^ chip) * 2 + core
            for plane in range(2):
                for block in range(2):
                    for part in range(2):
                        flip = block * (2 if part == plane else 1)
                        if plane:
                            flip = (1, 3)[block] if part == 0 else (2, 3)[block]
                        to_row = pl.multiple_of(shard * high + ((own ^ flip) * 2 + part) * rows, 16)
                        yield (
                            refs[2 + side * 2 + plane].at[
                                pl.ds((place * 2 + block) * rows, rows), pl.ds(part * wide, wide)
                            ],
                            into.at[pl.ds(to_row, rows), :],
                        )


def natural_copies(refs, into, pos):
    yield refs[0], into


class Weight:
    def __init__(self, shape, arrays, copies=natural_copies):
        self.shape, self.copies = shape, copies
        self.arrays = [in_vmem(array) for array in arrays]

    def specs(self):
        return [HELD] * len(self.arrays)

    def out(self):
        return inside(self.shape)

    def split(self, refs):
        return refs[: len(self.arrays)], refs[len(self.arrays) : -1], refs[-1]

    def arrive(self, refs, full, pos):
        @pl.when(pl.program_id(0) == 0)
        def _():
            for source, target in self.copies(refs, full, pos):
                target[...] = source[...]


def spread_kernel(pos, own, other, bias, hidden, rows, held):
    part = held.shape[2] * 3 // 4
    for at, chip in enumerate((0, *CHIPS)):
        held[(pos[0] ^ chip) * 2 + pos[1]] = own[at * 16 : at * 16 + 16].astype(F32)
        held[(pos[0] ^ chip) * 2 + 1 - pos[1]] = other[at * 16 : at * 16 + 16].astype(F32)
    bias[...] = jnp.zeros_like(bias)
    width = rows.shape[1]
    for shard in range(8):
        for at in range(2):
            to = (shard * 2 + at) * part
            to += width if to >= width else 0
            bias[0:1, to : to + part] = held[shard, at : at + 1, :part]
        for at in range(4):
            to = (shard * 4 + at) * part
            hidden[0:1, to : to + part] = held[shard, 5 + at : 6 + at, :part]
        to = shard * part
        rows[0:3, to : to + part] = held[shard, 2:5, :part]
        rows[3:6, to : to + part] = held[shard, 9:12, :part]


def spread(pos, shards, width, hidden_width):
    shapes = [(1, 3 * width), (1, hidden_width), (8, width)]
    return pl.pallas_call(
        spread_kernel,
        grid_spec=pltpu.PrefetchScalarGridSpec(
            num_scalar_prefetch=1,
            grid=(1,),
            in_specs=[whole((64, 128))] * 2,
            out_specs=[whole(shape) for shape in shapes],
            scratch_shapes=[pltpu.VMEM((8, 16, 128), F32)],
        ),
        out_shape=[jax.ShapeDtypeStruct(shape, F32) for shape in shapes],
        compiler_params=params(4),
        cost_estimate=cost(COVER),
        name="spread",
    )(pos, *shards)


def bundle_kernel(joined, first, second, hidden, out):
    part = out.shape[2] * 3 // 4
    out[...] = jnp.zeros_like(out)
    for shard in range(8):
        for at in range(2):
            of = (shard * 2 + at) * part
            out[shard, at : at + 1, :part] = joined[0:1, of : of + part]
        for at in range(4):
            of = (shard * 4 + at) * part
            out[shard, 5 + at : 6 + at, :part] = hidden[0:1, of : of + part]
        of = shard * part
        out[shard, 2:5, :part] = first[0:3, of : of + part]
        out[shard, 9:12, :part] = second[0:3, of : of + part]


def bundle(joined, first, second, hidden):
    return pl.pallas_call(
        bundle_kernel,
        out_shape=jax.ShapeDtypeStruct((8, 16, 128), F32),
        compiler_params=params(4),
        cost_estimate=cost(),
        name="bundle",
    )(joined, first, second, hidden)


def step_of(size):
    return pl.ds(pl.multiple_of(pl.program_id(0) * size, 16), size)


def columns_of(size):
    return pl.ds(pl.multiple_of(pl.program_id(0) * size, 128), size)


def join_kernel(pos, tokens, bias, *rest, weight, tile):
    pieces, (out, kept), (full, sem) = rest[: len(weight.arrays)], rest[-4:-2], rest[-2:]
    weight.arrive(pieces, full, pos)
    write = pltpu.make_async_copy(full, kept, sem)

    @pl.when(pl.program_id(0) == 0)
    def _():
        write.start()

    out[...] = (dot(tokens[...], full[:, columns_of(tile)]) + bias[...]).astype(BF16)

    @pl.when(pl.program_id(0) == pl.num_programs(0) - 1)
    def _():
        write.wait()


def join(pos, token_rows, weight, bias):
    rows, width = token_rows.shape
    columns = weight.shape[1]
    tile = tile_of(columns, 768)
    return pl.pallas_call(
        functools.partial(join_kernel, weight=weight, tile=tile),
        grid_spec=pltpu.PrefetchScalarGridSpec(
            num_scalar_prefetch=1,
            grid=(columns // tile,),
            in_specs=[whole((rows, width), 1), pl.BlockSpec((1, tile), lambda i, p: (0, i))] + weight.specs(),
            out_specs=[pl.BlockSpec((rows, tile), lambda i, p: (0, i)), pl.BlockSpec(memory_space=pltpu.HBM)],
            scratch_shapes=[pltpu.VMEM(weight.shape, BF16), pltpu.SemaphoreType.DMA(())],
        ),
        out_shape=[outside((rows, columns)), outside(weight.shape)],
        compiler_params=params(15),
        cost_estimate=cost(),
        name="join",
    )(pos, token_rows, bias, *weight.arrays)


def head_stack(block, low_half, padded):
    rows = block.shape[0]
    filler = jnp.zeros((padded - rows, block.shape[1]), F32)
    first = jnp.where(low_half, block, 0.0)
    second = jnp.where(low_half, 0.0, block)
    return jnp.concatenate([first, filler, second, filler], axis=0).astype(BF16)


def attend_kernel(captions, joined, context, probs):
    seq = joined.shape[1]
    width = context.shape[2]
    padded = probs.shape[3] // 2
    valid = captions[pl.program_id(0)] + 2 + REGIONS
    keep = lax.broadcasted_iota(jnp.int32, (seq, 2 * padded), 0) < valid
    low_half = lax.broadcasted_iota(jnp.int32, (1, 2 * HEAD_DIM), 1) < HEAD_DIM
    places = [pair * 2 * HEAD_DIM for pair in range(HEADS // 2)]
    scores = []
    for at in places:
        query = joined[0, :, at : at + 2 * HEAD_DIM].astype(F32)
        keys = joined[0, :, width + at : width + at + 2 * HEAD_DIM]
        scores.append(dot(keys, head_stack(query, low_half, padded), NT) * HEAD_DIM ** (-0.5))
    probabilities = []
    for score in scores:
        score = jnp.where(keep, score, -1000000000.0)
        grown = jnp.exp(score - jnp.max(score, axis=0, keepdims=True))
        total = jnp.sum(grown, axis=0, keepdims=True)
        probabilities.append((grown * (1.0 / total)).astype(BF16))
    for pair, at in enumerate(places):
        values = joined[0, :, 2 * width + at : 2 * width + at + 2 * HEAD_DIM]
        mixed = dot(probabilities[pair], values, TN)
        probs[0, pair] = probabilities[pair]
        context[0, :, at : at + 2 * HEAD_DIM] = jnp.where(
            low_half, mixed[:seq], mixed[padded : padded + seq]
        ).astype(BF16)


def attend(joined, captions):
    pairs, seq, columns = joined.shape
    width = columns // 3
    padded = (seq + 127) // 128 * 128
    return pl.pallas_call(
        attend_kernel,
        grid_spec=pltpu.PrefetchScalarGridSpec(
            num_scalar_prefetch=1,
            grid=(pairs,),
            in_specs=[pl.BlockSpec((1, seq, columns), lambda i, c: (i, 0, 0))],
            out_specs=[
                pl.BlockSpec((1, seq, width), lambda i, c: (i, 0, 0)),
                pl.BlockSpec((1, HEADS // 2, seq, 2 * padded), lambda i, c: (i, 0, 0, 0)),
            ],
        ),
        out_shape=[
            inside((pairs, seq, width)),
            outside((pairs, HEADS // 2, seq, 2 * padded)),
        ],
        compiler_params=params(8),
        cost_estimate=cost(),
        name="attend",
    )(captions, in_hbm(joined))


def attend_back_kernel(joined, probs, grads, out, sums):
    seq = joined.shape[1]
    width = grads.shape[2]
    padded = probs.shape[3] // 2
    low_half = lax.broadcasted_iota(jnp.int32, (1, 2 * HEAD_DIM), 1) < HEAD_DIM

    @pl.when(pl.program_id(0) == 0)
    def _():
        sums[...] = jnp.zeros_like(sums)

    places = [pair * 2 * HEAD_DIM for pair in range(HEADS // 2)]
    prob_grads, grad_stacks = [], []
    for at in places:
        values = joined[0, :, 2 * width + at : 2 * width + at + 2 * HEAD_DIM]
        grad_stacks.append(head_stack(grads[0, :, at : at + 2 * HEAD_DIM].astype(F32), low_half, padded))
        prob_grads.append(dot(values, grad_stacks[-1], NT))
    score_grads = []
    for pair, prob_grad in enumerate(prob_grads):
        prob = probs[0, pair].astype(F32)
        row_dot = jnp.sum(prob * prob_grad, axis=0, keepdims=True)
        score_grads.append((prob * (prob_grad - row_dot) * HEAD_DIM ** (-0.5)).astype(BF16))
    results = []
    for pair, at in enumerate(places):
        query = joined[0, :, at : at + 2 * HEAD_DIM].astype(F32)
        keys = joined[0, :, width + at : width + at + 2 * HEAD_DIM]
        mixed = dot(score_grads[pair], keys, TN)
        query_grad = jnp.where(low_half, mixed[:seq], mixed[padded : padded + seq])
        keys_grad = dot(score_grads[pair], head_stack(query, low_half, padded))
        results.append((query_grad, keys_grad, dot(probs[0, pair], grad_stacks[pair])))
    for at, blocks in zip(places, results):
        for part, block in enumerate(blocks):
            out[0, :, part * width + at : part * width + at + 2 * HEAD_DIM] = block.astype(BF16)
            if part != 1:
                to = part // 2 * width + at
                sums[:, to : to + 2 * HEAD_DIM] += jnp.sum(block, axis=0, keepdims=True)


def attend_back(joined, probs, grads):
    pairs, seq, columns = joined.shape
    width = columns // 3
    padded = probs.shape[3] // 2
    return pl.pallas_call(
        attend_back_kernel,
        grid=(pairs,),
        in_specs=[
            pl.BlockSpec((1, seq, columns), lambda i: (i, 0, 0)),
            pl.BlockSpec((1, HEADS // 2, seq, 2 * padded), lambda i: (i, 0, 0, 0)),
            pl.BlockSpec((1, seq, width), lambda i: (i, 0, 0)),
        ],
        out_specs=[
            pl.BlockSpec((1, seq, columns), lambda i: (i, 0, 0)),
            pl.BlockSpec((1, 2 * width), lambda i: (0, 0)),
        ],
        out_shape=[
            inside((pairs, seq, columns)),
            jax.ShapeDtypeStruct((1, 2 * width), F32),
        ],
        compiler_params=params(10),
        cost_estimate=cost(),
        name="attend_back",
    )(in_hbm(joined), in_hbm(probs), in_vmem(grads))


def norm_parts(values):
    centred = values - jnp.mean(values, axis=-1, keepdims=True)
    spread = jnp.mean(centred * centred, axis=-1, keepdims=True)
    scale = lax.rsqrt(spread + 1e-05)
    return centred * scale, scale


def norm_back(upstream, unit, scale, gain):
    scaled = upstream * gain
    return scale * (
        scaled
        - jnp.mean(scaled, axis=-1, keepdims=True)
        - unit * jnp.mean(scaled * unit, axis=-1, keepdims=True)
    )


def add_sums(sums, rows):
    for at, values in enumerate(rows):
        sums[at : at + 1, :] += jnp.sum(values, axis=0, keepdims=True)


def chunked(count, load, use):
    ready = load(0)
    for at in range(count):
        following = load(at + 1) if at + 1 < count else None
        use(at, ready)
        ready = following


def chunk_slices(rows, most):
    tile = rows_of(rows, most)
    return [slice(at, at + tile) for at in range(0, rows, tile)]


def first_kernel(pos, context, bias, tokens, gain, shift, *rest, weight):
    pieces, (unit, scale, normed_low), full = weight.split(rest)
    weight.arrive(pieces, full, pos)
    chunks = chunk_slices(tokens.shape[0], 416)

    def normalise(at, branch):
        rows = chunks[at]
        unit_rows, scale_rows = norm_parts(tokens[rows, :].astype(F32) + (branch + bias[...]))
        unit[rows, :] = unit_rows
        scale[rows, :] = scale_rows
        normed_low[rows, :] = (unit_rows * gain[...] + shift[...]).astype(BF16)

    chunked(len(chunks), lambda at: dot(context[chunks[at], :], full[...]), normalise)


def first_norm(pos, context, weight, bias, token_rows, gain, shift):
    rows, width = token_rows.shape
    row = whole((1, width))
    return pl.pallas_call(
        functools.partial(first_kernel, weight=weight),
        grid_spec=pltpu.PrefetchScalarGridSpec(
            num_scalar_prefetch=1,
            grid=(1,),
            in_specs=[HELD, row, HELD, row, row] + weight.specs(),
            out_specs=[HELD] * 4,
        ),
        out_shape=[inside((rows, width), F32), inside((rows, 1), F32), inside((rows, width)), weight.out()],
        compiler_params=params(10),
        cost_estimate=cost(),
        name="first_norm",
    )(pos, in_vmem(context), bias, in_vmem(token_rows), gain, shift, *weight.arrays)


def expand_kernel(pos, normed_low, bias, *rest, weight, tile):
    pieces, (active, slope), full = weight.split(rest)
    weight.arrive(pieces, full, pos)
    at = columns_of(tile)
    expand = dot(normed_low[...], full[:, at]) + bias[...]
    half = 0.5 * (1.0 + lax.erf(expand * 0.7071067811865476))
    active[:, at] = (expand * half).astype(BF16)
    slope[:, at] = (half + expand * jnp.exp(-0.5 * expand * expand) * 0.3989422804014327).astype(BF16)


def expand_act(pos, normed_low, weight, bias):
    rows, width = normed_low.shape
    columns = weight.shape[1]
    tile = tile_of(columns, 768)
    return pl.pallas_call(
        functools.partial(expand_kernel, weight=weight, tile=tile),
        grid_spec=pltpu.PrefetchScalarGridSpec(
            num_scalar_prefetch=1,
            grid=(columns // tile,),
            in_specs=[HELD, pl.BlockSpec((1, tile), lambda i, p: (0, i))] + weight.specs(),
            out_specs=[HELD] * 3,
        ),
        out_shape=[inside((rows, columns))] * 2 + [weight.out()],
        compiler_params=params(12),
        cost_estimate=cost(),
        name="expand_act",
    )(pos, in_vmem(normed_low), bias, *weight.arrays)


def second_kernel(pos, captions, active, bias, unit, gain, shift, gain2, shift2, cotangent, *rest, weight, seq):
    pieces, (out, low, grad, sums), full, (held, sems) = *weight.split(rest[:-2]), rest[-2:]
    weight.arrive(pieces, full, pos)
    sums[...] = jnp.zeros_like(sums)
    chunks = chunk_slices(held.shape[0], 208)
    writes = [
        pltpu.make_async_copy(held.at[rows, :], out.at[rows, :], sems.at[at]) for at, rows in enumerate(chunks)
    ]

    def normalise(at, shrunk):
        rows = chunks[at]
        normed = unit[rows, :] * gain[...] + shift[...]
        unit2, scale2 = norm_parts(normed + (shrunk + bias[...]))
        held[rows, :] = (unit2 * gain2[...] + shift2[...]).astype(BF16)
        writes[at].start()
        row = lax.broadcasted_iota(jnp.int32, (rows.stop - rows.start, 1), 0) + rows.start
        live = jnp.zeros(row.shape, jnp.bool_)
        for pair in range(rows.start // seq, (rows.stop - 1) // seq + 1):
            live = live | ((row >= pair * seq) & (row < pair * seq + captions[pair] + 2 + REGIONS))
        upstream = jnp.where(live, cotangent[rows, :].astype(F32), 0.0)
        second = norm_back(upstream, unit2, scale2, gain2[...])
        grad[rows, :] = second
        low[rows, :] = second.astype(BF16)
        add_sums(sums, (second, upstream * unit2, upstream))

    chunked(len(chunks), lambda at: dot(active[chunks[at], :], full[...]), normalise)
    for write in writes:
        write.wait()


def second_norm(pos, captions, active, weight, bias, unit, gain, shift, gain2, shift2, cotangent, seq):
    rows, width = unit.shape
    row = whole((1, width))
    return pl.pallas_call(
        functools.partial(second_kernel, weight=weight, seq=seq),
        grid_spec=pltpu.PrefetchScalarGridSpec(
            num_scalar_prefetch=2,
            grid=(1,),
            in_specs=[HELD, row, HELD, row, row, row, row, HELD] + weight.specs(),
            out_specs=[pl.BlockSpec(memory_space=pltpu.HBM), HELD, HELD, whole((8, width)), HELD],
            scratch_shapes=[pltpu.VMEM((rows, width), BF16), pltpu.SemaphoreType.DMA((rows // 16,))],
        ),
        out_shape=[
            outside((rows, width)),
            inside((rows, width)),
            inside((rows, width), F32),
            jax.ShapeDtypeStruct((8, width), F32),
            weight.out(),
        ],
        compiler_params=params(12),
        cost_estimate=cost(),
        name="second_norm",
    )(pos, captions, in_vmem(active), bias, in_vmem(unit), gain, shift, gain2, shift2, in_vmem(cotangent), *weight.arrays)


def hidden_back_kernel(low, weight, slope, out, sums):
    at = columns_of(sums.shape[1])
    grad = dot(low[...], weight[at, :], NT) * slope[:, at].astype(F32)
    out[:, at] = grad.astype(BF16)
    sums[...] = jnp.sum(grad, axis=0, keepdims=True)


def hidden_back(low, weight, slope):
    rows, width = low.shape
    hidden = weight.shape[0]
    tile = tile_of(hidden, 768)
    return pl.pallas_call(
        hidden_back_kernel,
        grid=(hidden // tile,),
        in_specs=[HELD] * 3,
        out_specs=[HELD, pl.BlockSpec((1, tile), lambda i: (0, i))],
        out_shape=[inside((rows, hidden)), jax.ShapeDtypeStruct((1, hidden), F32)],
        compiler_params=params(10),
        cost_estimate=cost(),
        name="hidden_back",
    )(in_vmem(low), in_vmem(weight), in_vmem(slope))


def first_back_kernel(hidden, weight, second, unit, scale, gain, out_weight, grad, low, context_grad, sums):
    sums[...] = jnp.zeros_like(sums)
    chunks = chunk_slices(grad.shape[0], 416)
    waiting = []

    def pass_on():
        rows, first_low = waiting.pop()
        context_grad[rows, :] = dot(first_low, out_weight[...], NT).astype(BF16)

    def normalise(at, product):
        rows = chunks[at]
        unit_rows = unit[rows, :]
        normed_grad = product + second[rows, :]
        first = norm_back(normed_grad, unit_rows, scale[rows, :], gain[...])
        grad[rows, :] = first
        first_low = first.astype(BF16)
        low[rows, :] = first_low
        add_sums(sums, (first, normed_grad * unit_rows, normed_grad))
        if waiting:
            pass_on()
        waiting.append((rows, first_low))

    chunked(len(chunks), lambda at: dot(hidden[chunks[at], :], weight[...], NT), normalise)
    pass_on()


def first_back(hidden, weight, second, unit, scale, gain, out_weight):
    rows, width = second.shape
    return pl.pallas_call(
        first_back_kernel,
        grid=(1,),
        in_specs=[HELD] * 5 + [whole((1, width)), HELD],
        out_specs=[HELD, HELD, HELD, whole((8, width))],
        out_shape=[
            inside((rows, width), F32),
            inside((rows, width)),
            inside((rows, width)),
            jax.ShapeDtypeStruct((8, width), F32),
        ],
        compiler_params=params(13),
        cost_estimate=cost(COVER),
        name="first_back",
    )(in_vmem(hidden), in_vmem(weight), in_vmem(second), in_vmem(unit), in_vmem(scale), gain, in_vmem(out_weight))


def token_back_kernel(grads, weight, first, out):
    at = step_of(out.shape[0])
    out[...] = dot(grads[at, :], weight[...], NT) + first[at, :]


def token_back(grads, weight, first):
    rows, width = first.shape
    tile = rows_of(rows, 416)
    return pl.pallas_call(
        token_back_kernel,
        grid=(rows // tile,),
        in_specs=[HELD] * 3,
        out_specs=pl.BlockSpec((tile, width), lambda i: (i, 0)),
        out_shape=outside((rows, width), F32),
        compiler_params=params(9),
        cost_estimate=cost(),
        name="token_back",
    )(in_vmem(grads), in_vmem(weight), in_vmem(first))


def weight_grad_kernel(left, right, out):
    out[...] = dot(left[...], right[...], TN).astype(BF16)


def weight_grad(left, right):
    rows, height = left.shape
    columns = right.shape[1]
    tile = tile_of(columns, 768)
    high = tile_of(height, 768)
    return pl.pallas_call(
        weight_grad_kernel,
        grid=(height // high, columns // tile),
        in_specs=[
            pl.BlockSpec((rows, high), lambda i, j: (0, i)),
            pl.BlockSpec((rows, tile), lambda i, j: (0, j)),
        ],
        out_specs=pl.BlockSpec((high, tile), lambda i, j: (i, j)),
        out_shape=outside((height, columns)),
        compiler_params=params(24),
        cost_estimate=cost(),
        name="weight_grad",
    )(left, right)


def regroup_kernel(values, out):
    part = values.shape[1] // 8
    blocks = [values[:, shard * part : (shard + 1) * part] for shard in (0, 2, 4, 6, 1, 3, 5, 7)]
    out[...] = jnp.concatenate(blocks, axis=1)


def regroup(values):
    return held_call(regroup_kernel, "regroup", [values.shape], [values])[0]


def by_core(pos, mine, theirs, store):
    store(mine, pos[1])
    store(theirs, 1 - pos[1])


def halves_grad_kernel(pos, left, right, *rest):
    extra, (mine, theirs) = (rest[0] if len(rest) == 3 else None), rest[-2:]
    along, half = pl.program_id(0), right.shape[1] // 2
    columns, high, rows = right[:, columns_of(half)], left.shape[1] // 2, mine.shape[3]

    def store(out, core):
        grads = dot(left[:, pl.ds(pl.multiple_of(core * high, 128), high)], columns, TN)
        for chip in range(4):
            for up in range(2):
                at = (chip * 2 + up) * rows
                to = (chip ^ pos[0], up ^ pos[2], along ^ pos[3])
                out[(*to, slice(None), slice(0, half))] = grads[at : at + rows].astype(BF16)
                if extra is not None:
                    out[(*to, slice(None), slice(half, None))] = jnp.zeros((rows, 128), BF16)
                    out[(*to, slice(0, 16), slice(half, None))] = extra[chip * 2 + core].astype(BF16)

    by_core(pos, mine, theirs, store)


def stacked_grad_kernel(pos, left, right, mine, theirs):
    high, rows, wide = left.shape[1] // 8, mine.shape[3], right.shape[1]

    def store(out, core):
        for part in range(2):
            chip = pl.program_id(0) * 2 + part
            columns = pl.ds(pl.multiple_of((chip * 2 + core) * high, 128), high)
            grads = dot(left[:, columns], right[...], TN)
            for quarter in range(4):
                for side in range(2):
                    at = (quarter * 2 + side) * rows
                    to = (chip ^ pos[0], (quarter // 2) ^ pos[2], (quarter % 2) ^ pos[3])
                    block = grads[at : at + rows].astype(BF16)
                    out[(*to, slice(None), slice(side * wide, (side + 1) * wide))] = block

    by_core(pos, mine, theirs, store)


def pieces_grad(kernel, name, pos, left, right, shape, extra=()):
    out = inside((4, 2, 2) + shape)
    return pl.pallas_call(
        kernel,
        grid_spec=pltpu.PrefetchScalarGridSpec(
            num_scalar_prefetch=1,
            grid=(2,),
            in_specs=[HELD, HELD] + [whole(array.shape) for array in extra],
            out_specs=[HELD, HELD],
        ),
        out_shape=[out, out],
        compiler_params=params(13),
        cost_estimate=cost(),
        name=name,
    )(pos, in_vmem(left), in_vmem(right), *extra)


def halves_grad(pos, left, right, extra=None):
    shape = (left.shape[1] // 16, right.shape[1] // 2 + (0 if extra is None else 128))
    more = () if extra is None else (extra,)
    return pieces_grad(halves_grad_kernel, "halves_grad", pos, left, right, shape, more)


def stacked_grad(pos, left, right):
    shape = (left.shape[1] // 64, 2 * right.shape[1])
    return pieces_grad(stacked_grad_kernel, "stacked_grad", pos, left, right, shape)


def held_call(kernel, name, outs, values, flops=0):
    return pl.pallas_call(
        kernel,
        in_specs=[HELD] * len(values),
        out_specs=[HELD] * len(outs),
        out_shape=[inside(out) for out in outs],
        compiler_params=params(4),
        cost_estimate=cost(flops),
        name=name,
    )(*map(in_vmem, values))


def add(*terms):
    total = terms[0].astype(F32)
    for term in terms[1:]:
        total += term.astype(F32)
    return total


FIRST = 1024


def shrink_sum_kernel(mine, theirs, keep, near, kept, send):
    for chip in range(4):
        for flip in range(4):
            pick = (chip, flip // 2, flip % 2)
            total = add(mine[pick], theirs[pick]).astype(BF16)
            (keep, near)[chip % 2][chip // 2, flip] = total[:, :FIRST]
            (kept, send)[flip % 2][flip // 2, chip] = total[:, FIRST:]


def shrink_sum(mine, theirs):
    rows, wide = mine.shape[3:]
    outs = [(2, 4, rows, FIRST)] * 2 + [(2, 4, rows, wide - FIRST)] * 2
    return held_call(shrink_sum_kernel, "shrink_sum", outs, [mine, theirs])


def core_split_kernel(*refs, count):
    outs = refs[-6:]
    for half in range(2):
        own, later, send = outs[3 * half : 3 * half + 3]
        first = 1 + half
        for flip, out in ((0, own), (3 - first, later), (first, send.at[0]), (3, send.at[1])):
            at = 0
            for mine, theirs in zip(refs[:count], refs[count : 2 * count]):
                wide = mine.shape[4]
                for chip in range(2):
                    pick = (2 * half + chip, flip // 2, flip % 2)
                    out[chip, :, at : at + wide] = add(mine[pick], theirs[pick]).astype(BF16)
                at += wide
            if len(refs) > 2 * count + 6:
                near, far = refs[2 * count : 2 * count + 2]
                wide = near.shape[2] // 4
                for chip in range(2):
                    columns = slice((2 * half + chip) * wide, (2 * half + chip + 1) * wide)
                    out[chip, :, at:] = add(near[flip, :, columns], far[flip, :, columns]).astype(BF16)


def core_split(mine, theirs, more=()):
    shape = (2, mine[0].shape[3], sum(m.shape[4] for m in mine) + sum(m.shape[2] // 8 for m in more))
    kernel = functools.partial(core_split_kernel, count=len(mine))
    return held_call(kernel, "core_split", [shape, shape, (2,) + shape] * 2, [*mine, *theirs, *more])


def middle_sum_kernel(*refs):
    for half in range(2):
        own, later, received = refs[3 * half : 3 * half + 3]
        refs[6 + 2 * half][...] = add(own[...], received[0]).astype(BF16)
        refs[7 + 2 * half][...] = add(later[...], received[1]).astype(BF16)


def middle_sum(parts):
    return held_call(middle_sum_kernel, "middle_sum", [parts[0].shape] * 4, parts)


def split_sum_kernel(own, received, own_too, received_too, keep, near, *rest):
    for chip in range(4):
        one, two = (own, received) if chip < 2 else (own_too, received_too)
        total = add(one[chip % 2], two[chip % 2]).astype(BF16)
        wide = keep.shape[2]
        (keep, near)[chip % 2][chip // 2] = total[:, :wide]
        if rest:
            part = total.shape[1] - wide
            rest[0][:, chip * part : (chip + 1) * part] = total[:, wide:]


def split_sum(parts, more=0, flops=0):
    _, rows, wide = parts[0].shape
    outs = [(2, rows, wide - more)] * 2 + ([(rows, 4 * more)] if more else [])
    return held_call(split_sum_kernel, "split_sum", outs, parts, flops)


def ahead_sum_kernel(one, two, keep, near, keep_out, near_out):
    wide = one.shape[2]
    for chip in range(4):
        source, out = (keep, keep_out) if chip % 2 == 0 else (near, near_out)
        out[chip // 2, :, :wide] = add(one[chip], two[chip]).astype(BF16)
        out[chip // 2, :, wide:] = source[chip // 2]


def ahead_sum(one, two, keep, near):
    shape = keep.shape[:2] + (keep.shape[2] + one.shape[2],)
    return held_call(ahead_sum_kernel, "ahead_sum", [shape] * 2, [one, two, keep, near])


def pair_sum_kernel(keep, received, one, two):
    one[...] = add(keep[0], received[0]).astype(BF16)
    two[...] = add(keep[1], received[1]).astype(BF16)


def pair_sum(keep, received, flops=0):
    return held_call(pair_sum_kernel, "pair_sum", [keep.shape[1:]] * 2, [keep, received], flops)


def last_sum_kernel(*refs, counts):
    out, at = refs[-1], 0
    for count in counts:
        terms, refs = refs[:count], refs[count:]
        wide = terms[0].shape[1]
        out[:, at : at + wide] = add(*(term[...] for term in terms)).astype(BF16)
        at += wide


def last_sum(*groups):
    kernel = functools.partial(last_sum_kernel, counts=[len(group) for group in groups])
    shape = (groups[0][0].shape[0], sum(group[0].shape[1] for group in groups))
    return held_call(kernel, "last_sum", [shape], [part for group in groups for part in group])[0]


def place_kernel(pos, *refs, layout):
    parts, outs = refs[:4], refs[4:]
    rows = parts[0].shape[0]
    for flip, part in enumerate(parts):
        up, along = pos[2] ^ (flip // 2), pos[3] ^ (flip % 2)
        at = 0
        for (kind, wide), out in zip(layout, outs):
            if kind == "halves":
                to_row = pl.multiple_of(up * rows, 16)
                to_column = pl.multiple_of(along * wide, 128)
                out[pl.ds(to_row, rows), pl.ds(to_column, wide)] = part[:, at : at + wide].astype(F32)
            elif kind == "stacked":
                for side in range(2):
                    to_row = pl.multiple_of(((up * 2 + along) * 2 + side) * rows, 16)
                    from_column = at + side * (wide // 2)
                    out[pl.ds(to_row, rows), :] = part[:, from_column : from_column + wide // 2].astype(F32)
            else:

                @pl.when((up == 0) & (along == 0))
                def _(part=part, at=at):
                    row = 0
                    for vector in outs[len(layout) - 1 :]:
                        for to in range(0, vector.shape[1], 96):
                            vector[:, to : to + 96] = part[row : row + 1, at : at + 96].astype(F32)
                            row += 1

            at += wide


def place(pos, parts, layout, sizes=()):
    rows = parts[0].shape[0]
    shapes = {
        "halves": lambda wide: (2 * rows, 2 * wide),
        "stacked": lambda wide: (8 * rows, wide // 2),
    }
    outs = [jax.ShapeDtypeStruct(shapes[kind](wide), F32) for kind, wide in layout if kind != "small"]
    outs += [jax.ShapeDtypeStruct((1, size), F32) for size in sizes]
    return pl.pallas_call(
        functools.partial(place_kernel, layout=layout),
        grid_spec=pltpu.PrefetchScalarGridSpec(
            num_scalar_prefetch=1,
            grid=(1,),
            in_specs=[HELD] * 4,
            out_specs=[whole(out.shape, 1) for out in outs],
        ),
        out_shape=outs,
        compiler_params=params(10),
        cost_estimate=cost(),
        name="place",
    )(pos, *map(in_vmem, parts))


def from_core(values):
    return lax.ppermute(values, "fsdp", [(i, i ^ 1) for i in range(8)])


def from_plane(values):
    parts = values if isinstance(values, (list, tuple)) else [values] * 3
    return [
        lax.ppermute(part, "dp", [(i, i ^ flip) for i in range(4)]) for flip, part in zip((1, 2, 3), parts)
    ]


def from_x(values):
    return lax.ppermute(values, "dp", [(i, i ^ 1) for i in range(4)])


def from_y(values):
    return lax.ppermute(values, "dp", [(i, i ^ 2) for i in range(4)])


def from_chips(values):
    return [from_chip(values, flip) for flip in CHIPS]


def from_chip(values, flip):
    return lax.ppermute(values, "fsdp", [(i, i ^ (2 * flip)) for i in range(8)])


def below_kernel(*refs):
    at = 0
    for ref in refs[:-1]:
        rows, wide = ref.shape[0], refs[-1].shape[1]
        refs[-1][at : at + rows] = ref[:, :wide]
        at += rows


def below(*parts, wide=None, flops=0):
    rows = sum(part.shape[0] for part in parts)
    return pl.pallas_call(
        below_kernel,
        in_specs=[HELD] * len(parts),
        out_specs=HELD,
        out_shape=inside((rows, wide or parts[0].shape[1])),
        compiler_params=params(4),
        cost_estimate=cost(flops),
        name="below",
    )(*map(in_vmem, parts))


def pick_kernel(pos, shard, out):
    rows, wide = out.shape[0] // 2, shard.shape[1]
    own = pos[2] * 2 + pos[3]
    for block, part, flip in ((0, 0, 0), (0, 1, 0), (1, 0, 2), (1, 1, 1)):
        from_row = pl.multiple_of(((own ^ flip) * 2 + part) * rows, 16)
        out[block * rows : (block + 1) * rows, part * wide : (part + 1) * wide] = shard[pl.ds(from_row, rows), :]


def pick(pos, shard):
    return pl.pallas_call(
        pick_kernel,
        grid_spec=pltpu.PrefetchScalarGridSpec(
            num_scalar_prefetch=1, grid=(1,), in_specs=[whole(shard.shape, 1)], out_specs=HELD
        ),
        out_shape=inside((shard.shape[0] // 4, 2 * shard.shape[1])),
        compiler_params=params(4),
        cost_estimate=cost(),
        name="pick",
    )(pos, shard)


def left_right_kernel(whole_ref, left, right):
    half = left.shape[1]
    left[...] = whole_ref[:, :half]
    right[...] = whole_ref[:, half:]


def left_right(values):
    rows, wide = values.shape
    return held_call(left_right_kernel, "left_right", [(rows, wide // 2)] * 2, [values])


def beside_kernel(left, right, out):
    half = left.shape[1]
    out[:, :half] = left[...]
    out[:, half:] = right[...]


def beside(left, right):
    rows, wide = left.shape
    return held_call(beside_kernel, "beside", [(rows, 2 * wide)], [left, right])[0]


def after(values, *others):
    return lax.optimization_barrier((values, others))[0]


def half_of(pos, shard):
    rows, wide = shard.shape[0] // 2, shard.shape[1] // 2
    return lax.dynamic_slice(shard, (pos[2] * rows, pos[3] * wide), (rows, wide))


def both_cores(pieces):
    return [*pieces, *(from_core(piece) for piece in pieces)]


def gather(values):
    return lax.all_gather(values, "fsdp", axis=0, tiled=True)


def local(
    pieces,
    tokens,
    captions,
    cotangent,
    project_weight,
    project_bias,
    output_weight,
    output_bias,
    first_gain,
    first_shift,
    expand_weight,
    expand_bias,
    shrink_weight,
    shrink_bias,
    second_gain,
    second_shift,
):
    pairs, seq, width = tokens.shape
    rows = pairs * seq
    parts = lax.axis_size("fsdp")
    token_rows = tokens.reshape(rows, width)
    cot_rows = cotangent.reshape(rows, width)

    vectors = (project_bias, output_bias, first_gain, first_shift, expand_bias, shrink_bias, second_gain, second_shift)
    widths = [vector.shape[0] for vector in vectors]
    replica, part = lax.axis_index("dp"), lax.axis_index("fsdp")
    pos = jnp.stack([part // 2, part % 2, replica // 2, replica % 2]).astype(jnp.int32)
    shapes = [(parts * shard.shape[0], shard.shape[1]) for shard in (project_weight, output_weight, expand_weight, shrink_weight)]
    if pieces:
        chips_p = from_chips(half_of(pos, project_weight))
        sibling_p = from_core(project_weight)
        held = jnp.concatenate([vector.reshape(-1, 96) for vector in vectors], axis=0)
        held = jnp.pad(held, ((0, 4), (0, 32)))
        quarter_e = [half_of(pos, expand_weight), half_of(pos, output_weight), jnp.pad(held, ((0, 32), (0, 0)))]
        quarter_e = jnp.concatenate(quarter_e, axis=1)
        wide_e = quarter_e.shape[1] - 128
        quarter_s, token_group = pick(pos, shrink_weight), regroup(token_rows)
        chips_p = after(chips_p, sibling_p, quarter_e, quarter_s, token_group)
        mine_p = below(*chips_p)
        quarter_e = after(quarter_e, *chips_p)
        far_e = from_chip(quarter_e, 2)
        near_e = [from_chip(quarter_e, 1), from_chip(far_e, 1)]
        plane_p = from_plane(mine_p)
        plane_p = below(*plane_p, flops=COVER)
        near_e = after(near_e, plane_p)
        other_p = [from_core(mine_p), from_core(plane_p)]

        def halves(shape, shard, sibling, group, at):
            copies = functools.partial(halves_copies, at=at, high=shard.shape[0], wide=shard.shape[1])
            return Weight(shape, [shard, sibling, *group], copies)

        project = halves(shapes[0], project_weight, sibling_p, (mine_p, plane_p, *other_p), 0)
        quarter_s = after(quarter_s, plane_p)
        far_s = from_chip(quarter_s, 2)
        mine_e = below(*near_e, far_e, wide=wide_e)
        plane_e = from_plane(mine_e)
        held = jnp.concatenate([held, *(chip[:16, wide_e:] for chip in (*near_e, far_e))], axis=0)
        held = after(held, mine_e)
        bias_full, hidden_bias, rows6 = spread(pos, [held, from_core(held)], width, expand_weight.shape[1])
        out_bias, gain1, shift1, down_bias, gain2, shift2 = (rows6[at : at + 1] for at in range(6))
    else:
        project, output, expand, shrink = (
            Weight(shape, [gather(shard)])
            for shape, shard in zip(shapes, (project_weight, output_weight, expand_weight, shrink_weight))
        )
        packed = gather(jnp.concatenate(vectors)[None, :])
        full, at = [], 0
        for size in widths:
            full.append(packed[:, at : at + size].reshape(1, parts * size).astype(F32))
            at += size
        bias_row, out_bias, gain1, shift1, hidden_bias, down_bias, gain2, shift2 = full
        bias_full = jnp.concatenate([bias_row[:, :width], jnp.zeros((1, width), F32), bias_row[:, width:]], axis=1)

    joined, project = join(pos, token_rows, project, bias_full)
    joined3 = joined.reshape(pairs, seq, 3 * width)
    if pieces:
        near_s = from_chip(after(quarter_s, joined), 1)
    context, probs = attend(joined3, captions)
    context_rows = context.reshape(rows, width)
    if pieces:
        far_s = after(far_s, context)
        near_s = [near_s, from_chip(far_s, 1)]
        context_group = regroup(context_rows)
        plane_e = below(*after(plane_e, far_s, context_group))
        mine_s = below(*after(near_s, plane_e), far_s, flops=COVER)
        left_s, right_s = left_right(mine_s)
        plane_s = [from_x(left_s), from_y(right_s)]
        context_rows = after(context_rows, mine_s)
        group_e = (mine_e, plane_e, *after([from_core(mine_e), from_core(plane_e)], mine_s))
        sibling_e = from_core(after(expand_weight, joined))
        sibling_o = from_core(after(output_weight, joined))
        expand = halves(shapes[2], expand_weight, sibling_e, group_e, 0)
        output = halves(shapes[1], output_weight, sibling_o, group_e, expand_weight.shape[1] // 2)
    unit1, scale1, normed_low, output = first_norm(pos, context_rows, output, out_bias, token_rows, gain1, shift1)
    active, slope, expand = expand_act(pos, normed_low, expand, hidden_bias)
    if pieces:
        plane_s = beside(*after(plane_s, active))
        normed_group = regroup(after(normed_low, plane_s))
        other_s = [from_core(mine_s), from_core(plane_s)]
        sibling_s = from_core(after(shrink_weight, active))
        shrink = Weight(
            shapes[3],
            [shrink_weight, sibling_s, mine_s, plane_s, *after(other_s, normed_group)],
            functools.partial(stacked_copies, high=shrink_weight.shape[0], wide=shrink_weight.shape[1]),
        )
    out_rows, shrink_low, second_grad, sums2, shrink = second_norm(
        pos, captions, active, shrink, down_bias, unit1, gain1, shift1, gain2, shift2, cot_rows, seq
    )
    if pieces:
        mine_s, theirs_s = stacked_grad(pos, active, shrink_low)
        theirs_s = from_core(theirs_s)
        shrink_low = after(shrink_low, mine_s)
    else:
        grad_shrink = weight_grad(active, shrink_low)
    expand_low, sums_hidden = hidden_back(shrink_low, shrink, slope)
    if pieces:
        keep_s, near_s, kept_s, send_s = shrink_sum(mine_s, after(theirs_s, expand_low))
        expand_low = after(expand_low, kept_s)
        near_s, send_s = from_chip(near_s, 1), from_x(send_s)
        mine_e, theirs_e = halves_grad(pos, normed_group, expand_low)
        theirs_e = from_core(theirs_e)
        expand_low = after(expand_low, mine_e)
    first_grad, branch_low, context_grad, sums1 = first_back(
        expand_low, expand, second_grad, unit1, scale1, gain1, output
    )
    if pieces:
        own_s, later_s = pair_sum(kept_s, after(send_s, branch_low))
        mine_o, theirs_o = halves_grad(pos, context_group, after(branch_low, own_s))
        theirs_o = from_core(theirs_o)
        later_s = from_y(later_s)
        keep_s, far_s = pair_sum(keep_s, after(near_s, mine_o))
        own_x, later_x, out_x, own_y, later_y, out_y = core_split(
            [mine_e, mine_o], after([theirs_e, theirs_o], keep_s)
        )
        far_s = from_chip(far_s, 2)
        out_x, out_y = from_x(out_x), from_y(out_y)
        context_grad = after(context_grad, own_x)
    else:
        grad_expand = weight_grad(normed_low, expand_low)
        grad_output = weight_grad(context_rows, branch_low)
    joined_grad, sums_joined = attend_back(joined3, probs, context_grad.reshape(pairs, seq, width))
    joined_grad_rows = joined_grad.reshape(rows, 3 * width)
    if pieces:
        extra = bundle(sums_joined, sums1, sums2, sums_hidden)
        mine_p, theirs_p = halves_grad(pos, token_group, joined_grad_rows, extra)
        theirs_p = from_core(theirs_p)
        out_x, out_y = after((out_x, out_y), mine_p)
        own_x, later_x, own_y, later_y = middle_sum([own_x, later_x, out_x, own_y, later_y, out_y])
        later_x, later_y = after((from_y(later_x), from_x(later_y)), far_s)
        keep_eo, near_eo = split_sum([own_x, later_x, own_y, later_y], flops=COVER)
        keep_eo, near_eo = ahead_sum(own_s, after(later_s, keep_eo), keep_eo, near_eo)
        own_x, later_x, out_x, own_y, later_y, out_y = core_split(
            [mine_p], [after(theirs_p, near_eo)], (keep_s, far_s)
        )
        near_eo = from_chip(near_eo, 1)
        out_x, out_y = from_x(out_x), from_y(out_y)
        joined_grad_rows = after(joined_grad_rows, own_x)
    else:
        grad_project = weight_grad(token_rows, joined_grad_rows)

        def owned(grad):
            part = lax.psum_scatter(grad, "fsdp", scatter_dimension=0, tiled=True)
            return lax.psum(part, "dp").astype(F32)

        own_project, own_output, own_expand, own_shrink = (
            owned(grad) for grad in (grad_project, grad_output, grad_expand, grad_shrink)
        )
        small = (sums_joined[0], sums1[0], sums1[1], sums1[2], sums_hidden[0], sums2[0], sums2[1], sums2[2])
        packed_grad = jnp.concatenate([v.reshape(parts, -1) for v in small], axis=1)
        shard = lax.psum(lax.psum_scatter(packed_grad.reshape(-1), "fsdp", scatter_dimension=0, tiled=True), "dp")
    token_grad = token_back(joined_grad_rows, project, first_grad)
    if pieces:
        half_p, half_e, half_o = project_weight.shape[1] // 2, expand_weight.shape[1] // 2, width // 2
        out_x, out_y = after((out_x, out_y), token_grad)
        own_x, later_x, own_y, later_y = middle_sum([own_x, later_x, out_x, own_y, later_y, out_y])
        later_x, later_y = from_y(later_x), from_x(later_y)
        keep_eo, far_eo = pair_sum(keep_eo, after(near_eo, own_x))
        far_eo = from_chip(far_eo, 2)
        later_x, later_y = after((later_x, later_y), keep_eo)
        keep_p, near_p, total_s = split_sum([own_x, later_x, own_y, later_y], more=FIRST // 4)
        near_p = from_chip(near_p, 1)
        total_seo = last_sum((total_s,), (keep_eo, after(far_eo, keep_p)))
        quarters_seo = from_plane(total_seo)
        keep_p, far_p = pair_sum(keep_p, after(near_p, total_seo))
        total_p = last_sum((keep_p, from_chip(far_p, 2)))
        quarters_p = from_plane(total_p)
        own_shrink, own_expand, own_output = place(
            pos,
            [total_seo, *after(quarters_seo, total_p)],
            (("stacked", 2 * width), ("halves", half_e), ("halves", half_o)),
        )
        own_project, *smalls = place(
            pos, [total_p, *after(quarters_p, own_expand)], (("halves", half_p), ("small", 128)), widths
        )
        smalls = [vector.reshape(-1) for vector in smalls]

    if not pieces:
        smalls, at = [], 0
        for size in widths:
            smalls.append(shard[at : at + size])
            at += size
    return (
        out_rows.reshape(pairs, seq, width),
        token_grad.reshape(pairs, seq, width),
        own_project,
        smalls[0],
        own_output,
        smalls[1],
        smalls[2],
        smalls[3],
        own_expand,
        smalls[4],
        own_shrink,
        smalls[5],
        smalls[6],
        smalls[7],
    )


def solution(mesh):
    rows3 = P(("dp", "fsdp"), None, None)
    matrix, vector = P("fsdp", None), P("fsdp")
    pieces = mesh.shape["dp"] == 4 and mesh.shape["fsdp"] == 8
    return jax.shard_map(
        functools.partial(local, pieces),
        mesh=mesh,
        in_specs=(
            rows3, P(("dp", "fsdp")), rows3,
            matrix, vector, matrix, vector, vector, vector,
            matrix, vector, matrix, vector, vector, vector,
        ),
        out_specs=(
            rows3, rows3,
            matrix, vector, matrix, vector, vector, vector,
            matrix, vector, matrix, vector, vector, vector,
        ),
        check_vma=False,
    )
```
